32 devices in a mesh: dp: 8 (over z, x), mp: 4 (over y, core).
Axes of the slice: x: 2, y: 2, z: 4, core: 2. Of those that a mesh axis runs over, the one named last changes fastest.
Arguments:
- tokens: bfloat16 [16, 680, 1024], P('dp'), may hold values from -6 to 6
- cotangent: bfloat16 [16, 680, 1024], P('dp'), may hold values from -6 to 6
- stop_scales: int32 [16], P('dp'), may hold values from 6 to 10, as said below
- labels: int32 [16], P('dp'), may hold values from 0 to 1000
- class_table: bfloat16 [1001, 1024], P(None, 'mp'), may hold values from -6 to 6
- ada_weight: bfloat16 [1024, 6144], P('mp'), may hold values from -0.09375 to 0.09375
- ada_bias: float32 [6144], replicated, may hold values from 0.5 to 1.5
- qkv_weight: bfloat16 [1024, 3, 1024], P(None, None, 'mp'), may hold values from -0.1875 to 0.1875
- qv_bias: float32 [2, 1024], P(None, 'mp'), may hold values from -5 to 5
- log_scale: float32 [16], P('mp'), may hold values from 2 to 3.2
- proj_weight: bfloat16 [1024, 1024], P('mp'), may hold values from -0.75 to 0.75
- proj_bias: float32 [1024], replicated, may hold values from -3 to 3
- fc1_weight: bfloat16 [1024, 4096], P(None, 'mp'), may hold values from -0.1875 to 0.1875
- fc1_bias: float32 [4096], P('mp'), may hold values from -3 to 3
- fc2_weight: bfloat16 [4096, 1024], P('mp'), may hold values from -0.09375 to 0.09375
- fc2_bias: float32 [1024], replicated, may hold values from -3 to 3
Outputs:
- block_out: bfloat16 [16, 680, 1024], P('dp')
- token_grad: bfloat16 [16, 680, 1024], P('dp')
- table_grad: float32 [1001, 1024], P(None, 'mp')
- ada_weight_grad: float32 [1024, 6144], P('mp')
- ada_bias_grad: float32 [6144], replicated
- qkv_weight_grad: float32 [1024, 3, 1024], P(None, None, 'mp')
- qv_bias_grad: float32 [2, 1024], P(None, 'mp')
- log_scale_grad: float32 [16], P('mp')
- proj_weight_grad: float32 [1024, 1024], P('mp')
- proj_bias_grad: float32 [1024], replicated
- fc1_weight_grad: float32 [1024, 4096], P(None, 'mp')
- fc1_bias_grad: float32 [4096], P('mp')
- fc2_weight_grad: float32 [4096, 1024], P('mp')
- fc2_bias_grad: float32 [1024], replicated
The draws below stay inside these ranges and needn't reach their ends.
Inputs may be any that keep to these rules, and one draw needn't show every extreme that they name: `stop_scales`: an item with stop scale s has its first 1, 5, 14, 30, 55, 91, 155, 255, 424 or 680 slots live for s = 1 to 10; in every draw some item stops at 10 and some at 6.
All inputs are finite; a program needn't handle non-finite values.
Results may differ from the reference program's by a relative error of at most 0.028.
Values sent between devices are 32-bit elements; how exact they have to be, the bound alone decides.
A program may use at most 192 MiB of HBM per device.

```python
import jax
import jax.numpy as jnp
import numpy as np
from jax import lax

D = 1024
HEADS = 16
FF = 4096
CLASSES = 1001
SLOTS = 680
ITEMS = 16


def draw_stop_scales(key, part):
    key = jax.random.fold_in(key, 11)
    first_key, second_key = jax.random.split(key)
    values = jax.random.randint(first_key, (ITEMS,), 6, 11, dtype=jnp.int32)
    shuffled = jax.random.permutation(second_key, ITEMS)
    values = values.at[shuffled[0]].set(10)
    return values.at[shuffled[1]].set(6)


def with_ends(values, stream_key, smallest, largest):
    longest = values.shape.index(max(values.shape))
    spots = []
    for shift in (0, 1):
        where = [jax.random.randint(jax.random.fold_in(stream_key, axis), (), 0, length) for axis, length in enumerate(values.shape)]
        where[longest] = (where[longest] + shift) % values.shape[longest]
        spots.append(tuple(where))
    return values.at[spots[0]].set(smallest).at[spots[1]].set(largest)


def level_of(key, shape, cuts, smallest, top_value):
    loudness = 1.0
    for axis_at, blocks in cuts:
        draws = jax.random.uniform(jax.random.fold_in(jax.random.fold_in(key, 6), axis_at), (blocks,), jnp.float32, smallest / len(cuts), top_value / len(cuts))
        loudness = loudness * jnp.repeat(jnp.exp(draws), shape[axis_at] // blocks).reshape((-1,) + (1,) * (len(shape) - 1 - axis_at))
    return loudness


def bell_draw(stream_key, shape, scale, limit, pieces=(), held_as=jnp.bfloat16):
    values = scale * jax.random.normal(stream_key, shape, jnp.float32)
    if pieces:
        values = values * level_of(stream_key, shape, pieces, -0.22, 0.18)
    return jnp.clip(values, -limit, limit).astype(held_as)


def setup_inputs(seed: int = 0) -> dict:
    splits = jax.random.split(jax.random.key(seed), 17)
    return {
        "tokens": bell_draw(splits[0], (ITEMS, SLOTS, D), 1.0, 6.0, ((0, 8),)),
        "cotangent": bell_draw(splits[1], (ITEMS, SLOTS, D), 1.0, 6.0, ((0, 8),)),
        "stop_scales": draw_stop_scales(jax.random.fold_in(splits[16], 71), 0),
        "labels": with_ends(jax.random.randint(splits[3], (ITEMS,), 0, CLASSES), jax.random.fold_in(splits[3], 1), 0, CLASSES - 1).astype(jnp.int32),
        "class_table": bell_draw(splits[4], (CLASSES, D), 1.0, 6.0, ((1, 4),)),
        "ada_weight": bell_draw(splits[5], (D, 6 * D), (4 * D) ** -0.5, 0.09375, ((0, 4),)),
        "ada_bias": jnp.clip(1.0 + 0.1 * jax.random.normal(splits[6], (6 * D,), jnp.float32), 0.5, 1.5),
        "qkv_weight": bell_draw(splits[7], (D, 3, D), D ** -0.5, 0.1875, ((2, 4),)),
        "qv_bias": bell_draw(splits[8], (2, D), 1.0, 5.0, ((1, 4),), jnp.float32),
        "log_scale": jnp.clip(2.0 + 1.2 * jax.random.uniform(splits[9], (HEADS,), jnp.float32) ** level_of(splits[9], (HEADS,), ((0, 4),), -0.2, 0.2), 2.0, 3.2),
        "proj_weight": bell_draw(splits[10], (D, D), (D // 16) ** -0.5, 0.75, ((0, 4),)),
        "proj_bias": bell_draw(splits[11], (D,), 0.5, 3.0, (), jnp.float32),
        "fc1_weight": bell_draw(splits[12], (D, FF), D ** -0.5, 0.1875, ((1, 4),)),
        "fc1_bias": bell_draw(splits[13], (FF,), 0.5, 3.0, ((0, 4),), jnp.float32),
        "fc2_weight": bell_draw(splits[14], (FF, D), FF ** -0.5, 0.09375, ((0, 4),)),
        "fc2_bias": bell_draw(splits[15], (D,), 0.5, 3.0, (), jnp.float32),
    }


SIDE_LIST = (1, 2, 3, 4, 5, 6, 8, 10, 13, 16)
EPSILON = 1e-06
PRECISE = lax.Precision.HIGHEST

@jax.custom_vjp
def low(v):
    return lax.optimization_barrier(v.astype(jnp.bfloat16)).astype(jnp.float32)

@jax.custom_vjp
def low_back(v):
    return v

def low_keep(v):
    return (low(v), None)

def low_pass(kept, grad):
    return (grad,)

def back_keep(v):
    return (v, None)

def back_low(kept, grad):
    return (low(grad),)
low.defvjp(low_keep, low_pass)
low_back.defvjp(back_keep, back_low)

def scale_table(stop_scales, slot_count):
    scale_ends = np.cumsum(np.array([side_length * side_length for side_length in SIDE_LIST]))
    positions = jnp.arange(slot_count, dtype=jnp.int32)
    bounds = jnp.asarray(scale_ends[:-1], dtype=jnp.int32)
    levels = lax.optimization_barrier(jnp.sum((positions[:, None] >= bounds[None, :]).astype(jnp.int32), axis=1))
    counters = jnp.arange(1, len(SIDE_LIST) + 1, dtype=jnp.int32)
    ends_array = jnp.asarray(scale_ends, dtype=jnp.int32)
    lengths = lax.optimization_barrier(jnp.sum(jnp.where(stop_scales[:, None] == counters[None, :], ends_array[None, :], 0), axis=1)).astype(jnp.int32)
    return (positions, levels, lengths)

def modulate(row_block, scale_row, shift_row):
    center = row_block - lax.optimization_barrier(jnp.mean(row_block, axis=-1, keepdims=True))
    spread = lax.optimization_barrier(jnp.mean(center * center, axis=-1, keepdims=True))
    return center * lax.rsqrt(spread + EPSILON) * (1.0 + scale_row) + shift_row

def unit_heads(query_rows, key_rows, head_scale):
    query_unit = query_rows * lax.rsqrt(lax.optimization_barrier(jnp.sum(query_rows * query_rows, axis=-1, keepdims=True)) + EPSILON) * jnp.exp(head_scale)[:, None]
    key_unit = key_rows * lax.rsqrt(lax.optimization_barrier(jnp.sum(key_rows * key_rows, axis=-1, keepdims=True)) + EPSILON)
    return (query_unit, key_unit)

def block_item(params, token_rows, ada_row, length, positions, levels):
    qkv_matrix, qv_shift, head_scale, proj_matrix, proj_shift, fc1_matrix, fc1_shift, fc2_matrix, fc2_shift = params
    gamma_one, gamma_two, scale_one, scale_two, shift_one, shift_two = ada_row.reshape(6, D)
    head_dim = D // HEADS
    first_low = low(modulate(token_rows, scale_one, shift_one))
    bias_rows = jnp.stack([qv_shift[0], jnp.zeros_like(qv_shift[0]), qv_shift[1]])
    triple = low_back(jnp.einsum('sd,dcf->scf', first_low, qkv_matrix, precision=PRECISE) + bias_rows)
    query_rows = triple[:, 0].reshape(SLOTS, HEADS, head_dim)
    key_rows = triple[:, 1].reshape(SLOTS, HEADS, head_dim)
    value_low = low(triple[:, 2].reshape(SLOTS, HEADS, head_dim))
    query_unit, key_unit = unit_heads(query_rows, key_rows, head_scale)
    query_low = low(query_unit)
    key_low = low(key_unit)
    allowed = (levels[None, :] <= levels[:, None]) & (positions[None, :] < length)
    scores = low_back(jnp.einsum('qhe,khe->hqk', query_low, key_low, precision=PRECISE))
    masked = jnp.where(allowed[None], scores, -1e+30)
    row_peak = lax.optimization_barrier(jnp.max(masked, axis=-1, keepdims=True))
    exp_terms = jnp.exp(masked - row_peak)
    probabilities = low(exp_terms / lax.optimization_barrier(jnp.sum(exp_terms, axis=-1, keepdims=True)))
    mixed_rows = jnp.einsum('hqk,khe->qhe', probabilities, value_low, precision=PRECISE)
    mixed_low = low(low_back(mixed_rows)).reshape(SLOTS, D)
    attended = low_back(jnp.dot(mixed_low, proj_matrix, precision=PRECISE) + proj_shift)
    middle = token_rows + gamma_one * attended
    second_low = low(modulate(middle, scale_two, shift_two))
    upper = low_back(jnp.dot(second_low, fc1_matrix, precision=PRECISE) + fc1_shift)
    hidden_low = low(jax.nn.gelu(upper, approximate=True))
    branch = low_back(jnp.dot(hidden_low, fc2_matrix, precision=PRECISE) + fc2_shift)
    return middle + gamma_two * branch

def reference(tokens, cotangent, stop_scales, labels, class_table, ada_weight, ada_bias, qkv_weight, qv_bias, log_scale, proj_weight, proj_bias, fc1_weight, fc1_bias, fc2_weight, fc2_bias):
    positions, levels, lengths = scale_table(stop_scales, SLOTS)

    def forward(token_all, class_matrix, ada_matrix, ada_shift, qkv_matrix, qv_shift, head_scale, proj_matrix, proj_shift, fc1_matrix, fc1_shift, fc2_matrix, fc2_shift):
        class_rows = class_matrix[labels]
        modulation = low_back(jnp.dot(low(jax.nn.silu(class_rows)), ada_matrix, precision=PRECISE) + ada_shift)
        params = (qkv_matrix, qv_shift, head_scale, proj_matrix, proj_shift, fc1_matrix, fc1_shift, fc2_matrix, fc2_shift)

        def one_item(packed):
            return block_item(params, packed[0], packed[1], packed[2], positions, levels)
        return lax.map(jax.checkpoint(one_item), (token_all, modulation, lengths))
    inputs = (tokens, class_table, ada_weight, ada_bias, qkv_weight, qv_bias, log_scale, proj_weight, proj_bias, fc1_weight, fc1_bias, fc2_weight, fc2_bias)
    floats = tuple((array_in.astype(jnp.float32) for array_in in inputs))
    result, pullback = jax.vjp(forward, *floats)
    grads = pullback(cotangent.astype(jnp.float32))
    return (result.astype(jnp.bfloat16), grads[0].astype(jnp.bfloat16), grads[1], grads[2], grads[3], grads[4], grads[5], grads[6], grads[7], grads[8], grads[9], grads[10], grads[11], grads[12])
```

```python
import functools

import jax
import jax.numpy as jnp
import numpy as np
from jax import lax
from jax.experimental import pallas as pl
from jax.experimental.pallas import tpu as pltpu
from jax.sharding import PartitionSpec as P

SIDE_LIST = (1, 2, 3, 4, 5, 6, 8, 10, 13, 16)
EPSILON = 1e-06
MESH = pl.DeviceIdType.MESH
F32, BF16 = jnp.float32, jnp.bfloat16
GELU_C = 0.7978845608028654
GELU_A = 0.044715
LN_TILE = 64
NT = (((1,), (1,)), ((), ()))
TN = (((0,), (0,)), ((), ()))
NN = (((1,), (0,)), ((), ()))
ATT, DS, DF, BR = 0, 2, 4, 6


def dot(a, b, dims=NN):
    return lax.dot_general(a, b, dims, preferred_element_type=F32)


def norm_rows(v):
    center = v - jnp.mean(v, axis=-1, keepdims=True)
    scale = lax.rsqrt(jnp.mean(center * center, axis=-1, keepdims=True) + EPSILON)
    return center * scale, scale


def fold(v):
    return jnp.sum(v.reshape(v.shape[0] // 8, 8, v.shape[1]), axis=0)


def head_sum(v, blocks):
    high = v.astype(BF16)
    rest = (v - high.astype(F32)).astype(BF16)
    return dot(high, blocks) + dot(rest, blocks)


def block_kernel(
    slots,
    mod_part, ada_b, tok_hbm, cot_hbm, stops, lim_hbm,
    qkvw_hbm, projw_hbm, fc1w_hbm, fc2w_hbm,
    qv_b, es_row, proj_b, fc1_b, fc2_b,
    out_hbm, tg_hbm, g1_hbm, g2_hbm, gp_hbm, gq_hbm, modg_out, small_out,
    tok, cot, fst, sec, dbr, hid, dup,
    att, dst, dfr,
    qk, qkn, mix, dmx, acc,
    rs_buf, y_buf,
    qkvw, projw, fc1w, fc2w, lim,
    stage, modr, mod, g2r, fb1, lanes,
    in_sem, out_sem, stage_sem,
    mod_s, mod_r, g2_s, g2_r, rs_s, rs_r, y_s, y_r, ag_s, ag_r,
):
    items, padded, width = tok.shape
    half = width // 2
    me = lax.axis_index("mp")
    core = lax.rem(me, 2)
    core_mate = me + 1 - 2 * core
    y_mate = lax.rem(me + 2, 4)
    n_ln = padded // LN_TILE
    mt = padded // 2

    def rows_of(t, n):
        return pl.ds(pl.multiple_of(t * n, n), n)

    loads = {}
    for k, (name, src, to) in enumerate((
        ("tok", tok_hbm, tok), ("qkvw", qkvw_hbm, qkvw), ("lim", lim_hbm, lim),
        ("projw", projw_hbm, projw), ("cot", cot_hbm, cot),
        ("fc1w", fc1w_hbm, fc1w), ("fc2w", fc2w_hbm, fc2w),
    )):
        loads[name] = pltpu.make_async_copy(src, to, in_sem.at[k])
        loads[name].start()

    barrier = pltpu.get_barrier_semaphore()
    for step in (1, 2, 3):
        pl.semaphore_signal(barrier, inc=1, device_id={"mp": lax.rem(me + step, 4)}, device_id_type=MESH)
    pl.semaphore_wait(barrier, 3)

    def share(buf, send, recv):
        copies = []
        for step in (1, 2, 3):
            copies.append(pltpu.make_async_remote_copy(
                src_ref=buf.at[me], dst_ref=buf.at[me], send_sem=send.at[step - 1], recv_sem=recv.at[step - 1],
                device_id={"mp": lax.rem(me + step, 4)}, device_id_type=MESH))
        for copy in copies:
            copy.start()
        return copies

    modr[me] = mod_part[...]
    sent = share(modr, mod_s, mod_r)
    for copy in sent:
        copy.wait()
    mod[...] = ((modr[0] + modr[1]) + (modr[2] + modr[3])) + ada_b[...]

    def vec(i, k):
        return mod[i, k:k + 1, :]

    def rs_copy(buf, i, k):
        return pltpu.make_async_remote_copy(
            src_ref=buf.at[i, 1 - core, pl.ds(0, slots)], dst_ref=rs_buf.at[i], send_sem=rs_s.at[k + i], recv_sem=rs_r.at[k + i],
            device_id={"mp": core_mate}, device_id_type=MESH)

    def y_copy(buf, i, k):
        dst = dfr.at[i, 0, pl.ds(0, slots)] if k == DS else y_buf.at[i]
        return pltpu.make_async_remote_copy(
            src_ref=buf.at[i, core, pl.ds(0, slots)], dst_ref=dst, send_sem=y_s.at[k + i], recv_sem=y_r.at[k + i],
            device_id={"mp": y_mate}, device_id_type=MESH)

    def ag_copy(buf, i, k):
        return pltpu.make_async_remote_copy(
            src_ref=buf.at[i, core, pl.ds(0, slots)], dst_ref=buf.at[i, core, pl.ds(0, slots)],
            send_sem=ag_s.at[k + i], recv_sem=ag_r.at[k + i],
            device_id={"mp": core_mate}, device_id_type=MESH)

    add_rows = slots // 5

    def rs_finish(buf, i, k):
        rs_copy(buf, i, k).wait()

        def add(t, _):
            rows = rows_of(t, add_rows)
            buf[i, core, rows, :] = buf[i, core, rows, :] + rs_buf[i, rows, :]
            return 0
        lax.fori_loop(0, 5, add, 0)

    def y_finish(buf, i, k):
        y_copy(buf, i, k).wait()

        def add(t, _):
            rows = rows_of(t, add_rows)
            other = dfr[i, 0, rows, :] if k == DS else y_buf[i, rows, :]
            buf[i, core, rows, :] = buf[i, core, rows, :] + other
            return 0
        lax.fori_loop(0, 5, add, 0)

    def wide(buf, i, rows):
        return jnp.concatenate([buf[i, 0, rows, :], buf[i, 1, rows, :]], axis=1)

    def put_wide(buf, i, rows, v):
        buf[i, 0, rows, :] = v[:, :half]
        buf[i, 1, rows, :] = v[:, half:]

    def blocks_of(n):
        a = lax.broadcasted_iota(jnp.int32, (n, n), 0) // 64
        b = lax.broadcasted_iota(jnp.int32, (n, n), 1) // 64
        return jnp.where(a == b, 1.0, 0.0).astype(BF16)

    ends = np.cumsum(np.array([s * s for s in SIDE_LIST]))
    tiles = ((0, 240, 1, 256), (240, 176, 1, 512), (416, 96, 3, padded))

    def keep_of(i, rows, keys):
        live = jnp.int32(0)
        for s in range(len(SIDE_LIST)):
            live = jnp.where(stops[i] == s + 1, int(ends[s]), live)
        bound = jnp.minimum(lim[rows, :], live)
        n = bound.shape[0]
        return lax.broadcasted_iota(jnp.int32, (n, keys), 1) < bound[:, 0:1]

    def head_lanes(shape, h):
        return (lax.broadcasted_iota(jnp.int32, shape, 1) // 64) == h

    def mask_head(v, h):
        return jnp.where(head_lanes(v.shape, h), v.astype(F32), 0.0).astype(BF16)

    def each_tile(body):
        for first_row, n, steps, keys in tiles:
            if steps == 1:
                body(pl.ds(first_row, n), keys)
            else:
                def step(t, _, first_row=first_row, n=n, keys=keys):
                    body(pl.ds(pl.multiple_of(first_row + t * n, 16), n), keys)
                    return 0
                lax.fori_loop(0, steps, step, 0)

    def first_norm(i):
        def body(t, _):
            rows = rows_of(t, LN_TILE)
            n, _r = norm_rows(tok[i, rows, :].astype(F32))
            fst[i, rows, :] = (n * (1.0 + vec(i, 2)) + vec(i, 4)).astype(BF16)
            return 0
        lax.fori_loop(0, n_ln, body, 0)

    def project(i):
        blocks = blocks_of(256)

        def body(t, _):
            rows = rows_of(t, mt)
            f = fst[i, rows, :]
            q = dot(f, qkvw[0]) + qv_b[0:1, :]
            qk[i, 0, rows, :] = q
            u = q * lax.rsqrt(head_sum(q * q, blocks) + EPSILON) * es_row[...]
            qkn[i, 0, 0, rows, :] = u[:, :128].astype(BF16)
            qkn[i, 0, 1, rows, :] = u[:, 128:].astype(BF16)
            k = dot(f, qkvw[1])
            qk[i, 1, rows, :] = k
            u = k * lax.rsqrt(head_sum(k * k, blocks) + EPSILON)
            qkn[i, 1, 0, rows, :] = u[:, :128].astype(BF16)
            qkn[i, 1, 1, rows, :] = u[:, 128:].astype(BF16)
            v = dot(f, qkvw[2]) + qv_b[1:2, :]
            qkn[i, 2, 0, rows, :] = v[:, :128].astype(BF16)
            qkn[i, 2, 1, rows, :] = v[:, 128:].astype(BF16)
            return 0
        lax.fori_loop(0, 2, body, 0)

    def attend(i):
        def slab_body(slab, _):
            def body(rows, keys):
                keep = keep_of(i, rows, keys)
                total = None
                for h in (0, 1):
                    s = dot(qkn[i, 0, slab, rows, :], mask_head(qkn[i, 1, slab, pl.ds(0, keys), :], h), NT)
                    e = jnp.where(keep, jnp.exp(s), 0.0)
                    p = (e * (1.0 / jnp.sum(e, axis=-1, keepdims=True))).astype(BF16)
                    o = dot(p, mask_head(qkn[i, 2, slab, pl.ds(0, keys), :], h))
                    total = o if total is None else total + o
                mix[i, slab, rows, :] = total.astype(BF16)
            each_tile(body)
            return 0
        lax.fori_loop(0, 2, slab_body, 0)

    def attend_out(i):
        def body(t, _):
            rows = rows_of(t, mt)
            m = jnp.concatenate([mix[i, 0, rows, :], mix[i, 1, rows, :]], axis=1)
            for h in (0, 1):
                att[i, h, rows, :] = dot(m, projw[:, h * half:(h + 1) * half])
            return 0
        lax.fori_loop(0, 2, body, 0)

    def mlp(i):
        def body(t, total):
            rows = rows_of(t, LN_TILE)
            middle = tok[i, rows, :].astype(F32) + vec(i, 0) * (wide(att, i, rows) + proj_b[...])
            n, _r = norm_rows(middle)
            sec[i, rows, :] = (n * (1.0 + vec(i, 3)) + vec(i, 5)).astype(BF16)
            d = (cot[i, rows, :].astype(F32) * vec(i, 1)).astype(BF16)
            dbr[i, rows, :] = d
            return total + fold(d.astype(F32))
        total = lax.fori_loop(0, n_ln, body, jnp.zeros((8, width), F32))
        small_out[0:1, :] = small_out[0:1, :] + jnp.sum(total, axis=0, keepdims=True)

        def column(j, _):
            cols = pl.ds(pl.multiple_of(j * 256, 256), 256)

            def body(t, _):
                rows = rows_of(t, mt)
                u = dot(sec[i, rows, :], fc1w[:, cols]) + fc1_b[j]
                dh = dot(dbr[i, rows, :], fc2w[cols, :], NT)
                th = jnp.tanh(GELU_C * (u + GELU_A * u * u * u))
                hid[i, rows, cols] = (0.5 * u * (1.0 + th)).astype(BF16)
                slope = 0.5 * (1.0 + th) + 0.5 * u * (1.0 - th * th) * (GELU_C + (3.0 * GELU_C * GELU_A) * u * u)
                d = (dh * slope).astype(BF16)
                dup[i, j, rows, :] = d
                fb1[j] = fb1[j] + fold(d.astype(F32))
                return 0
            lax.fori_loop(0, 2, body, 0)
            return 0
        lax.fori_loop(0, dup.shape[1], column, 0)

        def back(t, _):
            rows = rows_of(t, mt)
            d = jnp.concatenate([dup[i, j, rows, :] for j in range(dup.shape[1])], axis=1)
            for h in (0, 1):
                dst[i, h, rows, :] = dot(d, fc1w[h * half:(h + 1) * half, :], NT)
            return 0
        lax.fori_loop(0, 2, back, 0)

    def stage_out(slot, hbm, j):
        return pltpu.make_async_copy(stage.at[slot], hbm.at[rows_of(j, 256)], stage_sem.at[slot])

    def fc_grads():
        def pair(lhs, rhs, slot, hbm, j):
            cols = pl.ds(pl.multiple_of(j * 256, 256), 256)

            def piece(n, _):
                to = pl.ds(pl.multiple_of(n * 256, 256), 256)
                stage[slot, :, to] = dot(lhs[0, :, cols], rhs(0, n), TN) + dot(lhs[1, :, cols], rhs(1, n), TN)
                return 0
            lax.fori_loop(0, width // 256, piece, 0)
            stage_out(slot, hbm, j).start()

        def body(j, _):
            @pl.when(j > 0)
            def _():
                stage_out(0, g2_hbm, j - 1).wait()
            pair(hid, lambda i, n: dbr[i, :, pl.ds(pl.multiple_of(n * 256, 256), 256)], 0, g2_hbm, j)

            @pl.when(j > 0)
            def _():
                stage_out(1, g1_hbm, j - 1).wait()
            pair(sec, lambda i, n: dup[i, n], 1, g1_hbm, j)
            return 0
        lax.fori_loop(0, 4, body, 0)
        stage_out(0, g2_hbm, 3).wait()
        stage_out(1, g1_hbm, 3).wait()

    def second_back(i):
        zero = jnp.zeros((8, width), F32)

        def body(t, sums):
            rows = rows_of(t, LN_TILE)
            attended = wide(att, i, rows) + proj_b[...]
            n, r = norm_rows(tok[i, rows, :].astype(F32) + vec(i, 0) * attended)
            dy = wide(dst, i, rows)
            dn = dy * (1.0 + vec(i, 3))
            dm = cot[i, rows, :].astype(F32) + r * (
                dn - jnp.mean(dn, axis=-1, keepdims=True) - n * jnp.mean(dn * n, axis=-1, keepdims=True))
            put_wide(dst, i, rows, dm)
            da = (dm * vec(i, 0)).astype(BF16)
            sec[i, rows, :] = da
            return (sums[0] + fold(dm * attended), sums[1] + fold(dy * n), sums[2] + fold(dy), sums[3] + fold(da.astype(F32)))
        sums = lax.fori_loop(0, n_ln, body, (zero, zero, zero, zero))
        for k, s in zip((0, 3, 5), sums[:3]):
            modg_out[i, k:k + 1, :] = jnp.sum(s, axis=0, keepdims=True)
        small_out[2:3, :] = small_out[2:3, :] + jnp.sum(sums[3], axis=0, keepdims=True)

        def mixed(t, _):
            rows = rows_of(t, mt)
            d = dot(sec[i, rows, :], projw[...], NT)
            dmx[0, rows, :] = d[:, :128].astype(BF16)
            dmx[1, rows, :] = d[:, 128:].astype(BF16)
            return 0
        lax.fori_loop(0, 2, mixed, 0)

    def attend_back(i):
        blocks = blocks_of(128)

        def slab_body(slab, _):
            acc[...] = jnp.zeros_like(acc)

            def body(rows, keys):
                keep = keep_of(i, rows, keys)
                kr = pl.ds(0, keys)
                for h in (0, 1):
                    km = mask_head(qkn[i, 1, slab, kr, :], h)
                    s = dot(qkn[i, 0, slab, rows, :], km, NT)
                    e = jnp.where(keep, jnp.exp(s), 0.0)
                    p = e * (1.0 / jnp.sum(e, axis=-1, keepdims=True))
                    dom = mask_head(dmx[slab, rows, :], h)
                    acc[2, kr, :] += dot(p.astype(BF16), dom, TN)
                    dp = dot(dom, qkn[i, 2, slab, kr, :], NT)
                    ds = (p * (dp - jnp.sum(dp * p, axis=-1, keepdims=True))).astype(BF16)
                    acc[0, rows, :] += dot(ds, km)
                    acc[1, kr, :] += dot(ds, mask_head(qkn[i, 0, slab, rows, :], h), TN)
            each_tile(body)

            es = jnp.where(slab == 0, es_row[:, :128], es_row[:, 128:])

            def close(t, sums):
                rows = rows_of(t, LN_TILE)

                def unit(c, g):
                    pre = qk[i, c, rows, pl.ds(pl.multiple_of(slab * 128, 128), 128)]
                    r = lax.rsqrt(head_sum(pre * pre, blocks) + EPSILON)
                    u = pre * r
                    gu = g * u
                    return r * (g - u * head_sum(gu, blocks)), gu
                dq, gu = unit(0, acc[0, rows, :] * es)
                dk, _g = unit(1, acc[1, rows, :])
                dq, dk, dv = dq.astype(BF16), dk.astype(BF16), acc[2, rows, :].astype(BF16)
                to = pl.ds(pl.multiple_of(slab * 128, 128), 128)
                dup[i, 0, rows, to] = dq
                dup[i, 1, rows, to] = dk
                dup[i, 2, rows, to] = dv
                return sums[0] + fold(dq.astype(F32)), sums[1] + fold(dv.astype(F32)), sums[2] + fold(gu)
            zero = jnp.zeros((8, 128), F32)
            sums = lax.fori_loop(0, n_ln, close, (zero, zero, zero))
            for k in range(3):
                lanes[k, slab] = lanes[k, slab] + sums[k]
            return 0
        lax.fori_loop(0, 2, slab_body, 0)

    def first_grad(i):
        def body(t, _):
            rows = rows_of(t, mt)
            for h in (0, 1):
                total = None
                for c in range(3):
                    o = dot(dup[i, c, rows, :], qkvw[c, h * half:(h + 1) * half, :], NT)
                    total = o if total is None else total + o
                dfr[i, h, rows, :] = total
            return 0
        lax.fori_loop(0, 2, body, 0)

    def attention_grads():
        def piece(n, _):
            to = pl.ds(pl.multiple_of(n * 512, 512), 512)
            for slab in (0, 1):
                stage[0, slab * 128:(slab + 1) * 128, to] = (
                    dot(mix[0, slab], sec[0, :, to], TN) + dot(mix[1, slab], sec[1, :, to], TN))
            return 0
        lax.fori_loop(0, 2, piece, 0)
        to_proj = pltpu.make_async_copy(stage.at[0], gp_hbm, stage_sem.at[0])
        to_proj.start()
        to_proj.wait()

        def part(c, j):
            return pltpu.make_async_copy(
                stage.at[1, :, pl.ds(pl.multiple_of(c * 256, 256), 256)], gq_hbm.at[c, rows_of(j, 256)], stage_sem.at[1])

        def body(n, _):
            j, c = n // 3, lax.rem(n, 3)
            cols = pl.ds(pl.multiple_of(j * 256, 256), 256)
            to = pl.ds(pl.multiple_of(c * 256, 256), 256)
            total = None
            for i in (0, 1):
                o = dot(fst[i, :, cols], dup[i, c], TN)
                total = o if total is None else total + o
            stage[1, :, to] = total
            part(c, j).start()
            part(c, j).wait()
            return 0
        lax.fori_loop(0, 12, body, 0)

    def first_back(i):
        zero = jnp.zeros((8, width), F32)

        def body(t, sums):
            rows = rows_of(t, LN_TILE)
            n, r = norm_rows(tok[i, rows, :].astype(F32))
            dy = wide(dfr, i, rows)
            dn = dy * (1.0 + vec(i, 2))
            g = wide(dst, i, rows) + r * (
                dn - jnp.mean(dn, axis=-1, keepdims=True) - n * jnp.mean(dn * n, axis=-1, keepdims=True))
            fst[i, rows, :] = g.astype(BF16)
            return sums[0] + fold(dy * n), sums[1] + fold(dy)
        sums = lax.fori_loop(0, n_ln, body, (zero, zero))
        for k, s in zip((2, 4), sums):
            modg_out[i, k:k + 1, :] = jnp.sum(s, axis=0, keepdims=True)
        pltpu.make_async_copy(fst.at[i], tg_hbm.at[i], out_sem.at[i]).start()

    def branch(i):
        def body(t, _):
            rows = rows_of(t, mt)
            for h in (0, 1):
                dst[i, h, rows, :] = dot(hid[i, rows, :], fc2w[:, h * half:(h + 1) * half])
            return 0
        lax.fori_loop(0, 2, body, 0)

        def sums_of(t, sums):
            rows = rows_of(t, LN_TILE)
            g = cot[i, rows, :].astype(F32)
            return sums[0] + fold(g * wide(dst, i, rows)), sums[1] + fold(g)
        zero = jnp.zeros((8, width), F32)
        sums = lax.fori_loop(0, n_ln, sums_of, (zero, zero))
        g2r[me, i:i + 1, :] = jnp.sum(sums[0], axis=0, keepdims=True)
        modg_out[i, 1:2, :] = fc2_b[...] * jnp.sum(sums[1], axis=0, keepdims=True)

    def block_end(i):
        def body(t, _):
            rows = rows_of(t, LN_TILE)
            middle = tok[i, rows, :].astype(F32) + vec(i, 0) * (wide(att, i, rows) + proj_b[...])
            cot[i, rows, :] = (middle + vec(i, 1) * (wide(dst, i, rows) + fc2_b[...])).astype(BF16)
            return 0
        lax.fori_loop(0, n_ln, body, 0)
        pltpu.make_async_copy(cot.at[i], out_hbm.at[i], out_sem.at[2 + i]).start()

    small_out[...] = jnp.zeros_like(small_out)
    modg_out[...] = jnp.zeros_like(modg_out)
    fb1[...] = jnp.zeros_like(fb1)
    lanes[...] = jnp.zeros_like(lanes)
    g2r[...] = jnp.zeros_like(g2r)
    loads["tok"].wait()
    for i in (0, 1):
        first_norm(i)
        if i == 0:
            loads["qkvw"].wait()
        project(i)
        if i == 0:
            loads["lim"].wait()
        attend(i)
        if i == 0:
            loads["projw"].wait()
        attend_out(i)
        rs_copy(att, i, ATT).start()
        rs_finish(att, i, ATT)
        if i == 0:
            y_copy(att, 0, ATT).start()
    for name in ("cot", "fc1w", "fc2w"):
        loads[name].wait()

    y_finish(att, 0, ATT)
    y_copy(att, 1, ATT).start()
    ag_copy(att, 0, ATT).start()
    ag_copy(att, 0, ATT).wait()
    mlp(0)
    rs_copy(dst, 0, DS).start()
    rs_finish(dst, 0, DS)

    y_finish(att, 1, ATT)
    y_copy(dst, 0, DS).start()
    ag_copy(att, 1, ATT).start()
    ag_copy(att, 1, ATT).wait()
    mlp(1)
    rs_copy(dst, 1, DS).start()
    fc_grads()
    rs_finish(dst, 1, DS)

    for i in (0, 1):
        y_finish(dst, i, DS)
        if i == 0:
            y_copy(dst, 1, DS).start()
        else:
            y_copy(dfr, 0, DF).start()
        ag_copy(dst, i, DS).start()
        ag_copy(dst, i, DS).wait()
        second_back(i)
        attend_back(i)
        first_grad(i)
        rs_copy(dfr, i, DF).start()
        rs_finish(dfr, i, DF)
    attention_grads()

    for i in (0, 1):
        y_finish(dfr, i, DF)
        if i == 0:
            y_copy(dfr, 1, DF).start()
        else:
            y_copy(dst, 0, BR).start()
        ag_copy(dfr, i, DF).start()
        ag_copy(dfr, i, DF).wait()
        first_back(i)
        branch(i)
        rs_copy(dst, i, BR).start()
        rs_finish(dst, i, BR)

    sent = share(g2r, g2_s, g2_r)
    for copy in sent:
        copy.wait()
    total = (g2r[0] + g2r[1]) + (g2r[2] + g2r[3])
    for i in (0, 1):
        modg_out[i, 1:2, :] = modg_out[i, 1:2, :] + total[i:i + 1, :]
    for j in range(4):
        small_out[1:2, j * 256:(j + 1) * 256] = jnp.sum(fb1[j], axis=0, keepdims=True)
    for k in range(3):
        for slab in (0, 1):
            at = k * 256 + slab * 128
            small_out[3:4, at:at + 128] = jnp.sum(lanes[k, slab], axis=0, keepdims=True)

    for i in (0, 1):
        y_finish(dst, i, BR)
        if i == 0:
            y_copy(dst, 1, BR).start()
        ag_copy(dst, i, BR).start()
        ag_copy(dst, i, BR).wait()
        block_end(i)
    for i in (0, 1):
        pltpu.make_async_copy(fst.at[i], tg_hbm.at[i], out_sem.at[i]).wait()
        pltpu.make_async_copy(cot.at[i], out_hbm.at[i], out_sem.at[2 + i]).wait()


def run_block(mod_part, ada_b, tok, cot, stops, qkvw, projw, fc1w, fc2w, qv_b, es_row, proj_b, fc1_b, fc2_b, slots):
    items, padded, width = tok.shape
    half = width // 2
    hidden = fc1w.shape[1]
    ends = np.cumsum(np.array([s * s for s in SIDE_LIST]))
    level = np.minimum(np.searchsorted(ends, np.arange(padded), side="right"), len(SIDE_LIST) - 1)
    lim = jnp.asarray(np.broadcast_to(ends[level][:, None], (padded, 128)), jnp.int32)
    hbm = pl.BlockSpec(memory_space=pl.ANY)
    vmem = pl.BlockSpec(memory_space=pltpu.VMEM)
    smem = pl.BlockSpec(memory_space=pltpu.SMEM)
    wide_b = (items, padded, width)
    wide_f = (items, 2, padded, half)
    dma = pltpu.SemaphoreType.DMA
    return pl.pallas_call(
        functools.partial(block_kernel, slots),
        out_shape=(
            jax.ShapeDtypeStruct(wide_b, BF16), jax.ShapeDtypeStruct(wide_b, BF16),
            jax.ShapeDtypeStruct((width, hidden), F32), jax.ShapeDtypeStruct((hidden, width), F32),
            jax.ShapeDtypeStruct(projw.shape, F32), jax.ShapeDtypeStruct(qkvw.shape, F32),
            jax.ShapeDtypeStruct((items, 8, width), F32), jax.ShapeDtypeStruct((8, width), F32),
        ),
        in_specs=[vmem, vmem, hbm, hbm, smem, hbm, hbm, hbm, hbm, hbm, vmem, vmem, vmem, vmem, vmem],
        out_specs=(hbm, hbm, hbm, hbm, hbm, hbm, vmem, vmem),
        scratch_shapes=[
            *[pltpu.VMEM(wide_b, BF16) for _ in range(5)],
            pltpu.VMEM((items, padded, hidden), BF16), pltpu.VMEM((items, hidden // 256, padded, 256), BF16),
            *[pltpu.VMEM(wide_f, F32) for _ in range(3)],
            pltpu.VMEM((items, 2, padded, 256), F32),
            pltpu.VMEM((items, 3, 2, padded, 128), BF16),
            pltpu.VMEM((items, 2, padded, 128), BF16),
            pltpu.VMEM((2, padded, 128), BF16),
            pltpu.VMEM((3, padded, 128), F32),
            pltpu.VMEM((items, slots, half), F32),
            pltpu.VMEM((items, slots, half), F32),
            pltpu.VMEM(qkvw.shape, BF16), pltpu.VMEM(projw.shape, BF16),
            pltpu.VMEM(fc1w.shape, BF16), pltpu.VMEM(fc2w.shape, BF16),
            pltpu.VMEM((padded, 128), jnp.int32),
            pltpu.VMEM((2, 256, width), F32),
            pltpu.VMEM((4, items, 8, width), F32), pltpu.VMEM((items, 8, width), F32),
            pltpu.VMEM((4, 8, width), F32),
            pltpu.VMEM((4, 8, 256), F32), pltpu.VMEM((3, 2, 8, 128), F32),
            dma((7,)), dma((4,)), dma((2,)),
            dma((3,)), dma((3,)), dma((3,)), dma((3,)),
            *[dma((8,)) for _ in range(6)],
        ],
        compiler_params=pltpu.CompilerParams(
            collective_id=0, has_side_effects=True, vmem_limit_bytes=62 * 2**20),
        name="block",
    )(mod_part, ada_b, tok, cot, stops, lim, qkvw, projw, fc1w, fc2w, qv_b, es_row, proj_b, fc1_b, fc2_b)


def shards(
    tokens, cotangent, stop_scales, labels, class_table, ada_weight, ada_bias, qkv_weight, qv_bias, log_scale,
    proj_weight, proj_bias, fc1_weight, fc1_bias, fc2_weight, fc2_bias,
):
    items, slots, width = tokens.shape
    padded = -(-slots // LN_TILE) * LN_TILE
    classes = class_table.shape[0]
    class_local = jnp.concatenate(
        [lax.dynamic_slice_in_dim(class_table, labels[i], 1, 0) for i in range(items)], axis=0).astype(F32)
    lifted = jax.nn.silu(class_local).astype(BF16)
    part = jnp.dot(lifted, ada_weight, preferred_element_type=F32).reshape(items, 6, width)
    part = jnp.pad(part, ((0, 0), (0, 2), (0, 0)))
    ada_rows = jnp.pad(ada_bias.reshape(1, 6, width), ((0, 0), (0, 2), (0, 0)))
    tok = jnp.pad(tokens, ((0, 0), (0, padded - slots), (0, 0)))
    cot = jnp.pad(cotangent, ((0, 0), (0, padded - slots), (0, 0)))
    heads = log_scale.shape[0]
    es_row = jnp.repeat(jnp.exp(log_scale), qkv_weight.shape[2] // heads)[None, :]
    out, tg, g1, g2, gp, gq, modg, small = run_block(
        part, ada_rows, tok, cot, stop_scales, jnp.transpose(qkv_weight, (1, 0, 2)), proj_weight, fc1_weight, fc2_weight,
        qv_bias, es_row, proj_bias[None, :], fc1_bias.reshape(-1, 1, 256), fc2_bias[None, :], slots)

    tag = jnp.broadcast_to(labels.astype(F32)[:, None], (items, width))
    every = lax.all_gather(modg.at[:, 6].set(tag), "dp", axis=0, tiled=True)
    every_label = every[:, 6, 0]
    class_hot = every_label[:, None] == jnp.arange(classes, dtype=F32)[None, :]
    dmod = every[:, :6].reshape(-1, 6 * width)
    dmod = jnp.where(every_label[:, None] >= 0, dmod, 0.0).astype(BF16)
    every_class = jnp.dot(class_hot.astype(BF16), class_table, preferred_element_type=F32)
    every_lift = jax.nn.silu(every_class).astype(BF16)
    lifted_grad = jnp.einsum("ik,dk->id", dmod, ada_weight, preferred_element_type=F32)
    class_grad = jax.vjp(jax.nn.silu, every_class)[1](lifted_grad)[0]
    table_grad = jnp.einsum("ic,id->cd", class_hot.astype(F32), class_grad, precision=lax.Precision.HIGHEST)
    ada_weight_grad = jnp.einsum("id,ik->dk", every_lift, dmod, preferred_element_type=F32)
    ada_bias_grad = jnp.sum(dmod.astype(F32), axis=0)
    g1, g2, gp, gq, small = lax.psum((g1, g2, gp, gq, small), "dp")
    lanes = small[3]
    return (
        out[:, :slots], tg[:, :slots], table_grad, ada_weight_grad, ada_bias_grad,
        jnp.transpose(gq, (1, 0, 2)), lanes[:512].reshape(2, 256), lanes[512:768].reshape(heads, -1).sum(axis=1),
        gp, small[2], g1, small[1], g2, small[0],
    )


def solution(mesh):
    return jax.shard_map(
        shards,
        mesh=mesh,
        in_specs=(
            P("dp", None, None), P("dp", None, None), P("dp"), P("dp"), P(None, "mp"), P("mp", None), P(),
            P(None, None, "mp"), P(None, "mp"), P("mp"), P("mp", None), P(), P(None, "mp"), P("mp"), P("mp", None), P(),
        ),
        out_specs=(
            P("dp", None, None), P("dp", None, None), P(None, "mp"), P("mp", None), P(), P(None, None, "mp"), P(None, "mp"),
            P("mp"), P("mp", None), P(), P(None, "mp"), P("mp"), P("mp", None), P(),
        ),
        check_vma=False,
    )
```

```python
import functools

import jax
import jax.numpy as jnp
import numpy as np
from jax import lax
from jax.experimental import pallas as pl
from jax.experimental.pallas import tpu as pltpu
from jax.sharding import PartitionSpec as P

SIDE_LIST = (1, 2, 3, 4, 5, 6, 8, 10, 13, 16)
EPSILON = 1e-06
MESH = pl.DeviceIdType.MESH
F32, BF16 = jnp.float32, jnp.bfloat16
GELU_C = 0.7978845608028654
GELU_A = 0.044715
LN_TILE = 64
NT = (((1,), (1,)), ((), ()))
TN = (((0,), (0,)), ((), ()))
NN = (((1,), (0,)), ((), ()))
ATT, DS, DF, BR = 0, 2, 4, 6
X_CHUNKS = (0, 1, 2, 3, 8, 9)


def dot(a, b, dims=NN):
    return lax.dot_general(a, b, dims, preferred_element_type=F32)


def norm_rows(v):
    center = v - jnp.mean(v, axis=-1, keepdims=True)
    scale = lax.rsqrt(jnp.mean(center * center, axis=-1, keepdims=True) + EPSILON)
    return center * scale, scale


def fold(v):
    return jnp.sum(v.reshape(v.shape[0] // 8, 8, v.shape[1]), axis=0)


def head_sum(v, blocks):
    high = v.astype(BF16)
    rest = (v - high.astype(F32)).astype(BF16)
    return dot(high, blocks) + dot(rest, blocks)


def block_kernel(
    slots, n_dp,
    mod_part, ada_b, tok_hbm, cot_hbm, stops, labels, lim_hbm,
    qkvw_hbm, projw_hbm, fc1w_hbm, fc2w_hbm,
    qv_b, es_row, proj_b, fc1_b, fc2_b,
    out_hbm, tg_hbm, final, every, grads, x_in, z_in, mid_in, rest_in,
    tok, cot, fst, sec, dbr, hid, dup,
    att, dst, dfr,
    qk, qkn, mix, dmx, kv, acc,
    rs_buf, y_buf,
    qkvw, projw, fc1w, fc2w, lim,
    stage, modr, mod, g2r, fb1, lanes, sm,
    in_sem, out_sem, load_sem, store_sem,
    mod_s, mod_r, g2_s, g2_r, rs_s, rs_r, y_s, y_r, ag_s, ag_r,
    x1_s, x1_r, zi_s, zi_r, mi_s, mi_r, zo_s, zo_r, x2_s, x2_r, re_s, re_r, ev_s, ev_r,
):
    items, padded, width = tok.shape
    half = width // 2
    me = lax.axis_index("mp")
    dp = lax.axis_index("dp")
    xb = lax.rem(dp, 2)
    z = lax.rem(dp // 2, 4)
    zh = z // 2
    inner = jnp.logical_or(z == 1, z == 2)
    edge = jnp.logical_or(z == 0, z == 3)
    x_mate = dp + 1 - 2 * xb
    z_mate = dp + 2 - 4 * lax.rem(z, 2)
    mid_mate = jnp.where(z == 1, dp + 2, jnp.where(z == 2, dp - 2, dp))
    n_rest = rest_in.shape[0] if n_dp > 8 else 0
    rest_mates = [dp + (8 << k) * (1 - 2 * lax.rem(dp // (8 << k), 2)) for k in range(n_rest)]
    core = lax.rem(me, 2)
    core_mate = me + 1 - 2 * core
    y_mate = lax.rem(me + 2, 4)
    n_ln = padded // LN_TILE
    mt = padded // 2

    def rows_of(t, n):
        return pl.ds(pl.multiple_of(t * n, n), n)

    loads = {}
    for k, (name, src, to) in enumerate((
        ("tok", tok_hbm, tok), ("qkvw", qkvw_hbm, qkvw), ("lim", lim_hbm, lim),
        ("projw", projw_hbm, projw), ("cot", cot_hbm, cot),
        ("fc1w", fc1w_hbm, fc1w), ("fc2w", fc2w_hbm, fc2w),
    )):
        loads[name] = pltpu.make_async_copy(src, to, in_sem.at[k])
        loads[name].start()

    barrier = pltpu.get_barrier_semaphore()
    for step in (1, 2, 3):
        pl.semaphore_signal(barrier, inc=1, device_id={"mp": lax.rem(me + step, 4)}, device_id_type=MESH)
    def greet(step, _):
        pl.semaphore_signal(barrier, inc=1, device_id={"dp": lax.rem(dp + step, n_dp)}, device_id_type=MESH)
        return 0
    lax.fori_loop(1, n_dp, greet, 0)
    pl.semaphore_wait(barrier, 3 + n_dp - 1)

    def share(buf, send, recv):
        copies = []
        for step in (1, 2, 3):
            copies.append(pltpu.make_async_remote_copy(
                src_ref=buf.at[me], dst_ref=buf.at[me], send_sem=send.at[step - 1], recv_sem=recv.at[step - 1],
                device_id={"mp": lax.rem(me + step, 4)}, device_id_type=MESH))
        for copy in copies:
            copy.start()
        return copies

    modr[me] = mod_part[...]
    sent = share(modr, mod_s, mod_r)
    for copy in sent:
        copy.wait()
    mod[...] = ((modr[0] + modr[1]) + (modr[2] + modr[3])) + ada_b[...]

    def vec(i, k):
        return mod[i, k:k + 1, :]

    def rs_copy(buf, i, k):
        return pltpu.make_async_remote_copy(
            src_ref=buf.at[i, 1 - core, pl.ds(0, slots)], dst_ref=rs_buf.at[i], send_sem=rs_s.at[k + i], recv_sem=rs_r.at[k + i],
            device_id={"mp": core_mate}, device_id_type=MESH)

    def y_copy(buf, i, k):
        if k == DS:
            dst = dfr.at[i, 0, pl.ds(0, slots)]
        elif k == BR:
            dst = qk.at[i, pl.ds(0, slots)]
        else:
            dst = y_buf.at[i]
        return pltpu.make_async_remote_copy(
            src_ref=buf.at[i, core, pl.ds(0, slots)], dst_ref=dst, send_sem=y_s.at[k + i], recv_sem=y_r.at[k + i],
            device_id={"mp": y_mate}, device_id_type=MESH)

    def ag_copy(buf, i, k):
        return pltpu.make_async_remote_copy(
            src_ref=buf.at[i, core, pl.ds(0, slots)], dst_ref=buf.at[i, core, pl.ds(0, slots)],
            send_sem=ag_s.at[k + i], recv_sem=ag_r.at[k + i],
            device_id={"mp": core_mate}, device_id_type=MESH)

    add_rows = slots // 5

    def rs_finish(buf, i, k):
        rs_copy(buf, i, k).wait()

        def add(t, _):
            rows = rows_of(t, add_rows)
            buf[i, core, rows, :] = buf[i, core, rows, :] + rs_buf[i, rows, :]
            return 0
        lax.fori_loop(0, 5, add, 0)

    def y_finish(buf, i, k):
        y_copy(buf, i, k).wait()

        def add(t, _):
            rows = rows_of(t, add_rows)
            if k == DS:
                other = dfr[i, 0, rows, :]
            elif k == BR:
                other = qk[i, rows, :]
            else:
                other = y_buf[i, rows, :]
            buf[i, core, rows, :] = buf[i, core, rows, :] + other
            return 0
        lax.fori_loop(0, 5, add, 0)

    def wide(buf, i, rows):
        return jnp.concatenate([buf[i, 0, rows, :], buf[i, 1, rows, :]], axis=1)

    def put_wide(buf, i, rows, v):
        buf[i, 0, rows, :] = v[:, :half]
        buf[i, 1, rows, :] = v[:, half:]

    def blocks_of(n):
        a = lax.broadcasted_iota(jnp.int32, (n, n), 0) // 64
        b = lax.broadcasted_iota(jnp.int32, (n, n), 1) // 64
        return jnp.where(a == b, 1.0, 0.0).astype(BF16)

    ends = np.cumsum(np.array([s * s for s in SIDE_LIST]))
    tiles = ((0, 240, 1, 256), (240, 176, 1, 512), (416, 96, 3, 768))

    def keep_of(i, rows, keys):
        live = jnp.int32(0)
        for s in range(len(SIDE_LIST)):
            live = jnp.where(stops[i] == s + 1, int(ends[s]), live)
        bound = jnp.minimum(lim[rows, :], live)
        n = bound.shape[0]
        return lax.broadcasted_iota(jnp.int32, (n, keys), 1) < bound[:, 0:1]

    def one_head(h):
        lane = lax.broadcasted_iota(jnp.int32, (1, 128), 1) // 64
        return jnp.where(lane == h, 1.0, 0.0).astype(BF16)

    def fill_kv(i, slab):
        for c in (0, 1):
            for h in (0, 1):
                kv[c, h, 0:padded, :] = qkn[i, 1 + c, slab] * one_head(h)

    def exps(i, slab, rows, keys):
        keep = keep_of(i, rows, keys)
        s = dot(qkn[i, 0, slab, rows, :], kv[0, :, 0:keys, :].reshape(2 * keys, 128), NT)
        parts = []
        for h in (0, 1):
            e = jnp.where(keep, jnp.exp(s[:, h * keys:(h + 1) * keys]), 0.0)
            parts.append(e * (1.0 / jnp.sum(e, axis=-1, keepdims=True)))
        return parts

    def each_tile(body):
        for first_row, n, steps, keys in tiles:
            if steps == 1:
                body(pl.ds(first_row, n), keys)
            else:
                def step(t, _, first_row=first_row, n=n, keys=keys):
                    body(pl.ds(pl.multiple_of(first_row + t * n, 16), n), keys)
                    return 0
                lax.fori_loop(0, steps, step, 0)

    def first_norm(i):
        def body(t, _):
            rows = rows_of(t, LN_TILE)
            n, _r = norm_rows(tok[i, rows, :].astype(F32))
            fst[i, rows, :] = (n * (1.0 + vec(i, 2)) + vec(i, 4)).astype(BF16)
            return 0
        lax.fori_loop(0, n_ln, body, 0)

    def project(i):
        blocks = blocks_of(256)

        def body(t, _):
            rows = rows_of(t, mt)
            f = fst[i, rows, :]
            q = dot(f, qkvw[0]) + qv_b[0:1, :]
            qk[i, rows, 0:256] = q
            u = q * lax.rsqrt(head_sum(q * q, blocks) + EPSILON) * es_row[...]
            qkn[i, 0, 0, rows, :] = u[:, :128].astype(BF16)
            qkn[i, 0, 1, rows, :] = u[:, 128:].astype(BF16)
            k = dot(f, qkvw[1])
            qk[i, rows, 256:512] = k
            u = k * lax.rsqrt(head_sum(k * k, blocks) + EPSILON)
            qkn[i, 1, 0, rows, :] = u[:, :128].astype(BF16)
            qkn[i, 1, 1, rows, :] = u[:, 128:].astype(BF16)
            v = dot(f, qkvw[2]) + qv_b[1:2, :]
            qkn[i, 2, 0, rows, :] = v[:, :128].astype(BF16)
            qkn[i, 2, 1, rows, :] = v[:, 128:].astype(BF16)
            return 0
        lax.fori_loop(0, 2, body, 0)

    def attend(i):
        def slab_body(slab, _):
            fill_kv(i, slab)

            def body(rows, keys):
                p = jnp.concatenate([v.astype(BF16) for v in exps(i, slab, rows, keys)], axis=1)
                o = dot(p, kv[1, :, 0:keys, :].reshape(2 * keys, 128))
                mix[i, slab, rows, :] = o.astype(BF16)
            each_tile(body)
            return 0
        lax.fori_loop(0, 2, slab_body, 0)

    def attend_out(i):
        def body(t, _):
            rows = rows_of(t, mt)
            m = jnp.concatenate([mix[i, 0, rows, :], mix[i, 1, rows, :]], axis=1)
            for h in (0, 1):
                att[i, h, rows, :] = dot(m, projw[:, h * half:(h + 1) * half])
            return 0
        lax.fori_loop(0, 2, body, 0)

    def mlp(i):
        def body(t, total):
            rows = rows_of(t, LN_TILE)
            middle = tok[i, rows, :].astype(F32) + vec(i, 0) * (wide(att, i, rows) + proj_b[...])
            n, _r = norm_rows(middle)
            sec[i, rows, :] = (n * (1.0 + vec(i, 3)) + vec(i, 5)).astype(BF16)
            d = (cot[i, rows, :].astype(F32) * vec(i, 1)).astype(BF16)
            dbr[i, rows, :] = d
            return total + fold(d.astype(F32))
        total = lax.fori_loop(0, n_ln, body, jnp.zeros((8, width), F32))
        sm[2, 0:1, :] = sm[2, 0:1, :] + jnp.sum(total, axis=0, keepdims=True)

        def column(j, _):
            cols = pl.ds(pl.multiple_of(j * 256, 256), 256)

            def body(t, _):
                rows = rows_of(t, mt)
                u = dot(sec[i, rows, :], fc1w[:, cols]) + fc1_b[j]
                dh = dot(dbr[i, rows, :], fc2w[cols, :], NT)
                th = jnp.tanh(GELU_C * (u + GELU_A * u * u * u))
                hid[i, rows, cols] = (0.5 * u * (1.0 + th)).astype(BF16)
                slope = 0.5 * (1.0 + th) + 0.5 * u * (1.0 - th * th) * (GELU_C + (3.0 * GELU_C * GELU_A) * u * u)
                d = (dh * slope).astype(BF16)
                dup[i, j, rows, :] = d
                fb1[j] = fb1[j] + fold(d.astype(F32))
                return 0
            lax.fori_loop(0, 2, body, 0)
            return 0
        lax.fori_loop(0, dup.shape[1], column, 0)

        def back(t, _):
            rows = rows_of(t, mt)
            d = jnp.concatenate([dup[i, j, rows, :] for j in range(dup.shape[1])], axis=1)
            for h in (0, 1):
                dst[i, h, rows, :] = dot(d, fc1w[h * half:(h + 1) * half, :], NT)
            return 0
        lax.fori_loop(0, 2, back, 0)

    def half_of(n, h, buf=None):
        return (grads if buf is None else buf).at[n, pl.ds(pl.multiple_of(h * 128, 128), 128)]

    def to_dp(src, to, send, recv, mate):
        return pltpu.make_async_remote_copy(
            src_ref=src, dst_ref=to, send_sem=send, recv_sem=recv, device_id={"dp": mate}, device_id_type=MESH)

    def own(n):
        return xb if n in X_CHUNKS else zh

    def x1(n):
        h = 1 - xb if n in X_CHUNKS else zh
        return to_dp(half_of(n, h), x_in.at[n], x1_s.at[n], x1_r.at[n], x_mate)

    def zin(n):
        if n in X_CHUNKS:
            return to_dp(half_of(n, xb), z_in.at[n, pl.ds(0, 128)], zi_s.at[n], zi_r.at[n], z_mate)
        return to_dp(grads.at[n], z_in.at[n], zi_s.at[n], zi_r.at[n], z_mate)

    def mid(n):
        h = xb if n in X_CHUNKS else 1 - zh
        return to_dp(half_of(n, h), mid_in.at[n], mi_s.at[n], mi_r.at[n], mid_mate)

    def zout(n):
        view = half_of(n, xb, final) if n in X_CHUNKS else final.at[n]
        return to_dp(view, view, zo_s.at[n], zo_r.at[n], z_mate)

    def x2(n):
        return to_dp(half_of(n, xb, final), half_of(n, xb, final), x2_s.at[n], x2_r.at[n], x_mate)

    def swap(n):
        return to_dp(half_of(n, zh, final), half_of(n, zh, final), x2_s.at[n], x2_r.at[n], mid_mate)

    def add_all(pairs, then):
        def load(k):
            rows = pl.ds((k % 2) * 128, 128)
            return [pltpu.make_async_copy(pairs[k][c], stage.at[c, rows], load_sem.at[c, k % 2]) for c in (0, 1)]

        def store(k):
            return pltpu.make_async_copy(stage.at[0, pl.ds((k % 2) * 128, 128)], pairs[k][2 if len(pairs[k]) == 3 else 0], store_sem.at[k % 2])

        def finish(k):
            store(k).wait()
            then(k)
        for copy in load(0):
            copy.start()
        for k in range(len(pairs)):
            if k >= 1:
                finish(k - 1)
            if k + 1 < len(pairs):
                for copy in load(k + 1):
                    copy.start()
            for copy in load(k):
                copy.wait()

            def add(t, _, k=k):
                rows = pl.ds(pl.multiple_of((k % 2) * 128 + t * 16, 16), 16)
                stage[0, rows, :] = stage[0, rows, :] + stage[1, rows, :]
                return 0
            lax.fori_loop(0, 8, add, 0)
            store(k).start()
        finish(len(pairs) - 1)

    def at_edge(body):
        pl.when(edge)(body)

    def at_inner(body):
        pl.when(inner)(body)

    def mid_sum(n, to, then):
        for k in range(n_rest):
            source = mid_in.at[n] if k == 0 else rest_in.at[k - 1, n]
            add_all([(half_of(n, own(n)), source)], lambda _: None)
            copy = to_dp(half_of(n, own(n)), rest_in.at[k, n], re_s.at[k, n], re_r.at[k, n], rest_mates[k])
            copy.start()
            copy.wait()
        source = rest_in.at[n_rest - 1, n] if n_rest else mid_in.at[n]
        add_all([(half_of(n, own(n)), source, half_of(n, own(n), to))], lambda _: then())

    def launch(n):
        if n in X_CHUNKS:
            x1(n).start()
        else:
            at_edge(lambda: zin(n).start())

    def s2(*ns):
        for n in ns:
            if n in X_CHUNKS:
                x1(n).wait()
                add_all([(half_of(n, xb), x_in.at[n])], lambda _: at_edge(lambda: zin(n).start()))
            else:
                @at_inner
                def _():
                    zin(n).wait_recv()
                    view = lambda h: z_in.at[n, pl.ds(pl.multiple_of(h * 128, 128), 128)]
                    add_all([(half_of(n, 1 - zh), view(1 - zh)), (half_of(n, zh), view(zh))],
                            lambda k: mid(n).start() if k == 0 else None)

    def s3(*ns):
        for n in ns:
            @at_inner
            def _():
                if n in X_CHUNKS:
                    zin(n).wait_recv()
                    add_all([(half_of(n, xb), z_in.at[n, pl.ds(0, 128)])], lambda _: mid(n).start())
                else:
                    mid(n).wait()
                    mid_sum(n, grads, lambda: x1(n).start())

    def s4(*ns):
        for n in ns:
            @at_inner
            def _():
                if n in X_CHUNKS:
                    mid(n).wait()
                    mid_sum(n, final, lambda: (zout(n).start(), x2(n).start()))
                else:
                    x1(n).wait()
                    add_all([(half_of(n, zh), x_in.at[n], half_of(n, zh, final))], lambda _: swap(n).start())

    def s5(*ns):
        for n in ns:
            if n in X_CHUNKS:
                @at_edge
                def _():
                    zin(n).wait_send()
                    zout(n).wait_recv()
                    x2(n).start()
            else:
                @at_inner
                def _():
                    swap(n).wait()
                    zout(n).start()

    def s6(*ns):
        for n in ns:
            if n in X_CHUNKS:
                x2(n).wait()
            else:
                @at_edge
                def _():
                    zin(n).wait_send()
                    zout(n).wait_recv()
            at_inner(lambda: zout(n).wait_send())

    def put(slot, n):
        return pltpu.make_async_copy(stage.at[slot], grads.at[n], store_sem.at[slot])

    def produce(ns, make):
        for k, n in enumerate(ns):
            make(k % 2, n)
            put(k % 2, n).start()
            if k >= 1:
                put((k - 1) % 2, ns[k - 1]).wait()
                launch(ns[k - 1])
        put((len(ns) - 1) % 2, ns[-1]).wait()
        launch(ns[-1])

    def both(ref, *rest):
        return jnp.concatenate([ref[(0, *rest)], ref[(1, *rest)]], axis=0)

    def fc_grads(ns):
        def make(slot, n):
            j = n % 4
            cols = pl.ds(j * 256, 256)
            if n < 4:
                stage[slot] = dot(both(hid, slice(None), cols), both(dbr), TN)
            else:
                d = jnp.concatenate([both(dup, m) for m in range(4)], axis=1)
                stage[slot] = dot(both(sec, slice(None), cols), d, TN)
        produce(ns, make)

    def attention_grads(ns):
        def make(slot, n):
            if n == 8:
                for slab in (0, 1):
                    stage[slot, slab * 128:(slab + 1) * 128, :] = dot(both(mix, slab), both(sec), TN)
            else:
                def piece(j, _):
                    cols = pl.ds(pl.multiple_of(j * 256, 256), 256)
                    stage[slot, :, cols] = dot(both(fst, slice(None), cols), both(dup, n - 9), TN)
                    return 0
                lax.fori_loop(0, 4, piece, 0)
        produce(ns, make)

    def second_back(i):
        zero = jnp.zeros((8, width), F32)

        def body(t, sums):
            rows = rows_of(t, LN_TILE)
            attended = wide(att, i, rows) + proj_b[...]
            n, r = norm_rows(tok[i, rows, :].astype(F32) + vec(i, 0) * attended)
            dy = wide(dst, i, rows)
            dn = dy * (1.0 + vec(i, 3))
            dm = cot[i, rows, :].astype(F32) + r * (
                dn - jnp.mean(dn, axis=-1, keepdims=True) - n * jnp.mean(dn * n, axis=-1, keepdims=True))
            put_wide(dst, i, rows, dm)
            da = (dm * vec(i, 0)).astype(BF16)
            sec[i, rows, :] = da
            return (sums[0] + fold(dm * attended), sums[1] + fold(dy * n), sums[2] + fold(dy), sums[3] + fold(da.astype(F32)))
        sums = lax.fori_loop(0, n_ln, body, (zero, zero, zero, zero))
        for k, s in zip((0, 3, 5), sums[:3]):
            sm[i, k:k + 1, :] = jnp.sum(s, axis=0, keepdims=True)
        sm[2, 2:3, :] = sm[2, 2:3, :] + jnp.sum(sums[3], axis=0, keepdims=True)

        def mixed(t, _):
            rows = rows_of(t, mt)
            d = dot(sec[i, rows, :], projw[...], NT)
            dmx[0, rows, :] = d[:, :128].astype(BF16)
            dmx[1, rows, :] = d[:, 128:].astype(BF16)
            return 0
        lax.fori_loop(0, 2, mixed, 0)

    def attend_back(i, slab):
        blocks = blocks_of(128)
        fill_kv(i, slab)
        acc[...] = jnp.zeros_like(acc)

        def body(rows, keys):
            p = exps(i, slab, rows, keys)
            d = dmx[slab, rows, :]
            q = qkn[i, 0, slab, rows, :]
            ds = []
            dp_both = dot(d, kv[1, :, 0:keys, :].reshape(2 * keys, 128), NT)
            for h in (0, 1):
                dpr = dp_both[:, h * keys:(h + 1) * keys]
                ds.append((p[h] * (dpr - jnp.sum(dpr * p[h], axis=-1, keepdims=True))).astype(BF16))
            acc[0, rows, :] = dot(jnp.concatenate(ds, axis=1), kv[0, :, 0:keys, :].reshape(2 * keys, 128))
            kr = pl.ds(0, keys)
            acc[1, kr, :] += dot(
                jnp.concatenate(ds, axis=0), jnp.concatenate([q * one_head(h) for h in (0, 1)], axis=0), TN)
            acc[2, kr, :] += dot(
                jnp.concatenate([v.astype(BF16) for v in p], axis=0),
                jnp.concatenate([d * one_head(h) for h in (0, 1)], axis=0), TN)
        each_tile(body)
        es = es_row[:, slab * 128:(slab + 1) * 128]

        def close(t, sums):
            rows = rows_of(t, LN_TILE)

            def unit(c, g):
                at = c * 256 + slab * 128
                pre = qk[i, rows, at:at + 128]
                r = lax.rsqrt(head_sum(pre * pre, blocks) + EPSILON)
                u = pre * r
                gu = g * u
                return r * (g - u * head_sum(gu, blocks)), gu
            dq, gu = unit(0, acc[0, rows, :] * es)
            dk, _g = unit(1, acc[1, rows, :])
            dq, dk, dv = dq.astype(BF16), dk.astype(BF16), acc[2, rows, :].astype(BF16)
            to = pl.ds(slab * 128, 128)
            dup[i, 0, rows, to] = dq
            dup[i, 1, rows, to] = dk
            dup[i, 2, rows, to] = dv
            return sums[0] + fold(dq.astype(F32)), sums[1] + fold(dv.astype(F32)), sums[2] + fold(gu)
        zero = jnp.zeros((8, 128), F32)
        sums = lax.fori_loop(0, n_ln, close, (zero, zero, zero))
        for k in range(3):
            lanes[k, slab] = lanes[k, slab] + sums[k]

    def first_grad(i):
        def body(t, _):
            rows = rows_of(t, mt)
            for h in (0, 1):
                total = None
                for c in range(3):
                    o = dot(dup[i, c, rows, :], qkvw[c, h * half:(h + 1) * half, :], NT)
                    total = o if total is None else total + o
                dfr[i, h, rows, :] = total
            return 0
        lax.fori_loop(0, 2, body, 0)

    def first_back(i):
        zero = jnp.zeros((8, width), F32)

        def body(t, sums):
            rows = rows_of(t, LN_TILE)
            n, r = norm_rows(tok[i, rows, :].astype(F32))
            dy = wide(dfr, i, rows)
            dn = dy * (1.0 + vec(i, 2))
            g = wide(dst, i, rows) + r * (
                dn - jnp.mean(dn, axis=-1, keepdims=True) - n * jnp.mean(dn * n, axis=-1, keepdims=True))
            fst[i, rows, :] = g.astype(BF16)
            return sums[0] + fold(dy * n), sums[1] + fold(dy)
        sums = lax.fori_loop(0, n_ln, body, (zero, zero))
        for k, s in zip((2, 4), sums):
            sm[i, k:k + 1, :] = jnp.sum(s, axis=0, keepdims=True)
        pltpu.make_async_copy(fst.at[i], tg_hbm.at[i], out_sem.at[i]).start()

    def branch(i):
        def body(t, _):
            rows = rows_of(t, mt)
            for h in (0, 1):
                dst[i, h, rows, :] = dot(hid[i, rows, :], fc2w[:, h * half:(h + 1) * half])
            return 0
        lax.fori_loop(0, 2, body, 0)

        def sums_of(t, sums):
            rows = rows_of(t, LN_TILE)
            g = cot[i, rows, :].astype(F32)
            return sums[0] + fold(g * wide(dst, i, rows)), sums[1] + fold(g)
        zero = jnp.zeros((8, width), F32)
        sums = lax.fori_loop(0, n_ln, sums_of, (zero, zero))
        g2r[me, i:i + 1, :] = jnp.sum(sums[0], axis=0, keepdims=True)
        sm[i, 1:2, :] = fc2_b[...] * jnp.sum(sums[1], axis=0, keepdims=True)

    def block_end(i):
        def body(t, _):
            rows = rows_of(t, LN_TILE)
            middle = tok[i, rows, :].astype(F32) + vec(i, 0) * (wide(att, i, rows) + proj_b[...])
            cot[i, rows, :] = (middle + vec(i, 1) * (wide(dst, i, rows) + fc2_b[...])).astype(BF16)
            return 0
        lax.fori_loop(0, n_ln, body, 0)
        pltpu.make_async_copy(cot.at[i], out_hbm.at[i], out_sem.at[2 + i]).start()

    def every_copy(to, source):
        return pltpu.make_async_remote_copy(
            src_ref=sm, dst_ref=every.at[source], send_sem=ev_s.at[to], recv_sem=ev_r.at[source],
            device_id={"dp": to}, device_id_type=MESH)

    def every_start():
        pltpu.make_async_copy(sm, every.at[dp], out_sem.at[4]).start()

        def body(step, _):
            every_copy(lax.rem(dp + step, n_dp), dp).start()
            return 0
        lax.fori_loop(1, n_dp, body, 0)

    def every_finish():
        pltpu.make_async_copy(sm, every.at[dp], out_sem.at[4]).wait()

        def body(step, _):
            every_copy(lax.rem(dp + step, n_dp), dp).wait_send()
            source = lax.rem(dp + n_dp - step, n_dp)
            every_copy(source, source).wait_recv()
            return 0
        lax.fori_loop(1, n_dp, body, 0)

    def ag(buf, i, k):
        ag_copy(buf, i, k).start()
        ag_copy(buf, i, k).wait()

    sm[...] = jnp.zeros_like(sm)
    fb1[...] = jnp.zeros_like(fb1)
    lanes[...] = jnp.zeros_like(lanes)
    g2r[...] = jnp.zeros_like(g2r)
    kv[...] = jnp.zeros_like(kv)
    for i in (0, 1):
        sm[i, 6:7, :] = jnp.zeros((1, width), F32) + labels[i].astype(F32)
    loads["tok"].wait()
    for i in (0, 1):
        first_norm(i)
        if i == 0:
            loads["qkvw"].wait()
        project(i)
        if i == 0:
            loads["lim"].wait()
        attend(i)
        if i == 0:
            loads["projw"].wait()
        attend_out(i)
        rs_copy(att, i, ATT).start()
        rs_finish(att, i, ATT)
        y_copy(att, i, ATT).start()
    for name in ("cot", "fc1w", "fc2w"):
        loads[name].wait()

    y_finish(att, 0, ATT)
    ag(att, 0, ATT)
    mlp(0)
    rs_copy(dst, 0, DS).start()
    rs_finish(dst, 0, DS)
    y_copy(dst, 0, DS).start()

    y_finish(att, 1, ATT)
    ag(att, 1, ATT)
    mlp(1)
    rs_copy(dst, 1, DS).start()
    fc_grads((4, 0, 5, 1))
    rs_finish(dst, 1, DS)
    y_copy(dst, 1, DS).start()
    fc_grads((6, 2, 7, 3))

    y_finish(dst, 0, DS)
    ag(dst, 0, DS)
    second_back(0)
    attend_back(0, 0)
    s2(4)
    attend_back(0, 1)
    first_grad(0)
    rs_copy(dfr, 0, DF).start()
    s3(4)
    rs_finish(dfr, 0, DF)
    y_copy(dfr, 0, DF).start()
    s2(5)

    y_finish(dst, 1, DS)
    ag(dst, 1, DS)
    second_back(1)
    s2(0, 1, 2, 3)
    attend_back(1, 0)
    s4(4)
    s3(5)
    attend_back(1, 1)
    first_grad(1)
    rs_copy(dfr, 1, DF).start()
    s2(6)
    rs_finish(dfr, 1, DF)
    y_copy(dfr, 1, DF).start()
    s5(4)
    s4(5)
    attention_grads((10, 11, 8, 9))

    y_finish(dfr, 0, DF)
    ag(dfr, 0, DF)
    first_back(0)
    s3(6)
    s2(7)
    s5(5)
    s4(6)
    branch(0)
    rs_copy(dst, 0, BR).start()
    s3(7)
    rs_finish(dst, 0, BR)
    y_copy(dst, 0, BR).start()
    s3(0)
    s5(6)
    s3(1)

    y_finish(dfr, 1, DF)
    ag(dfr, 1, DF)
    first_back(1)
    branch(1)
    rs_copy(dst, 1, BR).start()
    s4(7, 0)
    rs_finish(dst, 1, BR)
    y_copy(dst, 1, BR).start()

    sent = share(g2r, g2_s, g2_r)
    for copy in sent:
        copy.wait()
    total = (g2r[0] + g2r[1]) + (g2r[2] + g2r[3])
    for i in (0, 1):
        sm[i, 1:2, :] = sm[i, 1:2, :] + total[i:i + 1, :]
    for j in range(4):
        sm[2, 1:2, j * 256:(j + 1) * 256] = jnp.sum(fb1[j], axis=0, keepdims=True)
    for k in range(3):
        for slab in (0, 1):
            at = k * 256 + slab * 128
            sm[2, 3:4, at:at + 128] = jnp.sum(lanes[k, slab], axis=0, keepdims=True)
    every_start()
    s2(8, 9)
    s3(2)
    s4(1)
    s5(7)
    s3(3)
    s4(2)

    y_finish(dst, 0, BR)
    ag(dst, 0, BR)
    block_end(0)
    s4(3)
    s5(0, 1)
    s2(10)
    s6(4, 5)
    s3(10)
    s5(2, 3)
    y_finish(dst, 1, BR)
    ag(dst, 1, BR)
    block_end(1)
    s2(11)
    s4(10)
    s3(11)
    s3(8)
    s5(10)
    s3(9)
    s4(11)
    s4(8)
    s5(11)
    s4(9)
    s5(8, 9)
    every_finish()
    s6(0, 1, 2, 3, 6, 7, 10, 11, 8, 9)
    for i in (0, 1):
        pltpu.make_async_copy(fst.at[i], tg_hbm.at[i], out_sem.at[i]).wait()
        pltpu.make_async_copy(cot.at[i], out_hbm.at[i], out_sem.at[2 + i]).wait()


def run_block(n_dp, mod_part, ada_b, tok, cot, stops, labels, qkvw, projw, fc1w, fc2w, qv_b, es_row, proj_b, fc1_b, fc2_b, slots):
    items, padded, width = tok.shape
    half = width // 2
    hidden = fc1w.shape[1]
    n_chunks = 12
    n_rest = max(1, (n_dp // 8).bit_length() - 1)
    ends = np.cumsum(np.array([s * s for s in SIDE_LIST]))
    level = np.minimum(np.searchsorted(ends, np.arange(padded), side="right"), len(SIDE_LIST) - 1)
    lim = jnp.asarray(np.broadcast_to(ends[level][:, None], (padded, 128)), jnp.int32)
    hbm = pl.BlockSpec(memory_space=pl.ANY)
    vmem = pl.BlockSpec(memory_space=pltpu.VMEM)
    smem = pl.BlockSpec(memory_space=pltpu.SMEM)
    wide_b = (items, padded, width)
    wide_f = (items, 2, padded, half)
    dma = pltpu.SemaphoreType.DMA
    return pl.pallas_call(
        functools.partial(block_kernel, slots, n_dp),
        out_shape=(
            jax.ShapeDtypeStruct(wide_b, BF16), jax.ShapeDtypeStruct(wide_b, BF16),
            jax.ShapeDtypeStruct((n_chunks, 256, width), F32), jax.ShapeDtypeStruct((n_dp, 3, 8, width), F32),
            jax.ShapeDtypeStruct((n_chunks, 256, width), F32),
            jax.ShapeDtypeStruct((n_chunks, 128, width), F32), jax.ShapeDtypeStruct((n_chunks, 256, width), F32),
            jax.ShapeDtypeStruct((n_chunks, 128, width), F32), jax.ShapeDtypeStruct((n_rest, n_chunks, 128, width), F32),
        ),
        in_specs=[vmem, vmem, hbm, hbm, smem, smem, hbm, hbm, hbm, hbm, hbm, vmem, vmem, vmem, vmem, vmem],
        out_specs=(hbm,) * 9,
        scratch_shapes=[
            *[pltpu.VMEM(wide_b, BF16) for _ in range(5)],
            pltpu.VMEM((items, padded, hidden), BF16), pltpu.VMEM((items, hidden // 256, padded, 256), BF16),
            *[pltpu.VMEM(wide_f, F32) for _ in range(3)],
            pltpu.VMEM((items, padded, half), F32),
            pltpu.VMEM((items, 3, 2, padded, 128), BF16),
            pltpu.VMEM((items, 2, padded, 128), BF16),
            pltpu.VMEM((2, padded, 128), BF16),
            pltpu.VMEM((2, 2, 768, 128), BF16),
            pltpu.VMEM((3, 768, 128), F32),
            pltpu.VMEM((items, slots, half), F32),
            pltpu.VMEM((items, slots, half), F32),
            pltpu.VMEM(qkvw.shape, BF16), pltpu.VMEM(projw.shape, BF16),
            pltpu.VMEM(fc1w.shape, BF16), pltpu.VMEM(fc2w.shape, BF16),
            pltpu.VMEM((padded, 128), jnp.int32),
            pltpu.VMEM((2, 256, width), F32),
            pltpu.VMEM((4, items, 8, width), F32), pltpu.VMEM((items, 8, width), F32),
            pltpu.VMEM((4, 8, width), F32),
            pltpu.VMEM((4, 8, 256), F32), pltpu.VMEM((3, 2, 8, 128), F32), pltpu.VMEM((3, 8, width), F32),
            dma((7,)), dma((5,)), dma((2, 2)), dma((2,)),
            dma((3,)), dma((3,)), dma((3,)), dma((3,)),
            *[dma((8,)) for _ in range(6)],
            *[dma((n_chunks,)) for _ in range(10)],
            dma((n_rest, n_chunks)), dma((n_rest, n_chunks)), dma((n_dp,)), dma((n_dp,)),
        ],
        compiler_params=pltpu.CompilerParams(
            collective_id=0, has_side_effects=True, vmem_limit_bytes=62 * 2**20),
        name="block",
    )(mod_part, ada_b, tok, cot, stops, labels, lim, qkvw, projw, fc1w, fc2w, qv_b, es_row, proj_b, fc1_b, fc2_b)


def shards(
    n_dp, tokens, cotangent, stop_scales, labels, class_table, ada_weight, ada_bias, qkv_weight, qv_bias, log_scale,
    proj_weight, proj_bias, fc1_weight, fc1_bias, fc2_weight, fc2_bias,
):
    items, slots, width = tokens.shape
    padded = -(-slots // LN_TILE) * LN_TILE
    classes = class_table.shape[0]
    class_local = jnp.concatenate(
        [lax.dynamic_slice_in_dim(class_table, labels[i], 1, 0) for i in range(items)], axis=0).astype(F32)
    lifted = jax.nn.silu(class_local).astype(BF16)
    part = jnp.dot(lifted, ada_weight, preferred_element_type=F32).reshape(items, 6, width)
    part = jnp.pad(part, ((0, 0), (0, 2), (0, 0)))
    ada_rows = jnp.pad(ada_bias.reshape(1, 6, width), ((0, 0), (0, 2), (0, 0)))
    tok = jnp.pad(tokens, ((0, 0), (0, padded - slots), (0, 0)))
    cot = jnp.pad(cotangent, ((0, 0), (0, padded - slots), (0, 0)))
    heads = log_scale.shape[0]
    es_row = jnp.repeat(jnp.exp(log_scale), qkv_weight.shape[2] // heads)[None, :]
    out, tg, grads, every, *_ = run_block(
        n_dp, part, ada_rows, tok, cot, stop_scales, labels, jnp.transpose(qkv_weight, (1, 0, 2)), proj_weight, fc1_weight, fc2_weight,
        qv_bias, es_row, proj_bias[None, :], fc1_bias.reshape(-1, 1, 256), fc2_bias[None, :], slots)

    small = jnp.sum(every[:, 2], axis=0)
    every = every[:, :2].reshape(-1, 8, width)
    every_label = every[:, 6, 0]
    class_hot = every_label[:, None] == jnp.arange(classes, dtype=F32)[None, :]
    dmod = every[:, :6].reshape(-1, 6 * width)
    dmod = jnp.where(every_label[:, None] >= 0, dmod, 0.0).astype(BF16)
    every_class = jnp.dot(class_hot.astype(BF16), class_table, preferred_element_type=F32)
    every_lift = jax.nn.silu(every_class).astype(BF16)
    lifted_grad = jnp.einsum("ik,dk->id", dmod, ada_weight, preferred_element_type=F32)
    class_grad = jax.vjp(jax.nn.silu, every_class)[1](lifted_grad)[0]
    table_grad = jnp.einsum("ic,id->cd", class_hot.astype(F32), class_grad, precision=lax.Precision.HIGHEST)
    ada_weight_grad = jnp.einsum("id,ik->dk", every_lift, dmod, preferred_element_type=F32)
    ada_bias_grad = jnp.sum(dmod.astype(F32), axis=0)
    g2 = grads[0:4].reshape(-1, width)
    g1 = grads[4:8].reshape(-1, width)
    gp = grads[8]
    gq = jnp.transpose(grads[9:12].reshape(3, 256, 4, 256), (2, 1, 0, 3)).reshape(width, 3, 256)
    lanes = small[3]
    return (
        out[:, :slots], tg[:, :slots], table_grad, ada_weight_grad, ada_bias_grad,
        gq, lanes[:512].reshape(2, 256), lanes[512:768].reshape(heads, -1).sum(axis=1),
        gp, small[2], g1, small[1], g2, small[0],
    )


def solution(mesh):
    return jax.shard_map(
        functools.partial(shards, mesh.shape["dp"]),
        mesh=mesh,
        in_specs=(
            P("dp", None, None), P("dp", None, None), P("dp"), P("dp"), P(None, "mp"), P("mp", None), P(),
            P(None, None, "mp"), P(None, "mp"), P("mp"), P("mp", None), P(), P(None, "mp"), P("mp"), P("mp", None), P(),
        ),
        out_specs=(
            P("dp", None, None), P("dp", None, None), P(None, "mp"), P("mp", None), P(), P(None, None, "mp"), P(None, "mp"),
            P("mp"), P("mp", None), P(), P(None, "mp"), P("mp"), P("mp", None), P(),
        ),
        check_vma=False,
    )
```

```python
import functools

import jax
import jax.numpy as jnp
import numpy as np
from jax import lax
from jax.experimental import pallas as pl
from jax.experimental.pallas import tpu as pltpu
from jax.sharding import PartitionSpec as P

SIDE_LIST = (1, 2, 3, 4, 5, 6, 8, 10, 13, 16)
EPSILON = 1e-06
MESH = pl.DeviceIdType.MESH
F32, BF16 = jnp.float32, jnp.bfloat16
GELU_C = 0.7978845608028654
GELU_A = 0.044715
LN_TILE = 64
NT = (((1,), (1,)), ((), ()))
TN = (((0,), (0,)), ((), ()))
NN = (((1,), (0,)), ((), ()))
ATT, DS, DF, BR = 0, 2, 4, 6
X_CHUNKS = (0, 1, 2, 3, 4, 5, 8, 9, 10)


def dot(a, b, dims=NN):
    return lax.dot_general(a, b, dims, preferred_element_type=F32)


def norm_rows(v):
    center = v - jnp.mean(v, axis=-1, keepdims=True)
    scale = lax.rsqrt(jnp.mean(center * center, axis=-1, keepdims=True) + EPSILON)
    return center * scale, scale


def fold(v):
    return jnp.sum(v.reshape(v.shape[0] // 8, 8, v.shape[1]), axis=0)


def head_sum(v, blocks):
    high = v.astype(BF16)
    rest = (v - high.astype(F32)).astype(BF16)
    return dot(high, blocks) + dot(rest, blocks)


def block_kernel(
    slots, n_dp,
    mod_part, ada_b, tok_hbm, cot_hbm, stops, labels,
    qkvw_hbm, projw_hbm, fc1w_hbm, fc2w_hbm,
    qv_b, es_row, proj_b, fc1_b, fc2_b,
    out_hbm, tg_hbm, final, every, x_out, x_in, z_in, mid_in, rest_in, spill,
    tok, cot, sec, dbr, hid, dup,
    att, dst,
    qk, qkn, mix, dmx, kv, acc,
    rs_buf, y_buf,
    qkvw, projw, fc1w, fc2w,
    px, pz, stage, extra, modr, mod, g2r, fb1, lanes, sm,
    in_sem, out_sem, load_sem, store_sem, keep_sem, final_sem, spill_sem, y_free,
    mod_s, mod_r, g2_s, g2_r, rs_s, rs_r, y_s, y_r, ag_s, ag_r,
    x1_s, x1_r, zi_s, zi_r, mi_s, mi_r, zo_s, zo_r, x2_s, x2_r, zb_s, zb_r, zc_s, zc_r, re_s, re_r, ev_s, ev_r,
):
    items, padded, width = tok.shape
    half = width // 2
    me = lax.axis_index("mp")
    dp = lax.axis_index("dp")
    xb = lax.rem(dp, 2)
    z = lax.rem(dp // 2, 4)
    zh = z // 2
    inner = jnp.logical_or(z == 1, z == 2)
    edge = jnp.logical_or(z == 0, z == 3)
    x_mate = dp + 1 - 2 * xb
    z_mate = dp + 2 - 4 * lax.rem(z, 2)
    mid_mate = jnp.where(z == 1, dp + 2, jnp.where(z == 2, dp - 2, dp))
    n_rest = rest_in.shape[0] if n_dp > 8 else 0
    rest_mates = [dp + (8 << k) * (1 - 2 * lax.rem(dp // (8 << k), 2)) for k in range(n_rest)]
    core = lax.rem(me, 2)
    core_mate = me + 1 - 2 * core
    y_mate = lax.rem(me + 2, 4)
    n_ln = padded // LN_TILE
    mt = padded // 2

    def rows_of(t, n):
        return pl.ds(pl.multiple_of(t * n, n), n)

    loads = {}
    for k, (name, src, to) in enumerate((
        ("tok", tok_hbm, tok), ("qkvw", qkvw_hbm, qkvw),
        ("projw", projw_hbm, projw), ("cot", cot_hbm, cot),
        ("fc1w", fc1w_hbm, fc1w), ("fc2w", fc2w_hbm, fc2w),
    )):
        loads[name] = pltpu.make_async_copy(src, to, in_sem.at[k])
        loads[name].start()

    barrier = pltpu.get_barrier_semaphore()
    for step in (1, 2, 3):
        pl.semaphore_signal(barrier, inc=1, device_id={"mp": lax.rem(me + step, 4)}, device_id_type=MESH)
    def greet(step, _):
        pl.semaphore_signal(barrier, inc=1, device_id={"dp": lax.rem(dp + step, n_dp)}, device_id_type=MESH)
        return 0
    lax.fori_loop(1, n_dp, greet, 0)
    pl.semaphore_wait(barrier, 3 + n_dp - 1)

    def share(buf, send, recv):
        copies = []
        for step in (1, 2, 3):
            copies.append(pltpu.make_async_remote_copy(
                src_ref=buf.at[me], dst_ref=buf.at[me], send_sem=send.at[step - 1], recv_sem=recv.at[step - 1],
                device_id={"mp": lax.rem(me + step, 4)}, device_id_type=MESH))
        for copy in copies:
            copy.start()
        return copies

    modr[me] = mod_part[...]
    sent = share(modr, mod_s, mod_r)
    for copy in sent:
        copy.wait()
    mod[...] = ((modr[0] + modr[1]) + (modr[2] + modr[3])) + ada_b[...]

    def vec(i, k):
        return mod[i, k:k + 1, :]

    def rs_copy(buf, i, k):
        return pltpu.make_async_remote_copy(
            src_ref=buf.at[i, 1 - core, pl.ds(0, slots)], dst_ref=rs_buf.at[i], send_sem=rs_s.at[k + i], recv_sem=rs_r.at[k + i],
            device_id={"mp": core_mate}, device_id_type=MESH)

    def y_copy(buf, i, k):
        dst = qk.at[i, pl.ds(0, slots)] if k == BR else y_buf.at[i]
        return pltpu.make_async_remote_copy(
            src_ref=buf.at[i, core, pl.ds(0, slots)], dst_ref=dst, send_sem=y_s.at[k + i], recv_sem=y_r.at[k + i],
            device_id={"mp": y_mate}, device_id_type=MESH)

    def ag_copy(buf, i, k):
        return pltpu.make_async_remote_copy(
            src_ref=buf.at[i, core, pl.ds(0, slots)], dst_ref=buf.at[i, core, pl.ds(0, slots)],
            send_sem=ag_s.at[k + i], recv_sem=ag_r.at[k + i],
            device_id={"mp": core_mate}, device_id_type=MESH)

    add_rows = slots // 5

    def rs_finish(buf, i, k):
        rs_copy(buf, i, k).wait()

        def add(t, _):
            rows = rows_of(t, add_rows)
            buf[i, core, rows, :] = buf[i, core, rows, :] + rs_buf[i, rows, :]
            return 0
        lax.fori_loop(0, 5, add, 0)

    def y_finish(buf, i, k):
        y_copy(buf, i, k).wait()

        def add(t, _):
            rows = rows_of(t, add_rows)
            other = qk[i, rows, :] if k == BR else y_buf[i, rows, :]
            buf[i, core, rows, :] = buf[i, core, rows, :] + other
            return 0
        lax.fori_loop(0, 5, add, 0)
        if k in (ATT, DS):
            pl.semaphore_signal(y_free.at[i], inc=1, device_id={"mp": y_mate}, device_id_type=MESH)

    def y_start(buf, i, k):
        if k in (DS, DF):
            pl.semaphore_wait(y_free.at[i], 1)
        y_copy(buf, i, k).start()

    def wide(buf, i, rows):
        return jnp.concatenate([buf[i, 0, rows, :], buf[i, 1, rows, :]], axis=1)

    def put_wide(buf, i, rows, v):
        buf[i, 0, rows, :] = v[:, :half]
        buf[i, 1, rows, :] = v[:, half:]

    def blocks_of(n):
        a = lax.broadcasted_iota(jnp.int32, (n, n), 0) // 64
        b = lax.broadcasted_iota(jnp.int32, (n, n), 1) // 64
        return jnp.where(a == b, 1.0, 0.0).astype(BF16)

    ends = np.cumsum(np.array([s * s for s in SIDE_LIST]))
    tiles = ((0, 240, 1, 256), (240, 176, 1, 512), (416, 96, 3, 768))

    def keep_of(i, rows, keys):
        live = jnp.int32(0)
        for s in range(len(SIDE_LIST)):
            live = jnp.where(stops[i] == s + 1, int(ends[s]), live)
        n = rows.size
        at = rows.start + lax.broadcasted_iota(jnp.int32, (n, 1), 0)
        bound = jnp.full((n, 1), int(ends[0]), jnp.int32)
        for s in range(1, len(SIDE_LIST)):
            bound = jnp.where(at >= int(ends[s - 1]), int(ends[s]), bound)
        bound = jnp.minimum(bound, live)
        return lax.broadcasted_iota(jnp.int32, (n, keys), 1) < bound

    def one_head(h):
        lane = lax.broadcasted_iota(jnp.int32, (1, 128), 1) // 64
        return jnp.where(lane == h, 1.0, 0.0).astype(BF16)

    def fill_kv(i, slab):
        for c in (0, 1):
            for h in (0, 1):
                kv[c, h, 0:padded, :] = qkn[i, 1 + c, slab] * one_head(h)

    def exps(i, slab, rows, keys):
        keep = keep_of(i, rows, keys)
        s = dot(qkn[i, 0, slab, rows, :], kv[0, :, 0:keys, :].reshape(2 * keys, 128), NT)
        parts = []
        for h in (0, 1):
            e = jnp.where(keep, jnp.exp(s[:, h * keys:(h + 1) * keys]), 0.0)
            parts.append(e * (1.0 / jnp.sum(e, axis=-1, keepdims=True)))
        return parts

    def each_tile(body):
        for first_row, n, steps, keys in tiles:
            if steps == 1:
                body(pl.ds(first_row, n), keys)
            else:
                def step(t, _, first_row=first_row, n=n, keys=keys):
                    body(pl.ds(pl.multiple_of(first_row + t * n, 16), n), keys)
                    return 0
                lax.fori_loop(0, steps, step, 0)

    def first_norm(i):
        def body(t, _):
            rows = rows_of(t, LN_TILE)
            n, _r = norm_rows(tok[i, rows, :].astype(F32))
            dbr[i, rows, :] = (n * (1.0 + vec(i, 2)) + vec(i, 4)).astype(BF16)
            return 0
        lax.fori_loop(0, n_ln, body, 0)

    def project(i):
        blocks = blocks_of(256)

        def body(t, _):
            rows = rows_of(t, mt)
            f = dbr[i, rows, :]
            q = dot(f, qkvw[0]) + qv_b[0:1, :]
            qk[i, rows, 0:256] = q
            u = q * lax.rsqrt(head_sum(q * q, blocks) + EPSILON) * es_row[...]
            qkn[i, 0, 0, rows, :] = u[:, :128].astype(BF16)
            qkn[i, 0, 1, rows, :] = u[:, 128:].astype(BF16)
            k = dot(f, qkvw[1])
            qk[i, rows, 256:512] = k
            u = k * lax.rsqrt(head_sum(k * k, blocks) + EPSILON)
            qkn[i, 1, 0, rows, :] = u[:, :128].astype(BF16)
            qkn[i, 1, 1, rows, :] = u[:, 128:].astype(BF16)
            v = dot(f, qkvw[2]) + qv_b[1:2, :]
            qkn[i, 2, 0, rows, :] = v[:, :128].astype(BF16)
            qkn[i, 2, 1, rows, :] = v[:, 128:].astype(BF16)
            return 0
        lax.fori_loop(0, 2, body, 0)

    def attend(i):
        def slab_body(slab, _):
            fill_kv(i, slab)

            def body(rows, keys):
                p = jnp.concatenate([v.astype(BF16) for v in exps(i, slab, rows, keys)], axis=1)
                o = dot(p, kv[1, :, 0:keys, :].reshape(2 * keys, 128))
                mix[i, slab, rows, :] = o.astype(BF16)
            each_tile(body)
            return 0
        lax.fori_loop(0, 2, slab_body, 0)

    def attend_out(i):
        def body(t, _):
            rows = rows_of(t, mt)
            m = jnp.concatenate([mix[i, 0, rows, :], mix[i, 1, rows, :]], axis=1)
            for h in (0, 1):
                att[i, h, rows, :] = dot(m, projw[:, h * half:(h + 1) * half])
            return 0
        lax.fori_loop(0, 2, body, 0)

    def mlp(i):
        def body(t, total):
            rows = rows_of(t, LN_TILE)
            middle = tok[i, rows, :].astype(F32) + vec(i, 0) * (wide(att, i, rows) + proj_b[...])
            n, _r = norm_rows(middle)
            sec[i, rows, :] = (n * (1.0 + vec(i, 3)) + vec(i, 5)).astype(BF16)
            d = (cot[i, rows, :].astype(F32) * vec(i, 1)).astype(BF16)
            dbr[i, rows, :] = d
            return total + fold(d.astype(F32))
        total = lax.fori_loop(0, n_ln, body, jnp.zeros((8, width), F32))
        sm[2, 0:1, :] = sm[2, 0:1, :] + jnp.sum(total, axis=0, keepdims=True)

        def column(j, _):
            cols = pl.ds(pl.multiple_of(j * 256, 256), 256)

            def body(t, _):
                rows = rows_of(t, mt)
                u = dot(sec[i, rows, :], fc1w[:, cols]) + fc1_b[j]
                dh = dot(dbr[i, rows, :], fc2w[cols, :], NT)
                th = jnp.tanh(GELU_C * (u + GELU_A * u * u * u))
                hid[i, rows, cols] = (0.5 * u * (1.0 + th)).astype(BF16)
                slope = 0.5 * (1.0 + th) + 0.5 * u * (1.0 - th * th) * (GELU_C + (3.0 * GELU_C * GELU_A) * u * u)
                d = (dh * slope).astype(BF16)
                dup[i, j, rows, :] = d
                fb1[j] = fb1[j] + fold(d.astype(F32))
                return 0
            lax.fori_loop(0, 2, body, 0)
            return 0
        lax.fori_loop(0, dup.shape[1], column, 0)

        def back(t, _):
            rows = rows_of(t, mt)
            d = jnp.concatenate([dup[i, j, rows, :] for j in range(dup.shape[1])], axis=1)
            for h in (0, 1):
                dst[i, h, rows, :] = dot(d, fc1w[h * half:(h + 1) * half, :], NT)
            return 0
        lax.fori_loop(0, 2, back, 0)

    x_list = [n for n in range(12) if n in X_CHUNKS]
    z_list = [n for n in range(12) if n not in X_CHUNKS]

    def is_x(n):
        return n in X_CHUNKS

    def side(h):
        return pl.ds(pl.multiple_of(h * 128, 128), 128)

    def own(n):
        return px.at[x_list.index(n)] if is_x(n) else pz.at[z_list.index(n), side(zh)]

    def final_own(n):
        return final.at[n, side(xb if is_x(n) else zh)]

    def to_dp(src, to, send, recv, mate):
        return pltpu.make_async_remote_copy(
            src_ref=src, dst_ref=to, send_sem=send, recv_sem=recv, device_id={"dp": mate}, device_id_type=MESH)

    def x1(n):
        return to_dp(x_out.at[n] if is_x(n) else own(n), x_in.at[n], x1_s.at[n], x1_r.at[n], x_mate)

    def zin(n):
        if is_x(n):
            return to_dp(own(n), z_in.at[n, pl.ds(0, 128)], zi_s.at[n], zi_r.at[n], z_mate)
        return to_dp(far(n), z_in.at[n, side(1 - zh)], zi_s.at[n], zi_r.at[n], z_mate)

    def far(n):
        return pz.at[z_list.index(n), side(1 - zh)]

    def zin_b(n):
        return to_dp(own(n), z_in.at[n, side(zh)], zb_s.at[n], zb_r.at[n], z_mate)

    def mid(n):
        return to_dp(own(n) if is_x(n) else far(n), mid_in.at[n], mi_s.at[n], mi_r.at[n], mid_mate)

    def zout(n):
        return to_dp(own(n), final_own(n), zo_s.at[n], zo_r.at[n], z_mate)

    def zout_b(n):
        view = final.at[n, side(1 - zh)]
        return to_dp(view, view, zc_s.at[n], zc_r.at[n], z_mate)

    def x2(n, at_the_edge=False):
        return to_dp(final_own(n) if at_the_edge else own(n), final_own(n), x2_s.at[n], x2_r.at[n], x_mate)

    def swap(n):
        return to_dp(own(n), final_own(n), x2_s.at[n], x2_r.at[n], mid_mate)

    def store_final(n):
        return pltpu.make_async_copy(own(n), final_own(n), final_sem.at[n])

    def at_edge(body):
        pl.when(edge)(body)

    def at_inner(body):
        pl.when(inner)(body)

    def accumulate(to, what):
        def add(t, _):
            rows = rows_of(t, 16)
            to[rows, :] = to[rows, :] + what[rows, :]
            return 0
        lax.fori_loop(0, 8, add, 0)

    def add_all(items):
        def slot(k):
            return stage.at[(k // 2) % 2, pl.ds((k % 2) * 128, 128)]

        def load(k):
            return pltpu.make_async_copy(items[k][1], slot(k), load_sem.at[k % 4])

        def begin(k):
            items[k][0]()
            load(k).start()
        for k in range(min(2, len(items))):
            begin(k)
        for k in range(len(items)):
            load(k).wait()
            accumulate(items[k][2], slot(k))
            items[k][3]()
            if k + 2 < len(items):
                begin(k + 2)

    def rest_sum(n):
        for k in range(n_rest):
            copy = to_dp(own(n), rest_in.at[k, n], re_s.at[k, n], re_r.at[k, n], rest_mates[k])
            copy.start()
            copy.wait()
            load = pltpu.make_async_copy(rest_in.at[k, n], extra, load_sem.at[4])
            load.start()
            load.wait()
            accumulate(own(n), extra)

    def items_of(step, n):
        if is_x(n):
            if step == 2:
                return [(lambda: x1(n).wait(), x_in.at[n], own(n), lambda: at_edge(lambda: zin(n).start()))]
            if step == 3:
                return [(lambda: zin(n).wait_recv(), z_in.at[n, pl.ds(0, 128)], own(n), lambda: mid(n).start())]

            def close():
                rest_sum(n)
                zout(n).start()
                x2(n).start()
                store_final(n).start()
            return [(lambda: mid(n).wait(), mid_in.at[n], own(n), close)]
        if step == 2:
            return [(lambda: zin(n).wait_recv(), z_in.at[n, side(1 - zh)], far(n), lambda: mid(n).start())]
        if step == 3:
            def close():
                rest_sum(n)
                x1(n).start()
            return [
                (lambda: zin_b(n).wait_recv(), z_in.at[n, side(zh)], own(n), lambda: None),
                (lambda: mid(n).wait(), mid_in.at[n], own(n), close)]

        def close():
            swap(n).start()
            zout(n).start()
            store_final(n).start()
        return [(lambda: x1(n).wait(), x_in.at[n], own(n), close)]

    def serve(*tasks):
        at_inner(lambda: add_all([item for step, n in tasks for item in items_of(step, n)]))
        outer = [item for step, n in tasks if step == 2 and is_x(n) for item in items_of(step, n)]
        if outer:
            at_edge(lambda: add_all(outer))

    def s5(*ns):
        for n in ns:
            if is_x(n):
                @at_edge
                def _():
                    zin(n).wait_send()
                    zout(n).wait_recv()
                    x2(n, True).start()
            else:
                @at_inner
                def _():
                    swap(n).wait()
                    zout_b(n).start()

    def s6(*ns):
        for n in ns:
            if is_x(n):
                x2(n).wait()
            else:
                @at_edge
                def _():
                    zin(n).wait_send()
                    zin_b(n).wait_send()
                    zout(n).wait_recv()
                    zout_b(n).wait_recv()
                at_inner(lambda: zout_b(n).wait_send())

            @at_inner
            def _():
                zout(n).wait_send()
                store_final(n).wait()

    def produce(ns, make):
        def copies(n):
            slot = stage.at[x_list.index(n) % 2]
            return (pltpu.make_async_copy(slot.at[side(1 - xb)], x_out.at[n], store_sem.at[x_list.index(n) % 2]),
                    pltpu.make_async_copy(slot.at[side(xb)], own(n), keep_sem.at[x_list.index(n) % 2]))

        def launch(n):
            for copy in copies(n):
                copy.wait()
            x1(n).start()
        waiting = []
        for n in ns:
            if is_x(n):
                make(stage.at[x_list.index(n) % 2], n)
                for copy in copies(n):
                    copy.start()
            else:
                make(pz.at[z_list.index(n)], n)

                @at_edge
                def _():
                    zin(n).start()
                    zin_b(n).start()
            for m in waiting:
                launch(m)
            waiting = [n] if is_x(n) else []
        for m in waiting:
            launch(m)

    def both(ref, *rest):
        return jnp.concatenate([ref[(0, *rest)], ref[(1, *rest)]], axis=0)

    def fc_grads(ns):
        def make(to, n):
            j = n % 4
            cols = pl.ds(j * 256, 256)
            if n < 4:
                to[...] = dot(both(hid, slice(None), cols), both(dbr), TN)
            else:
                d = jnp.concatenate([both(dup, m) for m in range(4)], axis=1)
                to[...] = dot(both(sec, slice(None), cols), d, TN)
        produce(ns, make)

    def attention_grads(ns):
        def make(to, n):
            if n == 8:
                for slab in (0, 1):
                    to[slab * 128:(slab + 1) * 128, :] = dot(both(mix, slab), both(sec), TN)
            else:
                def piece(j, _):
                    cols = pl.ds(pl.multiple_of(j * 256, 256), 256)
                    to[:, cols] = dot(both(dbr, slice(None), cols), both(dup, n - 9), TN)
                    return 0
                lax.fori_loop(0, 4, piece, 0)
        produce(ns, make)

    def second_back(i):
        zero = jnp.zeros((8, width), F32)

        def body(t, sums):
            rows = rows_of(t, LN_TILE)
            attended = wide(att, i, rows) + proj_b[...]
            n, r = norm_rows(tok[i, rows, :].astype(F32) + vec(i, 0) * attended)
            dy = wide(dst, i, rows)
            dn = dy * (1.0 + vec(i, 3))
            dm = cot[i, rows, :].astype(F32) + r * (
                dn - jnp.mean(dn, axis=-1, keepdims=True) - n * jnp.mean(dn * n, axis=-1, keepdims=True))
            put_wide(dst, i, rows, dm)
            da = (dm * vec(i, 0)).astype(BF16)
            sec[i, rows, :] = da
            return (sums[0] + fold(dm * attended), sums[1] + fold(dy * n), sums[2] + fold(dy), sums[3] + fold(da.astype(F32)))
        sums = lax.fori_loop(0, n_ln, body, (zero, zero, zero, zero))
        for k, s in zip((0, 3, 5), sums[:3]):
            sm[i, k:k + 1, :] = jnp.sum(s, axis=0, keepdims=True)
        sm[2, 2:3, :] = sm[2, 2:3, :] + jnp.sum(sums[3], axis=0, keepdims=True)

        def mixed(t, _):
            rows = rows_of(t, mt)
            d = dot(sec[i, rows, :], projw[...], NT)
            dmx[0, rows, :] = d[:, :128].astype(BF16)
            dmx[1, rows, :] = d[:, 128:].astype(BF16)
            return 0
        lax.fori_loop(0, 2, mixed, 0)

    def attend_back(i, slab):
        blocks = blocks_of(128)
        fill_kv(i, slab)
        acc[...] = jnp.zeros_like(acc)

        def body(rows, keys):
            p = exps(i, slab, rows, keys)
            d = dmx[slab, rows, :]
            q = qkn[i, 0, slab, rows, :]
            ds = []
            dp_both = dot(d, kv[1, :, 0:keys, :].reshape(2 * keys, 128), NT)
            for h in (0, 1):
                dpr = dp_both[:, h * keys:(h + 1) * keys]
                ds.append((p[h] * (dpr - jnp.sum(dpr * p[h], axis=-1, keepdims=True))).astype(BF16))
            acc[0, rows, :] = dot(jnp.concatenate(ds, axis=1), kv[0, :, 0:keys, :].reshape(2 * keys, 128))
            kr = pl.ds(0, keys)
            acc[1, kr, :] += dot(
                jnp.concatenate(ds, axis=0), jnp.concatenate([q * one_head(h) for h in (0, 1)], axis=0), TN)
            acc[2, kr, :] += dot(
                jnp.concatenate([v.astype(BF16) for v in p], axis=0),
                jnp.concatenate([d * one_head(h) for h in (0, 1)], axis=0), TN)
        each_tile(body)
        es = es_row[:, slab * 128:(slab + 1) * 128]

        def close(t, sums):
            rows = rows_of(t, LN_TILE)

            def unit(c, g):
                at = c * 256 + slab * 128
                pre = qk[i, rows, at:at + 128]
                r = lax.rsqrt(head_sum(pre * pre, blocks) + EPSILON)
                u = pre * r
                gu = g * u
                return r * (g - u * head_sum(gu, blocks)), gu
            dq, gu = unit(0, acc[0, rows, :] * es)
            dk, _g = unit(1, acc[1, rows, :])
            dq, dk, dv = dq.astype(BF16), dk.astype(BF16), acc[2, rows, :].astype(BF16)
            to = pl.ds(slab * 128, 128)
            dup[i, 0, rows, to] = dq
            dup[i, 1, rows, to] = dk
            dup[i, 2, rows, to] = dv
            return sums[0] + fold(dq.astype(F32)), sums[1] + fold(dv.astype(F32)), sums[2] + fold(gu)
        zero = jnp.zeros((8, 128), F32)
        sums = lax.fori_loop(0, n_ln, close, (zero, zero, zero))
        for k in range(3):
            lanes[k, slab] = lanes[k, slab] + sums[k]

    def first_grad(i):
        def body(t, _):
            rows = rows_of(t, mt)
            for h in (0, 1):
                total = None
                for c in range(3):
                    o = dot(dup[i, c, rows, :], qkvw[c, h * half:(h + 1) * half, :], NT)
                    total = o if total is None else total + o
                att[i, h, rows, :] = total
            return 0
        lax.fori_loop(0, 2, body, 0)

    def first_back(i):
        zero = jnp.zeros((8, width), F32)

        def body(t, sums):
            rows = rows_of(t, LN_TILE)
            n, r = norm_rows(tok[i, rows, :].astype(F32))
            dy = wide(att, i, rows)
            dn = dy * (1.0 + vec(i, 2))
            g = wide(dst, i, rows) + r * (
                dn - jnp.mean(dn, axis=-1, keepdims=True) - n * jnp.mean(dn * n, axis=-1, keepdims=True))
            dbr[i, rows, :] = g.astype(BF16)
            return sums[0] + fold(dy * n), sums[1] + fold(dy)
        sums = lax.fori_loop(0, n_ln, body, (zero, zero))
        for k, s in zip((2, 4), sums):
            sm[i, k:k + 1, :] = jnp.sum(s, axis=0, keepdims=True)
        pltpu.make_async_copy(dbr.at[i], tg_hbm.at[i], out_sem.at[i]).start()

    def branch(i):
        def body(t, _):
            rows = rows_of(t, mt)
            for h in (0, 1):
                dst[i, h, rows, :] = dot(hid[i, rows, :], fc2w[:, h * half:(h + 1) * half])
            return 0
        lax.fori_loop(0, 2, body, 0)

        def sums_of(t, sums):
            rows = rows_of(t, LN_TILE)
            g = cot[i, rows, :].astype(F32)
            return sums[0] + fold(g * wide(dst, i, rows)), sums[1] + fold(g)
        zero = jnp.zeros((8, width), F32)
        sums = lax.fori_loop(0, n_ln, sums_of, (zero, zero))
        g2r[me, i:i + 1, :] = jnp.sum(sums[0], axis=0, keepdims=True)
        sm[i, 1:2, :] = fc2_b[...] * jnp.sum(sums[1], axis=0, keepdims=True)

    def block_end(i):
        def body(t, _):
            rows = rows_of(t, LN_TILE)
            middle = tok[i, rows, :].astype(F32) + vec(i, 0) * (wide(att, i, rows) + proj_b[...])
            cot[i, rows, :] = (middle + vec(i, 1) * (wide(dst, i, rows) + fc2_b[...])).astype(BF16)
            return 0
        lax.fori_loop(0, n_ln, body, 0)
        pltpu.make_async_copy(cot.at[i], out_hbm.at[i], out_sem.at[2 + i]).start()

    def every_copy(to, source):
        return pltpu.make_async_remote_copy(
            src_ref=sm, dst_ref=every.at[source], send_sem=ev_s.at[to], recv_sem=ev_r.at[source],
            device_id={"dp": to}, device_id_type=MESH)

    def every_start():
        pltpu.make_async_copy(sm, every.at[dp], out_sem.at[4]).start()

        def body(step, _):
            every_copy(lax.rem(dp + step, n_dp), dp).start()
            return 0
        lax.fori_loop(1, n_dp, body, 0)

    def every_finish():
        pltpu.make_async_copy(sm, every.at[dp], out_sem.at[4]).wait()

        def body(step, _):
            every_copy(lax.rem(dp + step, n_dp), dp).wait_send()
            source = lax.rem(dp + n_dp - step, n_dp)
            every_copy(source, source).wait_recv()
            return 0
        lax.fori_loop(1, n_dp, body, 0)

    def rs_both(buf, i, k):
        rs_copy(buf, i, k).start()
        rs_finish(buf, i, k)

    def forward(i):
        first_norm(i)
        if i == 0:
            loads["qkvw"].wait()
        project(i)
        attend(i)
        if i == 0:
            loads["projw"].wait()
        attend_out(i)

    def close_sums():
        sent = share(g2r, g2_s, g2_r)
        for copy in sent:
            copy.wait()
        total = (g2r[0] + g2r[1]) + (g2r[2] + g2r[3])
        for i in (0, 1):
            sm[i, 1:2, :] = sm[i, 1:2, :] + total[i:i + 1, :]
        for j in range(4):
            sm[2, 1:2, j * 256:(j + 1) * 256] = jnp.sum(fb1[j], axis=0, keepdims=True)
        for k in range(3):
            for slab in (0, 1):
                at = k * 256 + slab * 128
                sm[2, 3:4, at:at + 128] = jnp.sum(lanes[k, slab], axis=0, keepdims=True)
        every_start()

    def spill_out(i):
        return pltpu.make_async_copy(att.at[i], spill.at[i], spill_sem.at[i])

    def spill_back(i):
        return pltpu.make_async_copy(spill.at[i], att.at[i], spill_sem.at[2 + i])

    def ag(buf, i, k):
        ag_copy(buf, i, k).start()
        ag_copy(buf, i, k).wait()

    sm[...] = jnp.zeros_like(sm)
    fb1[...] = jnp.zeros_like(fb1)
    lanes[...] = jnp.zeros_like(lanes)
    g2r[...] = jnp.zeros_like(g2r)
    kv[...] = jnp.zeros_like(kv)
    for i in (0, 1):
        sm[i, 6:7, :] = jnp.zeros((1, width), F32) + labels[i].astype(F32)
    loads["tok"].wait()
    forward(0)
    rs_both(att, 0, ATT)
    y_start(att, 0, ATT)
    forward(1)
    rs_both(att, 1, ATT)
    y_start(att, 1, ATT)
    for name in ("cot", "fc1w", "fc2w"):
        loads[name].wait()
    y_finish(att, 0, ATT)
    ag(att, 0, ATT)
    mlp(0)
    rs_both(dst, 0, DS)
    y_start(dst, 0, DS)
    y_finish(att, 1, ATT)
    ag(att, 1, ATT)
    mlp(1)
    rs_copy(dst, 1, DS).start()
    fc_grads((7, 0, 6,))
    rs_finish(dst, 1, DS)
    y_start(dst, 1, DS)
    fc_grads((1, 2, 3, 4, 5,))
    y_finish(dst, 0, DS)
    serve((2, 7))
    ag(dst, 0, DS)
    second_back(0)
    spill_out(0).start()
    serve((2, 0))
    attend_back(0, 0)
    attend_back(0, 1)
    serve((3, 7), (2, 6))
    spill_out(0).wait()
    first_grad(0)
    rs_both(att, 0, DF)
    y_start(att, 0, DF)
    serve((2, 1))
    y_finish(dst, 1, DS)
    ag(dst, 1, DS)
    serve((3, 0))
    serve((3, 6))
    second_back(1)
    spill_out(1).start()
    serve((2, 2))
    serve((3, 1))
    serve((4, 0))
    attend_back(1, 0)
    serve((2, 5))
    serve((4, 7))
    attend_back(1, 1)
    serve((3, 2), (4, 1))
    serve((4, 6), (2, 3), (3, 5))
    spill_out(1).wait()
    first_grad(1)
    rs_both(att, 1, DF)
    y_start(att, 1, DF)
    first_norm(0)
    first_norm(1)
    attention_grads((8,))
    serve((3, 3))
    attention_grads((11,))
    serve((4, 2))
    attention_grads((9,))
    s5(0)
    attention_grads((10,))
    y_finish(att, 0, DF)
    ag(att, 0, DF)
    first_back(0)
    spill_back(0).start()
    s5(7)
    branch(0)
    rs_both(dst, 0, BR)
    y_start(dst, 0, BR)
    serve((2, 4), (2, 8))
    s5(2)
    serve((4, 5))
    y_finish(att, 1, DF)
    ag(att, 1, DF)
    s5(6)
    serve((4, 3), (3, 4))
    first_back(1)
    spill_back(1).start()
    serve((2, 11))
    branch(1)
    rs_both(dst, 1, BR)
    serve((2, 9))
    serve((2, 10))
    s5(5)
    serve((3, 8))
    y_start(dst, 1, BR)
    serve((4, 4))
    serve((3, 11))
    s5(1)
    serve((3, 9))
    s5(3)
    serve((3, 10))
    s5(4)
    serve((4, 8))
    close_sums()
    s5(8)
    serve((4, 9))
    y_finish(dst, 0, BR)
    ag(dst, 0, BR)
    s5(9)
    serve((4, 10))
    s5(10)
    spill_back(0).wait()
    block_end(0)
    serve((4, 11))
    y_finish(dst, 1, BR)
    s5(11)
    ag(dst, 1, BR)
    spill_back(1).wait()
    block_end(1)
    every_finish()
    s6(0, 7, 2, 6, 5, 1, 3, 4, 8, 9, 10, 11)
    for i in (0, 1):
        pltpu.make_async_copy(dbr.at[i], tg_hbm.at[i], out_sem.at[i]).wait()
        pltpu.make_async_copy(cot.at[i], out_hbm.at[i], out_sem.at[2 + i]).wait()


def run_block(n_dp, mod_part, ada_b, tok, cot, stops, labels, qkvw, projw, fc1w, fc2w, qv_b, es_row, proj_b, fc1_b, fc2_b, slots):
    items, padded, width = tok.shape
    half = width // 2
    hidden = fc1w.shape[1]
    n_chunks = 12
    n_rest = max(1, (n_dp // 8).bit_length() - 1)
    hbm = pl.BlockSpec(memory_space=pl.ANY)
    vmem = pl.BlockSpec(memory_space=pltpu.VMEM)
    smem = pl.BlockSpec(memory_space=pltpu.SMEM)
    wide_b = (items, padded, width)
    wide_f = (items, 2, padded, half)
    dma = pltpu.SemaphoreType.DMA
    return pl.pallas_call(
        functools.partial(block_kernel, slots, n_dp),
        out_shape=(
            jax.ShapeDtypeStruct(wide_b, BF16), jax.ShapeDtypeStruct(wide_b, BF16),
            jax.ShapeDtypeStruct((n_chunks, 256, width), F32), jax.ShapeDtypeStruct((n_dp, 3, 8, width), F32),
            jax.ShapeDtypeStruct((n_chunks, 128, width), F32), jax.ShapeDtypeStruct((n_chunks, 128, width), F32),
            jax.ShapeDtypeStruct((n_chunks, 256, width), F32), jax.ShapeDtypeStruct((n_chunks, 128, width), F32),
            jax.ShapeDtypeStruct((n_rest, n_chunks, 128, width), F32), jax.ShapeDtypeStruct(wide_f, F32),
        ),
        in_specs=[vmem, vmem, hbm, hbm, smem, smem, hbm, hbm, hbm, hbm, vmem, vmem, vmem, vmem, vmem],
        out_specs=(hbm,) * 10,
        scratch_shapes=[
            *[pltpu.VMEM(wide_b, BF16) for _ in range(4)],
            pltpu.VMEM((items, padded, hidden), BF16), pltpu.VMEM((items, hidden // 256, padded, 256), BF16),
            *[pltpu.VMEM(wide_f, F32) for _ in range(2)],
            pltpu.VMEM((items, padded, half), F32),
            pltpu.VMEM((items, 3, 2, padded, 128), BF16),
            pltpu.VMEM((items, 2, padded, 128), BF16),
            pltpu.VMEM((2, padded, 128), BF16),
            pltpu.VMEM((2, 2, 768, 128), BF16),
            pltpu.VMEM((3, 768, 128), F32),
            pltpu.VMEM((items, slots, half), F32),
            pltpu.VMEM((items, slots, half), F32),
            pltpu.VMEM(qkvw.shape, BF16), pltpu.VMEM(projw.shape, BF16),
            pltpu.VMEM(fc1w.shape, BF16), pltpu.VMEM(fc2w.shape, BF16),
            pltpu.VMEM((len(X_CHUNKS), 128, width), F32), pltpu.VMEM((n_chunks - len(X_CHUNKS), 256, width), F32),
            pltpu.VMEM((2, 256, width), F32), pltpu.VMEM((128 if n_dp > 8 else 8, width), F32),
            pltpu.VMEM((4, items, 8, width), F32), pltpu.VMEM((items, 8, width), F32),
            pltpu.VMEM((4, 8, width), F32),
            pltpu.VMEM((4, 8, 256), F32), pltpu.VMEM((3, 2, 8, 128), F32), pltpu.VMEM((3, 8, width), F32),
            dma((6,)), dma((5,)), dma((5,)), dma((2,)), dma((2,)), dma((n_chunks,)), dma((4,)), pltpu.SemaphoreType.REGULAR((2,)),
            dma((3,)), dma((3,)), dma((3,)), dma((3,)),
            *[dma((8,)) for _ in range(6)],
            *[dma((n_chunks,)) for _ in range(14)],
            dma((n_rest, n_chunks)), dma((n_rest, n_chunks)), dma((n_dp,)), dma((n_dp,)),
        ],
        compiler_params=pltpu.CompilerParams(
            collective_id=0, has_side_effects=True, vmem_limit_bytes=62 * 2**20),
        name="block",
    )(mod_part, ada_b, tok, cot, stops, labels, qkvw, projw, fc1w, fc2w, qv_b, es_row, proj_b, fc1_b, fc2_b)


def shards(
    n_dp, tokens, cotangent, stop_scales, labels, class_table, ada_weight, ada_bias, qkv_weight, qv_bias, log_scale,
    proj_weight, proj_bias, fc1_weight, fc1_bias, fc2_weight, fc2_bias,
):
    items, slots, width = tokens.shape
    padded = -(-slots // LN_TILE) * LN_TILE
    classes = class_table.shape[0]
    class_local = jnp.concatenate(
        [lax.dynamic_slice_in_dim(class_table, labels[i], 1, 0) for i in range(items)], axis=0).astype(F32)
    lifted = jax.nn.silu(class_local).astype(BF16)
    part = jnp.dot(lifted, ada_weight, preferred_element_type=F32).reshape(items, 6, width)
    part = jnp.pad(part, ((0, 0), (0, 2), (0, 0)))
    ada_rows = jnp.pad(ada_bias.reshape(1, 6, width), ((0, 0), (0, 2), (0, 0)))
    tok = jnp.pad(tokens, ((0, 0), (0, padded - slots), (0, 0)))
    cot = jnp.pad(cotangent, ((0, 0), (0, padded - slots), (0, 0)))
    heads = log_scale.shape[0]
    es_row = jnp.repeat(jnp.exp(log_scale), qkv_weight.shape[2] // heads)[None, :]
    out, tg, grads, every, *_ = run_block(
        n_dp, part, ada_rows, tok, cot, stop_scales, labels, jnp.transpose(qkv_weight, (1, 0, 2)), proj_weight, fc1_weight, fc2_weight,
        qv_bias, es_row, proj_bias[None, :], fc1_bias.reshape(-1, 1, 256), fc2_bias[None, :], slots)

    small = jnp.sum(every[:, 2], axis=0)
    every = every[:, :2].reshape(-1, 8, width)
    every_label = every[:, 6, 0]
    class_hot = every_label[:, None] == jnp.arange(classes, dtype=F32)[None, :]
    dmod = every[:, :6].reshape(-1, 6 * width)
    dmod = jnp.where(every_label[:, None] >= 0, dmod, 0.0).astype(BF16)
    every_class = jnp.dot(class_hot.astype(BF16), class_table, preferred_element_type=F32)
    every_lift = jax.nn.silu(every_class).astype(BF16)
    lifted_grad = jnp.einsum("ik,dk->id", dmod, ada_weight, preferred_element_type=F32)
    class_grad = jax.vjp(jax.nn.silu, every_class)[1](lifted_grad)[0]
    table_grad = jnp.einsum("ic,id->cd", class_hot.astype(F32), class_grad, precision=lax.Precision.HIGHEST)
    ada_weight_grad = jnp.einsum("id,ik->dk", every_lift, dmod, preferred_element_type=F32)
    ada_bias_grad = jnp.sum(dmod.astype(F32), axis=0)
    g2 = grads[0:4].reshape(-1, width)
    g1 = grads[4:8].reshape(-1, width)
    gp = grads[8]
    gq = jnp.transpose(grads[9:12].reshape(3, 256, 4, 256), (2, 1, 0, 3)).reshape(width, 3, 256)
    lanes = small[3]
    return (
        out[:, :slots], tg[:, :slots], table_grad, ada_weight_grad, ada_bias_grad,
        gq, lanes[:512].reshape(2, 256), lanes[512:768].reshape(heads, -1).sum(axis=1),
        gp, small[2], g1, small[1], g2, small[0],
    )


def solution(mesh):
    return jax.shard_map(
        functools.partial(shards, mesh.shape["dp"]),
        mesh=mesh,
        in_specs=(
            P("dp", None, None), P("dp", None, None), P("dp"), P("dp"), P(None, "mp"), P("mp", None), P(),
            P(None, None, "mp"), P(None, "mp"), P("mp"), P("mp", None), P(), P(None, "mp"), P("mp"), P("mp", None), P(),
        ),
        out_specs=(
            P("dp", None, None), P("dp", None, None), P(None, "mp"), P("mp", None), P(), P(None, None, "mp"), P(None, "mp"),
            P("mp"), P("mp", None), P(), P(None, "mp"), P("mp"), P("mp", None), P(),
        ),
        check_vma=False,
    )
```

```python
import functools

import jax
import jax.numpy as jnp
import numpy as np
from jax import lax
from jax.experimental import pallas as pl
from jax.experimental.pallas import tpu as pltpu
from jax.sharding import PartitionSpec as P

SIDE_LIST = (1, 2, 3, 4, 5, 6, 8, 10, 13, 16)
EPSILON = 1e-06
MESH = pl.DeviceIdType.MESH
F32, BF16 = jnp.float32, jnp.bfloat16
GELU_C = 0.7978845608028654
GELU_A = 0.044715
LN_TILE = 64
NT = (((1,), (1,)), ((), ()))
TN = (((0,), (0,)), ((), ()))
NN = (((1,), (0,)), ((), ()))
ATT, DS, DF, BR = 0, 2, 4, 6
ROUTES = "CBCACACZABAA"


def dot(a, b, dims=NN):
    return lax.dot_general(a, b, dims, preferred_element_type=F32)


def norm_rows(v):
    center = v - jnp.mean(v, axis=-1, keepdims=True)
    scale = lax.rsqrt(jnp.mean(center * center, axis=-1, keepdims=True) + EPSILON)
    return center * scale, scale


def fold(v):
    return jnp.sum(v.reshape(v.shape[0] // 8, 8, v.shape[1]), axis=0)


def head_sum(v, blocks):
    high = v.astype(BF16)
    rest = (v - high.astype(F32)).astype(BF16)
    return dot(high, blocks) + dot(rest, blocks)


def block_kernel(
    slots, n_dp,
    lifted, ada_b, ada_hbm, tok_hbm, cot_hbm, stops, labels, log_scale,
    qkvw_hbm, projw_hbm, fc1w_hbm, fc2w_hbm,
    qv_b, proj_b, fc1_b, fc2_b,
    out_hbm, tg_hbm, g1_out, g2_out, gp_out, gq_out, every, x_out, x_in, z_in, mid_in, rest_in, spill,
    tok, cot, sec, dbr, hid, dup,
    att, dst,
    qk, qkn, mix, dmx, kv, acc,
    rs_buf, y_buf,
    qkvw, projw, fc1w, fc2w,
    raw, es_row, px, pz, stage, extra, modr, mod, g2r, fb1, lanes, sm,
    in_sem, raw_sem, out_sem, load_sem, store_sem, keep_sem, final_sem, spill_sem, y_free,
    mod_s, mod_r, g2_s, g2_r, rs_s, rs_r, y_s, y_r, ag_s, ag_r,
    x1_s, x1_r, zi_s, zi_r, mi_s, mi_r, zb_s, zb_r, zo_s, zo_r, x2_s, x2_r, zc_s, zc_r, re_s, re_r, ev_s, ev_r,
):
    items, padded, width = tok.shape
    half = width // 2
    me = lax.axis_index("mp")
    dp = lax.axis_index("dp")
    xb = lax.rem(dp, 2)
    z = lax.rem(dp // 2, 4)
    zh = z // 2
    inner = jnp.logical_or(z == 1, z == 2)
    edge = jnp.logical_or(z == 0, z == 3)
    x_mate = dp + 1 - 2 * xb
    z_mate = dp + 2 - 4 * lax.rem(z, 2)
    mid_mate = jnp.where(z == 1, dp + 2, jnp.where(z == 2, dp - 2, dp))
    n_rest = rest_in.shape[0] if n_dp > 8 else 0
    rest_mates = [dp + (8 << k) * (1 - 2 * lax.rem(dp // (8 << k), 2)) for k in range(n_rest)]
    core = lax.rem(me, 2)
    core_mate = me + 1 - 2 * core
    y_mate = lax.rem(me + 2, 4)
    n_ln = padded // LN_TILE
    mt = padded // 2

    def rows_of(t, n):
        return pl.ds(pl.multiple_of(t * n, n), n)

    def raw_copy(src, i):
        return pltpu.make_async_copy(src.at[i], raw, raw_sem)

    def unpack(src, i, to, then=None):
        raw_copy(src, i).wait()
        whole = slots // 16 * 16

        def body(t, _):
            rows = rows_of(t, 16)
            to[i, rows, :] = raw[rows, :]
            return 0
        lax.fori_loop(0, slots // 16, body, 0)
        tail = raw[whole:slots, :].astype(F32)
        rest = jnp.concatenate([tail, jnp.zeros((padded - slots, width), F32)], axis=0)
        to[i, whole:padded, :] = rest.astype(BF16)
        if then is not None:
            raw_copy(*then).start()

    raw_copy(tok_hbm, 0).start()
    rows_ada = ada_hbm.shape[0]
    ada_room = [buf.at[i, pl.ds(k * rows_ada, rows_ada)] for buf, i, k in (
        (hid, 0, 0), (hid, 0, 1), (hid, 1, 0), (hid, 1, 1), (sec, 0, 0), (sec, 1, 0))]
    loads = {}
    for k, (name, src, to) in enumerate((
        *[(f"ada{c}", ada_hbm.at[:, pl.ds(c * width, width)], ada_room[c]) for c in range(6)],
        ("qkvw", qkvw_hbm, qkvw), ("projw", projw_hbm, projw), ("fc1w", fc1w_hbm, fc1w), ("fc2w", fc2w_hbm, fc2w),
    )):
        loads[name] = pltpu.make_async_copy(src, to, in_sem.at[k])
        loads[name].start()

    barrier = pltpu.get_barrier_semaphore()
    for step in (1, 2, 3):
        pl.semaphore_signal(barrier, inc=1, device_id={"mp": lax.rem(me + step, 4)}, device_id_type=MESH)
    def greet(step, _):
        pl.semaphore_signal(barrier, inc=1, device_id={"dp": lax.rem(dp + step, n_dp)}, device_id_type=MESH)
        return 0
    lax.fori_loop(1, n_dp, greet, 0)
    pl.semaphore_wait(barrier, 3 + n_dp - 1)

    def share(buf, send, recv):
        copies = []
        for step in (1, 2, 3):
            copies.append(pltpu.make_async_remote_copy(
                src_ref=buf.at[me], dst_ref=buf.at[me], send_sem=send.at[step - 1], recv_sem=recv.at[step - 1],
                device_id={"mp": lax.rem(me + step, 4)}, device_id_type=MESH))
        for copy in copies:
            copy.start()
        return copies

    for c in range(6):
        loads[f"ada{c}"].wait()
        part = dot(lifted[...], ada_room[c][...])
        for i in range(items):
            modr[me, i, c:c + 1, :] = part[i:i + 1, :]
    for i in range(items):
        modr[me, i, 6:8, :] = jnp.zeros((2, width), F32)
    sent = share(modr, mod_s, mod_r)
    unpack(tok_hbm, 0, tok, (tok_hbm, 1))
    for copy in sent:
        copy.wait()
    mod[...] = (modr[0] + modr[1]) + (modr[2] + modr[3])
    for i in range(items):
        mod[i, 0:6, :] = mod[i, 0:6, :] + ada_b[...]
    lane = lax.broadcasted_iota(jnp.int32, es_row.shape, 1) // 64
    scales = jnp.zeros(es_row.shape, F32)
    for h in range(es_row.shape[1] // 64):
        scales = jnp.where(lane == h, log_scale[h], scales)
    es_row[...] = jnp.exp(scales)

    def vec(i, k):
        return mod[i, k:k + 1, :]

    def rs_copy(buf, i, k):
        return pltpu.make_async_remote_copy(
            src_ref=buf.at[i, 1 - core, pl.ds(0, slots)], dst_ref=rs_buf.at[i], send_sem=rs_s.at[k + i], recv_sem=rs_r.at[k + i],
            device_id={"mp": core_mate}, device_id_type=MESH)

    def y_copy(buf, i, k):
        dst = qk.at[i, pl.ds(0, slots)] if k == BR else y_buf.at[i]
        return pltpu.make_async_remote_copy(
            src_ref=buf.at[i, core, pl.ds(0, slots)], dst_ref=dst, send_sem=y_s.at[k + i], recv_sem=y_r.at[k + i],
            device_id={"mp": y_mate}, device_id_type=MESH)

    def ag_copy(buf, i, k):
        return pltpu.make_async_remote_copy(
            src_ref=buf.at[i, core, pl.ds(0, slots)], dst_ref=buf.at[i, core, pl.ds(0, slots)],
            send_sem=ag_s.at[k + i], recv_sem=ag_r.at[k + i],
            device_id={"mp": core_mate}, device_id_type=MESH)

    add_rows = slots // 5

    def rs_finish(buf, i, k):
        rs_copy(buf, i, k).wait()

        def add(t, _):
            rows = rows_of(t, add_rows)
            buf[i, core, rows, :] = buf[i, core, rows, :] + rs_buf[i, rows, :]
            return 0
        lax.fori_loop(0, 5, add, 0)

    def y_finish(buf, i, k):
        y_copy(buf, i, k).wait()

        def add(t, _):
            rows = rows_of(t, add_rows)
            other = qk[i, rows, :] if k == BR else y_buf[i, rows, :]
            buf[i, core, rows, :] = buf[i, core, rows, :] + other
            return 0
        lax.fori_loop(0, 5, add, 0)
        if k in (ATT, DS):
            pl.semaphore_signal(y_free.at[i], inc=1, device_id={"mp": y_mate}, device_id_type=MESH)

    def y_start(buf, i, k):
        if k in (DS, DF):
            pl.semaphore_wait(y_free.at[i], 1)
        y_copy(buf, i, k).start()

    def wide(buf, i, rows):
        return jnp.concatenate([buf[i, 0, rows, :], buf[i, 1, rows, :]], axis=1)

    def put_wide(buf, i, rows, v):
        buf[i, 0, rows, :] = v[:, :half]
        buf[i, 1, rows, :] = v[:, half:]

    def blocks_of(n):
        a = lax.broadcasted_iota(jnp.int32, (n, n), 0) // 64
        b = lax.broadcasted_iota(jnp.int32, (n, n), 1) // 64
        return jnp.where(a == b, 1.0, 0.0).astype(BF16)

    ends = np.cumsum(np.array([s * s for s in SIDE_LIST]))
    tiles = ((0, 240, 1, 256), (240, 176, 1, 512), (416, 96, 3, 768))

    def keep_of(i, rows, keys):
        live = jnp.int32(0)
        for s in range(len(SIDE_LIST)):
            live = jnp.where(stops[i] == s + 1, int(ends[s]), live)
        n = rows.size
        at = rows.start + lax.broadcasted_iota(jnp.int32, (n, 1), 0)
        bound = jnp.full((n, 1), int(ends[0]), jnp.int32)
        for s in range(1, len(SIDE_LIST)):
            bound = jnp.where(at >= int(ends[s - 1]), int(ends[s]), bound)
        bound = jnp.minimum(bound, live)
        return lax.broadcasted_iota(jnp.int32, (n, keys), 1) < bound

    def one_head(h):
        lane = lax.broadcasted_iota(jnp.int32, (1, 128), 1) // 64
        return jnp.where(lane == h, 1.0, 0.0).astype(BF16)

    def fill_kv(i, slab):
        for c in (0, 1):
            for h in (0, 1):
                kv[c, h, 0:padded, :] = qkn[i, 1 + c, slab] * one_head(h)

    def exps(i, slab, rows, keys):
        keep = keep_of(i, rows, keys)
        s = dot(qkn[i, 0, slab, rows, :], kv[0, :, 0:keys, :].reshape(2 * keys, 128), NT)
        parts = []
        for h in (0, 1):
            e = jnp.where(keep, jnp.exp(s[:, h * keys:(h + 1) * keys]), 0.0)
            parts.append(e * (1.0 / jnp.sum(e, axis=-1, keepdims=True)))
        return parts

    def each_tile(body):
        for first_row, n, steps, keys in tiles:
            if steps == 1:
                body(pl.ds(first_row, n), keys)
            else:
                def step(t, _, first_row=first_row, n=n, keys=keys):
                    body(pl.ds(pl.multiple_of(first_row + t * n, 16), n), keys)
                    return 0
                lax.fori_loop(0, steps, step, 0)

    def first_norm(i):
        def body(t, _):
            rows = rows_of(t, LN_TILE)
            n, _r = norm_rows(tok[i, rows, :].astype(F32))
            dbr[i, rows, :] = (n * (1.0 + vec(i, 2)) + vec(i, 4)).astype(BF16)
            return 0
        lax.fori_loop(0, n_ln, body, 0)

    def project(i):
        blocks = blocks_of(256)

        def body(t, _):
            rows = rows_of(t, mt)
            f = dbr[i, rows, :]
            q = dot(f, qkvw[0]) + qv_b[0:1, :]
            qk[i, rows, 0:256] = q
            u = q * lax.rsqrt(head_sum(q * q, blocks) + EPSILON) * es_row[...]
            qkn[i, 0, 0, rows, :] = u[:, :128].astype(BF16)
            qkn[i, 0, 1, rows, :] = u[:, 128:].astype(BF16)
            k = dot(f, qkvw[1])
            qk[i, rows, 256:512] = k
            u = k * lax.rsqrt(head_sum(k * k, blocks) + EPSILON)
            qkn[i, 1, 0, rows, :] = u[:, :128].astype(BF16)
            qkn[i, 1, 1, rows, :] = u[:, 128:].astype(BF16)
            v = dot(f, qkvw[2]) + qv_b[1:2, :]
            qkn[i, 2, 0, rows, :] = v[:, :128].astype(BF16)
            qkn[i, 2, 1, rows, :] = v[:, 128:].astype(BF16)
            return 0
        lax.fori_loop(0, 2, body, 0)

    def attend(i):
        def slab_body(slab, _):
            fill_kv(i, slab)

            def body(rows, keys):
                p = jnp.concatenate([v.astype(BF16) for v in exps(i, slab, rows, keys)], axis=1)
                o = dot(p, kv[1, :, 0:keys, :].reshape(2 * keys, 128))
                mix[i, slab, rows, :] = o.astype(BF16)
            each_tile(body)
            return 0
        lax.fori_loop(0, 2, slab_body, 0)

    def attend_out(i):
        def body(t, _):
            rows = rows_of(t, mt)
            m = jnp.concatenate([mix[i, 0, rows, :], mix[i, 1, rows, :]], axis=1)
            for h in (0, 1):
                att[i, h, rows, :] = dot(m, projw[:, h * half:(h + 1) * half])
            return 0
        lax.fori_loop(0, 2, body, 0)

    def mlp(i):
        def body(t, total):
            rows = rows_of(t, LN_TILE)
            middle = tok[i, rows, :].astype(F32) + vec(i, 0) * (wide(att, i, rows) + proj_b[...])
            n, _r = norm_rows(middle)
            sec[i, rows, :] = (n * (1.0 + vec(i, 3)) + vec(i, 5)).astype(BF16)
            d = (cot[i, rows, :].astype(F32) * vec(i, 1)).astype(BF16)
            dbr[i, rows, :] = d
            return total + fold(d.astype(F32))
        total = lax.fori_loop(0, n_ln, body, jnp.zeros((8, width), F32))
        sm[2, 0:1, :] = sm[2, 0:1, :] + jnp.sum(total, axis=0, keepdims=True)

        def column(j, _):
            cols = pl.ds(pl.multiple_of(j * 256, 256), 256)

            def body(t, _):
                rows = rows_of(t, mt)
                u = dot(sec[i, rows, :], fc1w[:, cols]) + fc1_b[j]
                dh = dot(dbr[i, rows, :], fc2w[cols, :], NT)
                th = jnp.tanh(GELU_C * (u + GELU_A * u * u * u))
                hid[i, rows, cols] = (0.5 * u * (1.0 + th)).astype(BF16)
                slope = 0.5 * (1.0 + th) + 0.5 * u * (1.0 - th * th) * (GELU_C + (3.0 * GELU_C * GELU_A) * u * u)
                d = (dh * slope).astype(BF16)
                dup[i, j, rows, :] = d
                fb1[j] = fb1[j] + fold(d.astype(F32))
                return 0
            lax.fori_loop(0, 2, body, 0)
            return 0
        lax.fori_loop(0, dup.shape[1], column, 0)

        def back(t, _):
            rows = rows_of(t, mt)
            d = jnp.concatenate([dup[i, j, rows, :] for j in range(dup.shape[1])], axis=1)
            for h in (0, 1):
                dst[i, h, rows, :] = dot(d, fc1w[h * half:(h + 1) * half, :], NT)
            return 0
        lax.fori_loop(0, 2, back, 0)

    x_list = [n for n in range(12) if ROUTES[n] != "Z"]
    z_list = [n for n in range(12) if ROUTES[n] == "Z"]

    def is_x(n):
        return ROUTES[n] != "Z"

    def side(h):
        return pl.ds(pl.multiple_of(h * 128, 128), 128)

    def own(n):
        return px.at[x_list.index(n)] if is_x(n) else pz.at[z_list.index(n), side(zh)]

    def final_of(n, h):
        if n < 8:
            return [(g2_out if n < 4 else g1_out).at[pl.ds(pl.multiple_of((n % 4) * 256 + h * 128, 128), 128)]]
        if n == 8:
            return [gp_out.at[side(h)]]
        return [gq_out.at[n - 9, pl.ds(pl.multiple_of(j * 256 + h * 128, 128), 128)] for j in range(4)]

    def in_pieces(n, ref):
        return [ref] if n < 9 else [ref.at[:, pl.ds(j * 256, 256)] for j in range(4)]

    def my_half(n):
        return xb if is_x(n) else zh

    class Pieces:
        def __init__(self, n, srcs, tos, send, recv, mate):
            self.parts = lambda: [
                to_dp(a, b, send.at[n, j], recv.at[n, j], mate) for j, (a, b) in enumerate(zip(srcs, tos))]

        def start(self):
            for part in self.parts():
                part.start()

        def wait_send(self):
            for part in self.parts():
                part.wait_send()

        def wait_recv(self):
            for part in self.parts():
                part.wait_recv()

        def wait(self):
            self.wait_send()
            self.wait_recv()

    def to_dp(src, to, send, recv, mate):
        return pltpu.make_async_remote_copy(
            src_ref=src, dst_ref=to, send_sem=send, recv_sem=recv, device_id={"dp": mate}, device_id_type=MESH)

    def x1(n):
        return to_dp(x_out.at[n] if is_x(n) else own(n), x_in.at[n], x1_s.at[n], x1_r.at[n], x_mate)

    def zin(n):
        if is_x(n):
            return to_dp(own(n), z_in.at[n, pl.ds(0, 128)], zi_s.at[n], zi_r.at[n], z_mate)
        return to_dp(far(n), z_in.at[n, side(1 - zh)], zi_s.at[n], zi_r.at[n], z_mate)

    def far(n):
        return pz.at[z_list.index(n), side(1 - zh)]

    def zin_b(n):
        return to_dp(own(n), z_in.at[n, side(zh)], zb_s.at[n], zb_r.at[n], z_mate)

    def mid(n):
        return to_dp(own(n) if is_x(n) else far(n), mid_in.at[n], mi_s.at[n], mi_r.at[n], mid_mate)

    def zout(n):
        return Pieces(n, in_pieces(n, own(n)), final_of(n, my_half(n)), zo_s, zo_r, z_mate)

    def zout_b(n):
        views = final_of(n, 1 - my_half(n))
        return Pieces(n, views, views, zc_s, zc_r, z_mate)

    def x2(n, at_the_edge=False):
        views = final_of(n, xb)
        return Pieces(n, views if at_the_edge else in_pieces(n, own(n)), views, x2_s, x2_r, x_mate)

    def swap(n):
        return Pieces(n, in_pieces(n, own(n)), final_of(n, zh), x2_s, x2_r, mid_mate)

    class store_final:
        def __init__(self, n):
            self.parts = lambda: [
                pltpu.make_async_copy(a, b, final_sem.at[n, j])
                for j, (a, b) in enumerate(zip(in_pieces(n, own(n)), final_of(n, my_half(n))))]

        def start(self):
            for part in self.parts():
                part.start()

        def wait(self):
            for part in self.parts():
                part.wait()

    def at_edge(body):
        pl.when(edge)(body)

    def at_inner(body):
        pl.when(inner)(body)

    def accumulate(to, what):
        def add(t, _):
            rows = rows_of(t, 16)
            to[rows, :] = to[rows, :] + what[rows, :]
            return 0
        lax.fori_loop(0, 8, add, 0)

    def add_all(items):
        def slot(k):
            return stage.at[(k // 2) % 2, pl.ds((k % 2) * 128, 128)]

        def load(k):
            return pltpu.make_async_copy(items[k][1], slot(k), load_sem.at[k % 4])

        def begin(k):
            items[k][0]()
            load(k).start()
        for k in range(min(2, len(items))):
            begin(k)
        for k in range(len(items)):
            load(k).wait()
            accumulate(items[k][2], slot(k))
            items[k][3]()
            if k + 2 < len(items):
                begin(k + 2)

    def rest_sum(n):
        for k in range(n_rest):
            copy = to_dp(own(n), rest_in.at[k, n], re_s.at[k, n], re_r.at[k, n], rest_mates[k])
            copy.start()
            copy.wait()
            load = pltpu.make_async_copy(rest_in.at[k, n], extra, load_sem.at[4])
            load.start()
            load.wait()
            accumulate(own(n), extra)

    def items_of(step, n):
        if is_x(n):
            if step == 2:
                return [(lambda: x1(n).wait(), x_in.at[n], own(n), lambda: at_edge(lambda: zin(n).start()))]
            if step == 3:
                return [(lambda: zin(n).wait_recv(), z_in.at[n, pl.ds(0, 128)], own(n), lambda: mid(n).start())]

            def close():
                rest_sum(n)
                zout(n).start()
                if ROUTES[n] != "C":
                    x2(n).start()
                store_final(n).start()
            return [(lambda: mid(n).wait(), mid_in.at[n], own(n), close)]
        if step == 2:
            return [(lambda: zin(n).wait_recv(), z_in.at[n, side(1 - zh)], far(n), lambda: mid(n).start())]
        if step == 3:
            def close():
                rest_sum(n)
                x1(n).start()
            return [
                (lambda: zin_b(n).wait_recv(), z_in.at[n, side(zh)], own(n), lambda: None),
                (lambda: mid(n).wait(), mid_in.at[n], own(n), close)]

        def close():
            swap(n).start()
            zout(n).start()
            store_final(n).start()
        return [(lambda: x1(n).wait(), x_in.at[n], own(n), close)]

    def serve(*tasks):
        at_inner(lambda: add_all([item for step, n in tasks for item in items_of(step, n)]))
        outer = [item for step, n in tasks if step == 2 and is_x(n) for item in items_of(step, n)]
        if outer:
            at_edge(lambda: add_all(outer))

    def s5(n):
        if ROUTES[n] == "Z":
            @at_inner
            def _():
                swap(n).wait()
                zout_b(n).start()
        elif ROUTES[n] == "B":
            @at_inner
            def _():
                x2(n).wait()
                zout_b(n).start()
        else:
            @at_edge
            def _():
                zin(n).wait_send()
                zout(n).wait_recv()
                x2(n, True).start()

    def s6(n):
        @at_edge
        def _():
            x2(n, True).wait()
            zout_b(n).start()

    def close_chunk(n):
        kind = ROUTES[n]

        @at_edge
        def _():
            if kind == "A":
                x2(n, True).wait()
            if kind in "BZ":
                zin(n).wait_send()
                if kind == "Z":
                    zin_b(n).wait_send()
                zout(n).wait_recv()
                zout_b(n).wait_recv()
            if kind == "C":
                zout_b(n).wait_send()

        @at_inner
        def _():
            if kind == "A":
                x2(n).wait()
            zout(n).wait_send()
            store_final(n).wait()
            if kind in "BZ":
                zout_b(n).wait_send()
            if kind == "C":
                zout_b(n).wait_recv()

    def produce(ns, make):
        turn = {n: k % 2 for k, n in enumerate(n for n in ns if is_x(n))}

        def copies(n):
            slot = stage.at[turn[n]]
            return (pltpu.make_async_copy(slot.at[side(1 - xb)], x_out.at[n], store_sem.at[turn[n]]),
                    pltpu.make_async_copy(slot.at[side(xb)], own(n), keep_sem.at[turn[n]]))

        def launch(n):
            for copy in copies(n):
                copy.wait()
            x1(n).start()
        waiting = []
        for n in ns:
            if is_x(n):
                make(stage.at[turn[n]], n)
                for copy in copies(n):
                    copy.start()
            else:
                make(pz.at[z_list.index(n)], n)

                @at_edge
                def _():
                    zin(n).start()
                    zin_b(n).start()
            for m in waiting:
                launch(m)
            waiting = [n] if is_x(n) else []
        for m in waiting:
            launch(m)

    def both(ref, *rest):
        return jnp.concatenate([ref[(0, *rest)], ref[(1, *rest)]], axis=0)

    def fc_grads(ns):
        def make(to, n):
            j = n % 4
            cols = pl.ds(j * 256, 256)
            if n < 4:
                to[...] = dot(both(hid, slice(None), cols), both(dbr), TN)
            else:
                d = jnp.concatenate([both(dup, m) for m in range(4)], axis=1)
                to[...] = dot(both(sec, slice(None), cols), d, TN)
        produce(ns, make)

    def attention_grads(ns):
        def make(to, n):
            if n == 8:
                for slab in (0, 1):
                    to[slab * 128:(slab + 1) * 128, :] = dot(both(mix, slab), both(sec), TN)
            else:
                def piece(j, _):
                    cols = pl.ds(pl.multiple_of(j * 256, 256), 256)
                    to[:, cols] = dot(both(dbr, slice(None), cols), both(dup, n - 9), TN)
                    return 0
                lax.fori_loop(0, 4, piece, 0)
        produce(ns, make)

    def second_back(i):
        zero = jnp.zeros((8, width), F32)

        def body(t, sums):
            rows = rows_of(t, LN_TILE)
            attended = wide(att, i, rows) + proj_b[...]
            n, r = norm_rows(tok[i, rows, :].astype(F32) + vec(i, 0) * attended)
            dy = wide(dst, i, rows)
            dn = dy * (1.0 + vec(i, 3))
            dm = cot[i, rows, :].astype(F32) + r * (
                dn - jnp.mean(dn, axis=-1, keepdims=True) - n * jnp.mean(dn * n, axis=-1, keepdims=True))
            put_wide(dst, i, rows, dm)
            da = (dm * vec(i, 0)).astype(BF16)
            sec[i, rows, :] = da
            return (sums[0] + fold(dm * attended), sums[1] + fold(dy * n), sums[2] + fold(dy), sums[3] + fold(da.astype(F32)))
        sums = lax.fori_loop(0, n_ln, body, (zero, zero, zero, zero))
        for k, s in zip((0, 3, 5), sums[:3]):
            sm[i, k:k + 1, :] = jnp.sum(s, axis=0, keepdims=True)
        sm[2, 2:3, :] = sm[2, 2:3, :] + jnp.sum(sums[3], axis=0, keepdims=True)

        def mixed(t, _):
            rows = rows_of(t, mt)
            d = dot(sec[i, rows, :], projw[...], NT)
            dmx[0, rows, :] = d[:, :128].astype(BF16)
            dmx[1, rows, :] = d[:, 128:].astype(BF16)
            return 0
        lax.fori_loop(0, 2, mixed, 0)

    def attend_back(i, slab):
        blocks = blocks_of(128)
        fill_kv(i, slab)
        acc[...] = jnp.zeros_like(acc)

        def body(rows, keys):
            p = exps(i, slab, rows, keys)
            d = dmx[slab, rows, :]
            q = qkn[i, 0, slab, rows, :]
            ds = []
            dp_both = dot(d, kv[1, :, 0:keys, :].reshape(2 * keys, 128), NT)
            for h in (0, 1):
                dpr = dp_both[:, h * keys:(h + 1) * keys]
                ds.append((p[h] * (dpr - jnp.sum(dpr * p[h], axis=-1, keepdims=True))).astype(BF16))
            acc[0, rows, :] = dot(jnp.concatenate(ds, axis=1), kv[0, :, 0:keys, :].reshape(2 * keys, 128))
            kr = pl.ds(0, keys)
            acc[1, kr, :] += dot(
                jnp.concatenate(ds, axis=0), jnp.concatenate([q * one_head(h) for h in (0, 1)], axis=0), TN)
            acc[2, kr, :] += dot(
                jnp.concatenate([v.astype(BF16) for v in p], axis=0),
                jnp.concatenate([d * one_head(h) for h in (0, 1)], axis=0), TN)
        each_tile(body)
        es = es_row[:, slab * 128:(slab + 1) * 128]

        def close(t, sums):
            rows = rows_of(t, LN_TILE)

            def unit(c, g):
                at = c * 256 + slab * 128
                pre = qk[i, rows, at:at + 128]
                r = lax.rsqrt(head_sum(pre * pre, blocks) + EPSILON)
                u = pre * r
                gu = g * u
                return r * (g - u * head_sum(gu, blocks)), gu
            dq, gu = unit(0, acc[0, rows, :] * es)
            dk, _g = unit(1, acc[1, rows, :])
            dq, dk, dv = dq.astype(BF16), dk.astype(BF16), acc[2, rows, :].astype(BF16)
            to = pl.ds(slab * 128, 128)
            dup[i, 0, rows, to] = dq
            dup[i, 1, rows, to] = dk
            dup[i, 2, rows, to] = dv
            return sums[0] + fold(dq.astype(F32)), sums[1] + fold(dv.astype(F32)), sums[2] + fold(gu)
        zero = jnp.zeros((8, 128), F32)
        sums = lax.fori_loop(0, n_ln, close, (zero, zero, zero))
        for k in range(3):
            lanes[k, slab] = lanes[k, slab] + sums[k]

    def first_grad(i):
        def body(t, _):
            rows = rows_of(t, mt)
            for h in (0, 1):
                total = None
                for c in range(3):
                    o = dot(dup[i, c, rows, :], qkvw[c, h * half:(h + 1) * half, :], NT)
                    total = o if total is None else total + o
                att[i, h, rows, :] = total
            return 0
        lax.fori_loop(0, 2, body, 0)

    def first_back(i):
        zero = jnp.zeros((8, width), F32)

        def body(t, sums):
            rows = rows_of(t, LN_TILE)
            n, r = norm_rows(tok[i, rows, :].astype(F32))
            dy = wide(att, i, rows)
            dn = dy * (1.0 + vec(i, 2))
            g = wide(dst, i, rows) + r * (
                dn - jnp.mean(dn, axis=-1, keepdims=True) - n * jnp.mean(dn * n, axis=-1, keepdims=True))
            dbr[i, rows, :] = g.astype(BF16)
            return sums[0] + fold(dy * n), sums[1] + fold(dy)
        sums = lax.fori_loop(0, n_ln, body, (zero, zero))
        for k, s in zip((2, 4), sums):
            sm[i, k:k + 1, :] = jnp.sum(s, axis=0, keepdims=True)
        pltpu.make_async_copy(dbr.at[i], tg_hbm.at[i], out_sem.at[i]).start()

    def branch(i):
        def body(t, _):
            rows = rows_of(t, mt)
            for h in (0, 1):
                dst[i, h, rows, :] = dot(hid[i, rows, :], fc2w[:, h * half:(h + 1) * half])
            return 0
        lax.fori_loop(0, 2, body, 0)

        def sums_of(t, sums):
            rows = rows_of(t, LN_TILE)
            g = cot[i, rows, :].astype(F32)
            return sums[0] + fold(g * wide(dst, i, rows)), sums[1] + fold(g)
        zero = jnp.zeros((8, width), F32)
        sums = lax.fori_loop(0, n_ln, sums_of, (zero, zero))
        g2r[me, i:i + 1, :] = jnp.sum(sums[0], axis=0, keepdims=True)
        sm[i, 1:2, :] = fc2_b[...] * jnp.sum(sums[1], axis=0, keepdims=True)

    def block_end(i):
        def body(t, _):
            rows = rows_of(t, LN_TILE)
            middle = tok[i, rows, :].astype(F32) + vec(i, 0) * (wide(att, i, rows) + proj_b[...])
            cot[i, rows, :] = (middle + vec(i, 1) * (wide(dst, i, rows) + fc2_b[...])).astype(BF16)
            return 0
        lax.fori_loop(0, n_ln, body, 0)
        pltpu.make_async_copy(cot.at[i], out_hbm.at[i], out_sem.at[2 + i]).start()

    def every_copy(to, source):
        return pltpu.make_async_remote_copy(
            src_ref=sm, dst_ref=every.at[source], send_sem=ev_s.at[to], recv_sem=ev_r.at[source],
            device_id={"dp": to}, device_id_type=MESH)

    def every_start():
        pltpu.make_async_copy(sm, every.at[dp], out_sem.at[4]).start()

        def body(step, _):
            every_copy(lax.rem(dp + step, n_dp), dp).start()
            return 0
        lax.fori_loop(1, n_dp, body, 0)

    def every_finish():
        pltpu.make_async_copy(sm, every.at[dp], out_sem.at[4]).wait()

        def body(step, _):
            every_copy(lax.rem(dp + step, n_dp), dp).wait_send()
            source = lax.rem(dp + n_dp - step, n_dp)
            every_copy(source, source).wait_recv()
            return 0
        lax.fori_loop(1, n_dp, body, 0)

    def rs_both(buf, i, k):
        rs_copy(buf, i, k).start()
        rs_finish(buf, i, k)

    def forward(i):
        first_norm(i)
        if i == 0:
            loads["qkvw"].wait()
        project(i)
        attend(i)
        if i == 0:
            loads["projw"].wait()
        attend_out(i)

    def close_sums():
        sent = share(g2r, g2_s, g2_r)
        for copy in sent:
            copy.wait()
        total = (g2r[0] + g2r[1]) + (g2r[2] + g2r[3])
        for i in (0, 1):
            sm[i, 1:2, :] = sm[i, 1:2, :] + total[i:i + 1, :]
        for j in range(4):
            sm[2, 1:2, j * 256:(j + 1) * 256] = jnp.sum(fb1[j], axis=0, keepdims=True)
        for k in range(3):
            for slab in (0, 1):
                at = k * 256 + slab * 128
                sm[2, 3:4, at:at + 128] = jnp.sum(lanes[k, slab], axis=0, keepdims=True)
        every_start()

    def spill_out(i):
        return pltpu.make_async_copy(att.at[i], spill.at[i], spill_sem.at[i])

    def spill_back(i):
        return pltpu.make_async_copy(spill.at[i], att.at[i], spill_sem.at[2 + i])

    def ag(buf, i, k):
        ag_copy(buf, i, k).start()
        ag_copy(buf, i, k).wait()

    sm[...] = jnp.zeros_like(sm)
    fb1[...] = jnp.zeros_like(fb1)
    lanes[...] = jnp.zeros_like(lanes)
    g2r[...] = jnp.zeros_like(g2r)
    kv[...] = jnp.zeros_like(kv)
    for i in (0, 1):
        sm[i, 6:7, :] = jnp.zeros((1, width), F32) + labels[i].astype(F32)
    unpack(tok_hbm, 1, tok, (cot_hbm, 0))
    forward(0)
    rs_both(att, 0, ATT)
    y_start(att, 0, ATT)
    forward(1)
    rs_both(att, 1, ATT)
    y_start(att, 1, ATT)
    unpack(cot_hbm, 0, cot, (cot_hbm, 1))
    unpack(cot_hbm, 1, cot)
    for name in ("fc1w", "fc2w"):
        loads[name].wait()
    y_finish(att, 0, ATT)
    ag(att, 0, ATT)
    mlp(0)
    rs_both(dst, 0, DS)
    y_start(dst, 0, DS)
    y_finish(att, 1, ATT)
    ag(att, 1, ATT)
    mlp(1)
    rs_copy(dst, 1, DS).start()
    fc_grads((7, 4, 0,))
    rs_finish(dst, 1, DS)
    y_start(dst, 1, DS)
    fc_grads((3, 1, 6, 5, 2,))
    serve((2, 7))
    y_finish(dst, 0, DS)
    ag(dst, 0, DS)
    serve((2, 4))
    second_back(0)
    spill_out(0).start()
    serve((2, 0))
    attend_back(0, 0)
    serve((3, 4))
    attend_back(0, 1)
    serve((2, 3))
    spill_out(0).wait()
    first_grad(0)
    serve((3, 0))
    serve((4, 4))
    rs_both(att, 0, DF)
    serve((2, 1), (3, 7))
    y_start(att, 0, DF)
    serve((3, 3))
    y_finish(dst, 1, DS)
    ag(dst, 1, DS)
    s5(4)
    serve((4, 0))
    second_back(1)
    spill_out(1).start()
    serve((3, 1), (2, 6))
    serve((2, 5))
    serve((4, 3))
    attend_back(1, 0)
    serve((3, 6))
    s5(0)
    serve((4, 1))
    attend_back(1, 1)
    spill_out(1).wait()
    first_grad(1)
    serve((4, 7))
    rs_both(att, 1, DF)
    y_start(att, 1, DF)
    serve((2, 2))
    first_norm(0)
    serve((4, 6), (3, 5))
    first_norm(1)
    attention_grads((11,))
    serve((3, 2))
    attention_grads((10, 9,))
    s5(7)
    s6(4)
    attention_grads((8,))
    serve((4, 5))
    y_finish(att, 0, DF)
    ag(att, 0, DF)
    first_back(0)
    spill_back(0).start()
    serve((2, 11))
    branch(0)
    rs_both(dst, 0, BR)
    y_start(dst, 0, BR)
    y_finish(att, 1, DF)
    serve((4, 2))
    ag(att, 1, DF)
    serve((3, 11), (2, 10))
    s5(1)
    first_back(1)
    spill_back(1).start()
    s5(3)
    serve((3, 10))
    branch(1)
    rs_both(dst, 1, BR)
    y_start(dst, 1, BR)
    serve((4, 11), (2, 9))
    serve((2, 8))
    s5(2)
    serve((3, 9))
    s5(6)
    serve((4, 10))
    serve((3, 8))
    close_sums()
    serve((4, 9))
    serve((4, 8))
    y_finish(dst, 0, BR)
    ag(dst, 0, BR)
    s6(0)
    s5(5)
    s5(11)
    s6(6)
    spill_back(0).wait()
    block_end(0)
    y_finish(dst, 1, BR)
    s5(10)
    s6(2)
    s5(9)
    ag(dst, 1, BR)
    s5(8)
    spill_back(1).wait()
    block_end(1)
    every_finish()
    for n in (4, 7, 3, 1, 0, 5, 6, 11, 2, 10, 9, 8):
        close_chunk(n)
    for i in (0, 1):
        pltpu.make_async_copy(dbr.at[i], tg_hbm.at[i], out_sem.at[i]).wait()
        pltpu.make_async_copy(cot.at[i], out_hbm.at[i], out_sem.at[2 + i]).wait()


def run_block(n_dp, lifted, ada_b, ada_w, tok, cot, stops, labels, log_scale, qkvw, projw, fc1w, fc2w, qv_b, proj_b, fc1_b, fc2_b):
    items, slots, width = tok.shape
    padded = -(-slots // LN_TILE) * LN_TILE
    x_count = sum(r != "Z" for r in ROUTES)
    half = width // 2
    hidden = fc1w.shape[1]
    n_chunks = 12
    n_rest = max(1, (n_dp // 8).bit_length() - 1)
    hbm = pl.BlockSpec(memory_space=pl.ANY)
    vmem = pl.BlockSpec(memory_space=pltpu.VMEM)
    smem = pl.BlockSpec(memory_space=pltpu.SMEM)
    wide_b = (items, padded, width)
    wide_f = (items, 2, padded, half)
    dma = pltpu.SemaphoreType.DMA
    return pl.pallas_call(
        functools.partial(block_kernel, slots, n_dp),
        out_shape=(
            jax.ShapeDtypeStruct(wide_b, BF16), jax.ShapeDtypeStruct(wide_b, BF16),
            jax.ShapeDtypeStruct(fc1w.shape, F32), jax.ShapeDtypeStruct(fc2w.shape, F32),
            jax.ShapeDtypeStruct(projw.shape, F32), jax.ShapeDtypeStruct(qkvw.shape, F32),
            jax.ShapeDtypeStruct((n_dp, 3, 8, width), F32),
            jax.ShapeDtypeStruct((n_chunks, 128, width), F32), jax.ShapeDtypeStruct((n_chunks, 128, width), F32),
            jax.ShapeDtypeStruct((n_chunks, 256, width), F32), jax.ShapeDtypeStruct((n_chunks, 128, width), F32),
            jax.ShapeDtypeStruct((n_rest, n_chunks, 128, width), F32), jax.ShapeDtypeStruct(wide_f, F32),
        ),
        in_specs=[vmem, vmem, hbm, hbm, hbm, smem, smem, smem, hbm, hbm, hbm, hbm, vmem, vmem, vmem, vmem],
        out_specs=(hbm,) * 13,
        scratch_shapes=[
            *[pltpu.VMEM(wide_b, BF16) for _ in range(4)],
            pltpu.VMEM((items, padded, hidden), BF16), pltpu.VMEM((items, hidden // 256, padded, 256), BF16),
            *[pltpu.VMEM(wide_f, F32) for _ in range(2)],
            pltpu.VMEM((items, padded, half), F32),
            pltpu.VMEM((items, 3, 2, padded, 128), BF16),
            pltpu.VMEM((items, 2, padded, 128), BF16),
            pltpu.VMEM((2, padded, 128), BF16),
            pltpu.VMEM((2, 2, 768, 128), BF16),
            pltpu.VMEM((3, 768, 128), F32),
            pltpu.VMEM((items, slots, half), F32),
            pltpu.VMEM((items, slots, half), F32),
            pltpu.VMEM(qkvw.shape, BF16), pltpu.VMEM(projw.shape, BF16),
            pltpu.VMEM(fc1w.shape, BF16), pltpu.VMEM(fc2w.shape, BF16),
            pltpu.VMEM((slots, width), BF16), pltpu.VMEM((1, qkvw.shape[2]), F32),
            pltpu.VMEM((max(1, x_count), 128, width), F32), pltpu.VMEM((max(1, n_chunks - x_count), 256, width), F32),
            pltpu.VMEM((2, 256, width), F32), pltpu.VMEM((128 if n_dp > 8 else 8, width), F32),
            pltpu.VMEM((4, items, 8, width), F32), pltpu.VMEM((items, 8, width), F32),
            pltpu.VMEM((4, 8, width), F32),
            pltpu.VMEM((4, 8, 256), F32), pltpu.VMEM((3, 2, 8, 128), F32), pltpu.VMEM((3, 8, width), F32),
            dma((10,)), dma, dma((5,)), dma((5,)), dma((2,)), dma((2,)), dma((n_chunks, 4)), dma((4,)), pltpu.SemaphoreType.REGULAR((2,)),
            dma((3,)), dma((3,)), dma((3,)), dma((3,)),
            *[dma((8,)) for _ in range(6)],
            *[dma((n_chunks,)) for _ in range(8)], *[dma((n_chunks, 4)) for _ in range(6)],
            dma((n_rest, n_chunks)), dma((n_rest, n_chunks)), dma((n_dp,)), dma((n_dp,)),
        ],
        compiler_params=pltpu.CompilerParams(
            collective_id=0, has_side_effects=True, vmem_limit_bytes=62 * 2**20),
        name="block",
    )(lifted, ada_b, ada_w, tok, cot, stops, labels, log_scale, qkvw, projw, fc1w, fc2w, qv_b, proj_b, fc1_b, fc2_b)


def tail_kernel(
    every_hbm, table_hbm, ada_hbm, g1_in, g2_in, gp_in, gq_in,
    table_grad, ada_grad, ada_rows, small, g1, g2, gp, gq,
    every, table, ada, part, sem, part_sem, copy_sem,
):
    n_dp, width = every.shape[0], every.shape[3]
    rows = 2 * n_dp
    copies = [pltpu.make_async_copy(a, b, copy_sem.at[k])
              for k, (a, b) in enumerate(((g1_in, g1), (g2_in, g2), (gp_in, gp), (gq_in, gq)))]
    loads = [pltpu.make_async_copy(a, b, sem.at[k])
             for k, (a, b) in enumerate(((every_hbm, every), (table_hbm, table), (ada_hbm, ada)))]
    for copy in (*loads, *copies):
        copy.start()
    loads[0].wait()
    total = every[0, 2]
    for d in range(1, n_dp):
        total = total + every[d, 2]
    small[...] = total

    def gathered(k):
        return jnp.concatenate([every[d, i, k:k + 1, :] for d in range(n_dp) for i in (0, 1)], axis=0)
    label = gathered(6)[:, 0:1]
    classes = table.shape[0]
    hot = jnp.where(lax.broadcasted_iota(jnp.int32, (rows, classes), 1).astype(F32) == label, 1.0, 0.0)
    loads[1].wait()
    local = dot(hot.astype(BF16), table[...])
    gate = 1.0 / (1.0 + jnp.exp(-local))
    lifted = (local * gate).astype(BF16)
    loads[2].wait()
    lifted_grad = jnp.zeros(local.shape, F32)

    def out_copy(k):
        return pltpu.make_async_copy(part.at[k % 2], ada_grad.at[:, pl.ds(k * width, width)], part_sem.at[k % 2])
    ada_rows[...] = jnp.zeros_like(ada_rows)
    for k in range(6):
        low = gathered(k).astype(BF16)
        ada_rows[k:k + 1, :] = jnp.sum(low.astype(F32), axis=0, keepdims=True)
        lifted_grad = lifted_grad + dot(low, ada[:, k * width:(k + 1) * width], NT)
        if k >= 2:
            out_copy(k - 2).wait()
        part[k % 2] = dot(lifted, low, TN)
        out_copy(k).start()
    class_grad = lifted_grad * (gate * (1.0 + local * (1.0 - gate)))
    table_grad[...] = lax.dot_general(hot, class_grad, TN, precision=lax.Precision.HIGHEST, preferred_element_type=F32)
    out_copy(4).wait()
    out_copy(5).wait()
    for copy in copies:
        copy.wait()


def run_tail(n_dp, every, class_table, ada_weight, g1, g2, gp, gq):
    classes, wide = class_table.shape
    width = every.shape[3]
    hbm = pl.BlockSpec(memory_space=pl.ANY)
    vmem = pl.BlockSpec(memory_space=pltpu.VMEM)
    dma = pltpu.SemaphoreType.DMA
    shape = lambda *dims: jax.ShapeDtypeStruct(dims, F32)
    return pl.pallas_call(
        tail_kernel,
        out_shape=(shape(classes, wide), shape(*ada_weight.shape), shape(8, width), shape(8, width),
                   shape(*g1.shape), shape(*g2.shape), shape(*gp.shape), shape(*gq.shape)),
        in_specs=[hbm] * 7,
        out_specs=(vmem, hbm, vmem, vmem, hbm, hbm, hbm, hbm),
        scratch_shapes=[
            pltpu.VMEM(every.shape, F32), pltpu.VMEM(class_table.shape, BF16), pltpu.VMEM(ada_weight.shape, BF16),
            pltpu.VMEM((2, wide, width), F32), dma((3,)), dma((2,)), dma((4,)),
        ],
        compiler_params=pltpu.CompilerParams(vmem_limit_bytes=24 * 2**20),
        name="tail",
    )(every, class_table, ada_weight, g1, g2, gp, gq)


def shards(
    n_dp, tokens, cotangent, stop_scales, labels, class_table, ada_weight, ada_bias, qkv_weight, qv_bias, log_scale,
    proj_weight, proj_bias, fc1_weight, fc1_bias, fc2_weight, fc2_bias,
):
    items, slots, width = tokens.shape
    heads = log_scale.shape[0]
    class_local = jnp.concatenate(
        [lax.dynamic_slice_in_dim(class_table, labels[i], 1, 0) for i in range(items)], axis=0).astype(F32)
    lifted = jnp.pad(jax.nn.silu(class_local).astype(BF16), ((0, 16 - items), (0, 0)))
    out, tg, g1, g2, gp, gq, every, *_ = run_block(
        n_dp, lifted, ada_bias.reshape(6, width), ada_weight, tokens, cotangent, stop_scales, labels, log_scale,
        jnp.transpose(qkv_weight, (1, 0, 2)), proj_weight, fc1_weight, fc2_weight,
        qv_bias, proj_bias[None, :], fc1_bias.reshape(-1, 1, 256), fc2_bias[None, :])
    table_grad, ada_weight_grad, ada_rows, small, g1, g2, gp, gq = run_tail(
        n_dp, every, class_table, ada_weight, g1, g2, gp, gq)
    lanes = small[3]
    return (
        out[:, :slots], tg[:, :slots], table_grad, ada_weight_grad, ada_rows[:6].reshape(-1),
        jnp.transpose(gq, (1, 0, 2)), lanes[:512].reshape(2, 256), lanes[512:768].reshape(heads, -1).sum(axis=1),
        gp, small[2], g1, small[1], g2, small[0],
    )


def solution(mesh):
    return jax.shard_map(
        functools.partial(shards, mesh.shape["dp"]),
        mesh=mesh,
        in_specs=(
            P("dp", None, None), P("dp", None, None), P("dp"), P("dp"), P(None, "mp"), P("mp", None), P(),
            P(None, None, "mp"), P(None, "mp"), P("mp"), P("mp", None), P(), P(None, "mp"), P("mp"), P("mp", None), P(),
        ),
        out_specs=(
            P("dp", None, None), P("dp", None, None), P(None, "mp"), P("mp", None), P(), P(None, None, "mp"), P(None, "mp"),
            P("mp"), P("mp", None), P(), P(None, "mp"), P("mp"), P("mp", None), P(),
        ),
        check_vma=False,
    )
```

```python
import functools

import jax
import jax.numpy as jnp
import numpy as np
from jax import lax
from jax.experimental import pallas as pl
from jax.experimental.pallas import tpu as pltpu
from jax.sharding import PartitionSpec as P

SIDE_LIST = (1, 2, 3, 4, 5, 6, 8, 10, 13, 16)
EPSILON = 1e-06
MESH = pl.DeviceIdType.MESH
F32, BF16 = jnp.float32, jnp.bfloat16
GELU_C = 0.7978845608028654
GELU_A = 0.044715
LN_TILE = 176
NT = (((1,), (1,)), ((), ()))
TN = (((0,), (0,)), ((), ()))
NN = (((1,), (0,)), ((), ()))
ATT, DS, DF, BR = 0, 2, 4, 6
ROUTES = "CAAZACBACAAZ"


def dot(a, b, dims=NN):
    return lax.dot_general(a, b, dims, preferred_element_type=F32)


def norm_rows(v):
    center = v - jnp.mean(v, axis=-1, keepdims=True)
    scale = lax.rsqrt(jnp.mean(center * center, axis=-1, keepdims=True) + EPSILON)
    return center * scale, scale


def fold(v):
    return jnp.sum(v.reshape(v.shape[0] // 8, 8, v.shape[1]), axis=0)


def head_sum(v, blocks):
    high = v.astype(BF16)
    rest = (v - high.astype(F32)).astype(BF16)
    return dot(high, blocks) + dot(rest, blocks)


def block_kernel(
    slots, n_dp,
    table_hbm, ada_b, ada_hbm, tok_hbm, cot_hbm, stops, labels, log_scale,
    qkvw_hbm, projw_hbm, fc1w_hbm, fc2w_hbm,
    qv_b, proj_b, fc1_b, fc2_b,
    out_hbm, tg_hbm, g1_out, g2_out, gp_out, gq_out, every, x_out, x_in, z_in, mid_in, rest_in, spill,
    tok, cot, sec, dbr, hid, dup,
    att, dst,
    qk, qkn, mix, dmx, kv, acc,
    rs_buf, y_buf,
    qkvw, projw, fc1w, fc2w,
    raw, table, es_row, px, pz, stage, modr, mod, g2r, fb1, lanes, sm,
    in_sem, raw_sem, out_sem, load_sem, store_sem, keep_sem, final_sem, spill_sem, y_free,
    mod_s, mod_r, g2_s, g2_r, rs_s, rs_r, y_s, y_r, ag_s, ag_r,
    x1_s, x1_r, zi_s, zi_r, mi_s, mi_r, zb_s, zb_r, zo_s, zo_r, x2_s, x2_r, zc_s, zc_r, re_s, re_r, ev_s, ev_r,
):
    items, padded, width = tok.shape
    half = width // 2
    me = lax.axis_index("mp")
    dp = lax.axis_index("dp")
    xb = lax.rem(dp, 2)
    z = lax.rem(dp // 2, 4)
    zh = z // 2
    inner = jnp.logical_or(z == 1, z == 2)
    edge = jnp.logical_or(z == 0, z == 3)
    x_mate = dp + 1 - 2 * xb
    z_mate = dp + 2 - 4 * lax.rem(z, 2)
    mid_mate = jnp.where(z == 1, dp + 2, jnp.where(z == 2, dp - 2, dp))
    n_rest = rest_in.shape[0] if n_dp > 8 else 0
    rest_mates = [dp + (8 << k) * (1 - 2 * lax.rem(dp // (8 << k), 2)) for k in range(n_rest)]
    core = lax.rem(me, 2)
    core_mate = me + 1 - 2 * core
    y_mate = lax.rem(me + 2, 4)
    n_ln = padded // LN_TILE
    mt = padded // 2

    def rows_of(t, n):
        return pl.ds(pl.multiple_of(t * n, n), n)

    def wide(buf, i, rows):
        return jnp.concatenate([buf[i, 0, rows, :], buf[i, 1, rows, :]], axis=1)

    def put_wide(buf, i, rows, v):
        buf[i, 0, rows, :] = v[:, :half]
        buf[i, 1, rows, :] = v[:, half:]

    def raw_copy(src, i):
        return pltpu.make_async_copy(src.at[i], raw, raw_sem)

    def unpack(src, i, to, then=None):
        raw_copy(src, i).wait()
        whole = slots // 16 * 16

        def body(t, _):
            rows = rows_of(t, 16)
            to[i, rows, :] = raw[rows, :]
            return 0
        lax.fori_loop(0, slots // 16, body, 0)
        tail = raw[whole:slots, :].astype(F32)
        rest = jnp.concatenate([tail, jnp.zeros((padded - slots, width), F32)], axis=0)
        to[i, whole:padded, :] = rest.astype(BF16)
        if then is not None:
            raw_copy(*then).start()

    raw_copy(tok_hbm, 0).start()
    rows_ada = ada_hbm.shape[0]
    ada_room = [buf.at[i, pl.ds(k * rows_ada, rows_ada)] for buf, i, k in (
        (hid, 0, 0), (hid, 0, 1), (hid, 1, 0), (hid, 1, 1), (sec, 0, 0), (sec, 1, 0))]
    loads = {}
    for k, (name, src, to) in enumerate((
        ("table", table_hbm, table),
        *[(f"ada{c}", ada_hbm.at[:, pl.ds(c * width, width)], ada_room[c]) for c in range(6)],
        ("qkvw", qkvw_hbm, qkvw), ("projw", projw_hbm, projw), ("fc1w", fc1w_hbm, fc1w), ("fc2w", fc2w_hbm, fc2w),
    )):
        loads[name] = pltpu.make_async_copy(src, to, in_sem.at[k])
        loads[name].start()

    barrier = pltpu.get_barrier_semaphore()
    for step in (1, 2, 3):
        pl.semaphore_signal(barrier, inc=1, device_id={"mp": lax.rem(me + step, 4)}, device_id_type=MESH)
    def greet(step, _):
        pl.semaphore_signal(barrier, inc=1, device_id={"dp": lax.rem(dp + step, n_dp)}, device_id_type=MESH)
        return 0
    lax.fori_loop(1, n_dp, greet, 0)

    def share(buf, send, recv):
        copies = []
        for step in (1, 2, 3):
            copies.append(pltpu.make_async_remote_copy(
                src_ref=buf.at[me], dst_ref=buf.at[me], send_sem=send.at[step - 1], recv_sem=recv.at[step - 1],
                device_id={"mp": lax.rem(me + step, 4)}, device_id_type=MESH))
        for copy in copies:
            copy.start()
        return copies

    loads["table"].wait()
    spot = (16, table.shape[0])
    item_at = lax.broadcasted_iota(jnp.int32, spot, 0)
    class_at = lax.broadcasted_iota(jnp.int32, spot, 1)
    hot = jnp.zeros(spot, F32)
    for i in range(items):
        hot = jnp.where(jnp.logical_and(item_at == i, class_at == labels[i]), 1.0, hot)
    local = dot(hot.astype(BF16), table[...])
    lifted = (local * (1.0 / (1.0 + jnp.exp(-local)))).astype(BF16)
    for c in range(6):
        loads[f"ada{c}"].wait()
        part = dot(lifted, ada_room[c][...])
        for i in range(items):
            modr[me, i, c:c + 1, :] = part[i:i + 1, :]
    for i in range(items):
        modr[me, i, 6:8, :] = jnp.zeros((2, width), F32)
    pl.semaphore_wait(barrier, 3 + n_dp - 1)
    sent = share(modr, mod_s, mod_r)
    unpack(tok_hbm, 0, tok, (tok_hbm, 1))

    def early(t, _):
        rows = rows_of(t, LN_TILE)
        n, _r = norm_rows(tok[0, rows, :].astype(F32))
        put_wide(att, 0, rows, n)
        return 0
    lax.fori_loop(0, n_ln, early, 0)
    for copy in sent:
        copy.wait()
    mod[...] = (modr[0] + modr[1]) + (modr[2] + modr[3])
    for i in range(items):
        for c in range(6):
            mod[i, c:c + 1, :] = mod[i, c:c + 1, :] + ada_b[:, c * width:(c + 1) * width]
    lane = lax.broadcasted_iota(jnp.int32, es_row.shape, 1) // 64
    scales = jnp.zeros(es_row.shape, F32)
    for h in range(es_row.shape[1] // 64):
        scales = jnp.where(lane == h, log_scale[h], scales)
    es_row[...] = jnp.exp(scales)

    def vec(i, k):
        return mod[i, k:k + 1, :]

    def rs_copy(buf, i, k):
        return pltpu.make_async_remote_copy(
            src_ref=buf.at[i, 1 - core, pl.ds(0, slots)], dst_ref=rs_buf.at[i], send_sem=rs_s.at[k + i], recv_sem=rs_r.at[k + i],
            device_id={"mp": core_mate}, device_id_type=MESH)

    def y_copy(buf, i, k):
        dst = qk.at[i, pl.ds(0, slots)] if k == BR else y_buf.at[i]
        return pltpu.make_async_remote_copy(
            src_ref=buf.at[i, core, pl.ds(0, slots)], dst_ref=dst, send_sem=y_s.at[k + i], recv_sem=y_r.at[k + i],
            device_id={"mp": y_mate}, device_id_type=MESH)

    def ag_copy(buf, i, k):
        return pltpu.make_async_remote_copy(
            src_ref=buf.at[i, core, pl.ds(0, slots)], dst_ref=buf.at[i, core, pl.ds(0, slots)],
            send_sem=ag_s.at[k + i], recv_sem=ag_r.at[k + i],
            device_id={"mp": core_mate}, device_id_type=MESH)

    add_rows = slots // 5

    def rs_finish(buf, i, k):
        rs_copy(buf, i, k).wait()

        def add(t, _):
            rows = rows_of(t, add_rows)
            buf[i, core, rows, :] = buf[i, core, rows, :] + rs_buf[i, rows, :]
            return 0
        lax.fori_loop(0, 5, add, 0)

    def y_finish(buf, i, k):
        y_copy(buf, i, k).wait()

        def add(t, _):
            rows = rows_of(t, add_rows)
            other = qk[i, rows, :] if k == BR else y_buf[i, rows, :]
            buf[i, core, rows, :] = buf[i, core, rows, :] + other
            return 0
        lax.fori_loop(0, 5, add, 0)
        if k in (ATT, DS):
            pl.semaphore_signal(y_free.at[i], inc=1, device_id={"mp": y_mate}, device_id_type=MESH)

    def y_start(buf, i, k):
        if k in (DS, DF):
            pl.semaphore_wait(y_free.at[i], 1)
        y_copy(buf, i, k).start()

    def blocks_of(n):
        a = lax.broadcasted_iota(jnp.int32, (n, n), 0) // 64
        b = lax.broadcasted_iota(jnp.int32, (n, n), 1) // 64
        return jnp.where(a == b, 1.0, 0.0).astype(BF16)

    ends = np.cumsum(np.array([s * s for s in SIDE_LIST]))
    tiles = ((0, 240, 1, 256), (240, 176, 1, 512), (416, 96, 3, 768))

    def keep_of(i, rows, keys):
        live = jnp.int32(0)
        for s in range(len(SIDE_LIST)):
            live = jnp.where(stops[i] == s + 1, int(ends[s]), live)
        n = rows.size
        at = rows.start + lax.broadcasted_iota(jnp.int32, (n, 1), 0)
        bound = jnp.full((n, 1), int(ends[0]), jnp.int32)
        for s in range(1, len(SIDE_LIST)):
            bound = jnp.where(at >= int(ends[s - 1]), int(ends[s]), bound)
        bound = jnp.minimum(bound, live)
        return lax.broadcasted_iota(jnp.int32, (n, keys), 1) < bound

    def one_head(h):
        lane = lax.broadcasted_iota(jnp.int32, (1, 128), 1) // 64
        return jnp.where(lane == h, 1.0, 0.0).astype(BF16)

    def fill_kv(i, slab):
        for c in (0, 1):
            for h in (0, 1):
                kv[c, h, 0:padded, :] = qkn[i, 1 + c, slab] * one_head(h)

    def exps(i, slab, rows, keys):
        keep = keep_of(i, rows, keys)
        s = dot(qkn[i, 0, slab, rows, :], kv[0, :, 0:keys, :].reshape(2 * keys, 128), NT)
        parts = []
        for h in (0, 1):
            e = jnp.where(keep, jnp.exp(s[:, h * keys:(h + 1) * keys]), 0.0)
            parts.append(e * (1.0 / jnp.sum(e, axis=-1, keepdims=True)))
        return parts

    def each_tile(body):
        for first_row, n, steps, keys in tiles:
            if steps == 1:
                body(pl.ds(first_row, n), keys)
            else:
                def step(t, _, first_row=first_row, n=n, keys=keys):
                    body(pl.ds(pl.multiple_of(first_row + t * n, 16), n), keys)
                    return 0
                lax.fori_loop(0, steps, step, 0)

    def first_norm(i, ready=False):
        def body(t, _):
            rows = rows_of(t, LN_TILE)
            n = wide(att, i, rows) if ready else norm_rows(tok[i, rows, :].astype(F32))[0]
            dbr[i, rows, :] = (n * (1.0 + vec(i, 2)) + vec(i, 4)).astype(BF16)
            return 0
        lax.fori_loop(0, n_ln, body, 0)

    def project(i):
        blocks = blocks_of(256)

        def body(t, _):
            rows = rows_of(t, mt)
            f = dbr[i, rows, :]
            q = dot(f, qkvw[0]) + qv_b[0:1, :]
            qk[i, rows, 0:256] = q
            u = q * lax.rsqrt(head_sum(q * q, blocks) + EPSILON) * es_row[...]
            qkn[i, 0, 0, rows, :] = u[:, :128].astype(BF16)
            qkn[i, 0, 1, rows, :] = u[:, 128:].astype(BF16)
            k = dot(f, qkvw[1])
            qk[i, rows, 256:512] = k
            u = k * lax.rsqrt(head_sum(k * k, blocks) + EPSILON)
            qkn[i, 1, 0, rows, :] = u[:, :128].astype(BF16)
            qkn[i, 1, 1, rows, :] = u[:, 128:].astype(BF16)
            v = dot(f, qkvw[2]) + qv_b[1:2, :]
            qkn[i, 2, 0, rows, :] = v[:, :128].astype(BF16)
            qkn[i, 2, 1, rows, :] = v[:, 128:].astype(BF16)
            return 0
        lax.fori_loop(0, 2, body, 0)

    def attend(i):
        def slab_body(slab, _):
            fill_kv(i, slab)

            def body(rows, keys):
                p = jnp.concatenate([v.astype(BF16) for v in exps(i, slab, rows, keys)], axis=1)
                o = dot(p, kv[1, :, 0:keys, :].reshape(2 * keys, 128))
                mix[i, slab, rows, :] = o.astype(BF16)
            each_tile(body)
            return 0
        lax.fori_loop(0, 2, slab_body, 0)

    def attend_out(i):
        def body(t, _):
            rows = rows_of(t, mt)
            m = jnp.concatenate([mix[i, 0, rows, :], mix[i, 1, rows, :]], axis=1)
            for h in (0, 1):
                att[i, h, rows, :] = dot(m, projw[:, h * half:(h + 1) * half])
            return 0
        lax.fori_loop(0, 2, body, 0)

    def mlp(i):
        def body(t, total):
            rows = rows_of(t, LN_TILE)
            middle = tok[i, rows, :].astype(F32) + vec(i, 0) * (wide(att, i, rows) + proj_b[...])
            n, _r = norm_rows(middle)
            sec[i, rows, :] = (n * (1.0 + vec(i, 3)) + vec(i, 5)).astype(BF16)
            d = (cot[i, rows, :].astype(F32) * vec(i, 1)).astype(BF16)
            dbr[i, rows, :] = d
            return total + fold(d.astype(F32))
        total = lax.fori_loop(0, n_ln, body, jnp.zeros((8, width), F32))
        sm[2, 0:1, :] = sm[2, 0:1, :] + jnp.sum(total, axis=0, keepdims=True)

        def column(j, _):
            cols = pl.ds(pl.multiple_of(j * 256, 256), 256)

            def body(t, _):
                rows = rows_of(t, mt)
                u = dot(sec[i, rows, :], fc1w[:, cols]) + fc1_b[j]
                dh = dot(dbr[i, rows, :], fc2w[cols, :], NT)
                th = jnp.tanh(GELU_C * (u + GELU_A * u * u * u))
                hid[i, rows, cols] = (0.5 * u * (1.0 + th)).astype(BF16)
                slope = 0.5 * (1.0 + th) + 0.5 * u * (1.0 - th * th) * (GELU_C + (3.0 * GELU_C * GELU_A) * u * u)
                d = (dh * slope).astype(BF16)
                dup[i, j, rows, :] = d
                fb1[j] = fb1[j] + fold(d.astype(F32))
                return 0
            lax.fori_loop(0, 2, body, 0)
            return 0
        lax.fori_loop(0, dup.shape[1], column, 0)

        def back(t, _):
            rows = rows_of(t, mt)
            d = jnp.concatenate([dup[i, j, rows, :] for j in range(dup.shape[1])], axis=1)
            for h in (0, 1):
                dst[i, h, rows, :] = dot(d, fc1w[h * half:(h + 1) * half, :], NT)
            return 0
        lax.fori_loop(0, 2, back, 0)

    x_list = [n for n in range(12) if ROUTES[n] != "Z"]
    z_list = [n for n in range(12) if ROUTES[n] == "Z"]

    def is_x(n):
        return ROUTES[n] != "Z"

    def side(h):
        return pl.ds(pl.multiple_of(h * 128, 128), 128)

    def own(n):
        return px.at[x_list.index(n)] if is_x(n) else pz.at[z_list.index(n), side(zh)]

    def final_of(n, h):
        if n < 8:
            return [(g2_out if n < 4 else g1_out).at[pl.ds(pl.multiple_of((n % 4) * 256 + h * 128, 128), 128)]]
        if n == 8:
            return [gp_out.at[side(h)]]
        return [gq_out.at[n - 9, pl.ds(pl.multiple_of(j * 256 + h * 128, 128), 128)] for j in range(4)]

    def in_pieces(n, ref):
        return [ref] if n < 9 else [ref.at[:, pl.ds(j * 256, 256)] for j in range(4)]

    def my_half(n):
        return xb if is_x(n) else zh

    class Pieces:
        def __init__(self, n, srcs, tos, send, recv, mate):
            self.parts = lambda: [
                to_dp(a, b, send.at[n, j], recv.at[n, j], mate) for j, (a, b) in enumerate(zip(srcs, tos))]

        def start(self):
            for part in self.parts():
                part.start()

        def wait_send(self):
            for part in self.parts():
                part.wait_send()

        def wait_recv(self):
            for part in self.parts():
                part.wait_recv()

        def wait(self):
            self.wait_send()
            self.wait_recv()

    def to_dp(src, to, send, recv, mate):
        return pltpu.make_async_remote_copy(
            src_ref=src, dst_ref=to, send_sem=send, recv_sem=recv, device_id={"dp": mate}, device_id_type=MESH)

    def x1(n):
        return to_dp(x_out.at[n] if is_x(n) else own(n), x_in.at[n], x1_s.at[n], x1_r.at[n], x_mate)

    def zin(n):
        if is_x(n):
            return to_dp(own(n), z_in.at[n, pl.ds(0, 128)], zi_s.at[n], zi_r.at[n], z_mate)
        return to_dp(far(n), z_in.at[n, side(1 - zh)], zi_s.at[n], zi_r.at[n], z_mate)

    def far(n):
        return pz.at[z_list.index(n), side(1 - zh)]

    def zin_b(n):
        return to_dp(own(n), z_in.at[n, side(zh)], zb_s.at[n], zb_r.at[n], z_mate)

    def mid(n):
        return to_dp(own(n) if is_x(n) else far(n), mid_in.at[n], mi_s.at[n], mi_r.at[n], mid_mate)

    def zout(n):
        return Pieces(n, in_pieces(n, own(n)), final_of(n, my_half(n)), zo_s, zo_r, z_mate)

    def zout_b(n):
        views = final_of(n, 1 - my_half(n))
        return Pieces(n, views, views, zc_s, zc_r, z_mate)

    def x2(n, at_the_edge=False):
        views = final_of(n, xb)
        return Pieces(n, views if at_the_edge else in_pieces(n, own(n)), views, x2_s, x2_r, x_mate)

    def swap(n):
        return Pieces(n, in_pieces(n, own(n)), final_of(n, zh), x2_s, x2_r, mid_mate)

    class store_final:
        def __init__(self, n):
            self.parts = lambda: [
                pltpu.make_async_copy(a, b, final_sem.at[n, j])
                for j, (a, b) in enumerate(zip(in_pieces(n, own(n)), final_of(n, my_half(n))))]

        def start(self):
            for part in self.parts():
                part.start()

        def wait(self):
            for part in self.parts():
                part.wait()

    def at_edge(body):
        pl.when(edge)(body)

    def at_inner(body):
        pl.when(inner)(body)

    def accumulate(to, what):
        def add(t, _):
            rows = rows_of(t, 16)
            to[rows, :] = to[rows, :] + what[rows, :]
            return 0
        lax.fori_loop(0, 8, add, 0)

    def add_all(items):
        def slot(k):
            return stage.at[0, pl.ds((k % 2) * 128, 128)]

        def load(k):
            return pltpu.make_async_copy(items[k][1], slot(k), load_sem.at[k % 4])

        def begin(k):
            items[k][0]()
            load(k).start()
        for k in range(min(2, len(items))):
            begin(k)
        for k in range(len(items)):
            load(k).wait()
            accumulate(items[k][2], slot(k))
            items[k][3]()
            if k + 2 < len(items):
                begin(k + 2)

    def rest_sum(n):
        for k in range(n_rest):
            copy = to_dp(own(n), rest_in.at[k, n], re_s.at[k, n], re_r.at[k, n], rest_mates[k])
            copy.start()
            copy.wait()
            extra = stage.at[1, pl.ds(0, 128)]
            load = pltpu.make_async_copy(rest_in.at[k, n], extra, load_sem.at[4])
            load.start()
            load.wait()
            accumulate(own(n), extra)

    def items_of(step, n):
        if is_x(n):
            if step == 2:
                return [(lambda: x1(n).wait(), x_in.at[n], own(n), lambda: at_edge(lambda: zin(n).start()))]
            if step == 3:
                return [(lambda: zin(n).wait_recv(), z_in.at[n, pl.ds(0, 128)], own(n), lambda: mid(n).start())]

            def close():
                rest_sum(n)
                zout(n).start()
                if ROUTES[n] != "C":
                    x2(n).start()
                store_final(n).start()
            return [(lambda: mid(n).wait(), mid_in.at[n], own(n), close)]
        if step == 2:
            return [(lambda: zin(n).wait_recv(), z_in.at[n, side(1 - zh)], far(n), lambda: mid(n).start())]
        if step == 3:
            def close():
                rest_sum(n)
                x1(n).start()
            return [
                (lambda: zin_b(n).wait_recv(), z_in.at[n, side(zh)], own(n), lambda: None),
                (lambda: mid(n).wait(), mid_in.at[n], own(n), close)]

        def close():
            swap(n).start()
            zout(n).start()
            store_final(n).start()
        return [(lambda: x1(n).wait(), x_in.at[n], own(n), close)]

    def serve(*tasks):
        at_inner(lambda: add_all([item for step, n in tasks for item in items_of(step, n)]))
        outer = [item for step, n in tasks if step == 2 and is_x(n) for item in items_of(step, n)]
        if outer:
            at_edge(lambda: add_all(outer))

    def s5(n):
        if ROUTES[n] == "Z":
            @at_inner
            def _():
                swap(n).wait()
                zout_b(n).start()
        elif ROUTES[n] == "B":
            @at_inner
            def _():
                x2(n).wait()
                zout_b(n).start()
        else:
            @at_edge
            def _():
                zin(n).wait_send()
                zout(n).wait_recv()
                x2(n, True).start()

    def s6(n):
        @at_edge
        def _():
            x2(n, True).wait()
            zout_b(n).start()

    def close_chunk(n):
        kind = ROUTES[n]

        @at_edge
        def _():
            if kind == "A":
                x2(n, True).wait()
            if kind in "BZ":
                zin(n).wait_send()
                if kind == "Z":
                    zin_b(n).wait_send()
                zout(n).wait_recv()
                zout_b(n).wait_recv()
            if kind == "C":
                zout_b(n).wait_send()

        @at_inner
        def _():
            if kind == "A":
                x2(n).wait()
            zout(n).wait_send()
            store_final(n).wait()
            if kind in "BZ":
                zout_b(n).wait_send()
            if kind == "C":
                zout_b(n).wait_recv()

    def produce(ns, make):
        turn = {n: k % 2 for k, n in enumerate(n for n in ns if is_x(n))}

        def copies(n):
            slot = stage.at[turn[n]]
            return (pltpu.make_async_copy(slot.at[side(1 - xb)], x_out.at[n], store_sem.at[turn[n]]),
                    pltpu.make_async_copy(slot.at[side(xb)], own(n), keep_sem.at[turn[n]]))

        def launch(n):
            for copy in copies(n):
                copy.wait()
            x1(n).start()
        waiting = []
        for n in ns:
            if is_x(n):
                make(stage.at[turn[n]], n)
                for copy in copies(n):
                    copy.start()
            else:
                make(pz.at[z_list.index(n)], n)

                @at_edge
                def _():
                    zin(n).start()
                    zin_b(n).start()
            for m in waiting:
                launch(m)
            waiting = [n] if is_x(n) else []
        for m in waiting:
            launch(m)

    def both(ref, *rest):
        return jnp.concatenate([ref[(0, *rest)], ref[(1, *rest)]], axis=0)

    def fc_grads(ns):
        def make(to, n):
            j = n % 4
            cols = pl.ds(j * 256, 256)
            if n < 4:
                to[...] = dot(both(hid, slice(None), cols), both(dbr), TN)
            else:
                d = jnp.concatenate([both(dup, m) for m in range(4)], axis=1)
                to[...] = dot(both(sec, slice(None), cols), d, TN)
        produce(ns, make)

    def attention_grads(ns):
        def make(to, n):
            if n == 8:
                for slab in (0, 1):
                    to[slab * 128:(slab + 1) * 128, :] = dot(both(mix, slab), both(sec), TN)
            else:
                def piece(j, _):
                    cols = pl.ds(pl.multiple_of(j * 256, 256), 256)
                    to[:, cols] = dot(both(dbr, slice(None), cols), both(dup, n - 9), TN)
                    return 0
                lax.fori_loop(0, 4, piece, 0)
        produce(ns, make)

    def second_back(i):
        zero = jnp.zeros((8, width), F32)

        def body(t, sums):
            rows = rows_of(t, LN_TILE)
            attended = wide(att, i, rows) + proj_b[...]
            n, r = norm_rows(tok[i, rows, :].astype(F32) + vec(i, 0) * attended)
            dy = wide(dst, i, rows)
            dn = dy * (1.0 + vec(i, 3))
            dm = cot[i, rows, :].astype(F32) + r * (
                dn - jnp.mean(dn, axis=-1, keepdims=True) - n * jnp.mean(dn * n, axis=-1, keepdims=True))
            put_wide(dst, i, rows, dm)
            da = (dm * vec(i, 0)).astype(BF16)
            sec[i, rows, :] = da
            return (sums[0] + fold(dm * attended), sums[1] + fold(dy * n), sums[2] + fold(dy), sums[3] + fold(da.astype(F32)))
        sums = lax.fori_loop(0, n_ln, body, (zero, zero, zero, zero))
        for k, s in zip((0, 3, 5), sums[:3]):
            sm[i, k:k + 1, :] = jnp.sum(s, axis=0, keepdims=True)
        sm[2, 2:3, :] = sm[2, 2:3, :] + jnp.sum(sums[3], axis=0, keepdims=True)

        def mixed(t, _):
            rows = rows_of(t, mt)
            d = dot(sec[i, rows, :], projw[...], NT)
            dmx[0, rows, :] = d[:, :128].astype(BF16)
            dmx[1, rows, :] = d[:, 128:].astype(BF16)
            return 0
        lax.fori_loop(0, 2, mixed, 0)

    def attend_back(i, slab):
        blocks = blocks_of(128)
        fill_kv(i, slab)
        acc[...] = jnp.zeros_like(acc)

        def body(rows, keys):
            p = exps(i, slab, rows, keys)
            d = dmx[slab, rows, :]
            q = qkn[i, 0, slab, rows, :]
            ds = []
            dp_both = dot(d, kv[1, :, 0:keys, :].reshape(2 * keys, 128), NT)
            for h in (0, 1):
                dpr = dp_both[:, h * keys:(h + 1) * keys]
                ds.append((p[h] * (dpr - jnp.sum(dpr * p[h], axis=-1, keepdims=True))).astype(BF16))
            acc[0, rows, :] = dot(jnp.concatenate(ds, axis=1), kv[0, :, 0:keys, :].reshape(2 * keys, 128))
            kr = pl.ds(0, keys)
            acc[1, kr, :] += dot(
                jnp.concatenate(ds, axis=0), jnp.concatenate([q * one_head(h) for h in (0, 1)], axis=0), TN)
            acc[2, kr, :] += dot(
                jnp.concatenate([v.astype(BF16) for v in p], axis=0),
                jnp.concatenate([d * one_head(h) for h in (0, 1)], axis=0), TN)
        each_tile(body)
        es = es_row[:, slab * 128:(slab + 1) * 128]

        def close(t, sums):
            rows = rows_of(t, LN_TILE)

            def unit(c, g):
                at = c * 256 + slab * 128
                pre = qk[i, rows, at:at + 128]
                r = lax.rsqrt(head_sum(pre * pre, blocks) + EPSILON)
                u = pre * r
                gu = g * u
                return r * (g - u * head_sum(gu, blocks)), gu
            dq, gu = unit(0, acc[0, rows, :] * es)
            dk, _g = unit(1, acc[1, rows, :])
            dq, dk, dv = dq.astype(BF16), dk.astype(BF16), acc[2, rows, :].astype(BF16)
            to = pl.ds(slab * 128, 128)
            dup[i, 0, rows, to] = dq
            dup[i, 1, rows, to] = dk
            dup[i, 2, rows, to] = dv
            return sums[0] + fold(dq.astype(F32)), sums[1] + fold(dv.astype(F32)), sums[2] + fold(gu)
        zero = jnp.zeros((8, 128), F32)
        sums = lax.fori_loop(0, n_ln, close, (zero, zero, zero))
        for k in range(3):
            lanes[k, slab] = lanes[k, slab] + sums[k]

    def first_grad(i):
        def body(t, _):
            rows = rows_of(t, mt)
            for h in (0, 1):
                total = None
                for c in range(3):
                    o = dot(dup[i, c, rows, :], qkvw[c, h * half:(h + 1) * half, :], NT)
                    total = o if total is None else total + o
                att[i, h, rows, :] = total
            return 0
        lax.fori_loop(0, 2, body, 0)

    def left(k):
        return pltpu.make_async_copy(raw, (tg_hbm, out_hbm)[k // 2].at[k % 2], out_sem.at[k])

    def leave(buf, i, to, k):
        if k > 0:
            left(k - 1).wait()

        def body(t, _):
            rows = rows_of(t, 16)
            raw[rows, :] = buf[i, rows, :]
            return 0
        lax.fori_loop(0, slots // 16, body, 0)
        whole = slots // 16 * 16
        raw[whole:slots, :] = buf[i, whole:whole + 16, :].astype(F32)[:slots - whole].astype(BF16)
        left(k).start()

    def first_back(i):
        zero = jnp.zeros((8, width), F32)

        def body(t, sums):
            rows = rows_of(t, LN_TILE)
            n, r = norm_rows(tok[i, rows, :].astype(F32))
            dy = wide(att, i, rows)
            dn = dy * (1.0 + vec(i, 2))
            g = wide(dst, i, rows) + r * (
                dn - jnp.mean(dn, axis=-1, keepdims=True) - n * jnp.mean(dn * n, axis=-1, keepdims=True))
            dbr[i, rows, :] = g.astype(BF16)
            return sums[0] + fold(dy * n), sums[1] + fold(dy)
        sums = lax.fori_loop(0, n_ln, body, (zero, zero))
        for k, s in zip((2, 4), sums):
            sm[i, k:k + 1, :] = jnp.sum(s, axis=0, keepdims=True)
        leave(dbr, i, tg_hbm, i)

    def branch(i):
        def body(t, _):
            rows = rows_of(t, mt)
            for h in (0, 1):
                dst[i, h, rows, :] = dot(hid[i, rows, :], fc2w[:, h * half:(h + 1) * half])
            return 0
        lax.fori_loop(0, 2, body, 0)

        def sums_of(t, sums):
            rows = rows_of(t, LN_TILE)
            g = cot[i, rows, :].astype(F32)
            return sums[0] + fold(g * wide(dst, i, rows)), sums[1] + fold(g)
        zero = jnp.zeros((8, width), F32)
        sums = lax.fori_loop(0, n_ln, sums_of, (zero, zero))
        g2r[me, i:i + 1, :] = jnp.sum(sums[0], axis=0, keepdims=True)
        sm[i, 1:2, :] = fc2_b[...] * jnp.sum(sums[1], axis=0, keepdims=True)

    def block_end(i):
        def body(t, _):
            rows = rows_of(t, LN_TILE)
            middle = tok[i, rows, :].astype(F32) + vec(i, 0) * (wide(att, i, rows) + proj_b[...])
            cot[i, rows, :] = (middle + vec(i, 1) * (wide(dst, i, rows) + fc2_b[...])).astype(BF16)
            return 0
        lax.fori_loop(0, n_ln, body, 0)
        leave(cot, i, out_hbm, 2 + i)

    def every_copy(to, source):
        return pltpu.make_async_remote_copy(
            src_ref=sm, dst_ref=every.at[source], send_sem=ev_s.at[to], recv_sem=ev_r.at[source],
            device_id={"dp": to}, device_id_type=MESH)

    def every_start():
        pltpu.make_async_copy(sm, every.at[dp], out_sem.at[4]).start()

        def body(step, _):
            every_copy(lax.rem(dp + step, n_dp), dp).start()
            return 0
        lax.fori_loop(1, n_dp, body, 0)

    def every_finish():
        pltpu.make_async_copy(sm, every.at[dp], out_sem.at[4]).wait()

        def body(step, _):
            every_copy(lax.rem(dp + step, n_dp), dp).wait_send()
            source = lax.rem(dp + n_dp - step, n_dp)
            every_copy(source, source).wait_recv()
            return 0
        lax.fori_loop(1, n_dp, body, 0)

    def rs_both(buf, i, k):
        rs_copy(buf, i, k).start()
        rs_finish(buf, i, k)

    def forward(i):
        first_norm(i, i == 0)
        if i == 0:
            loads["qkvw"].wait()
        project(i)
        attend(i)
        if i == 0:
            loads["projw"].wait()
        attend_out(i)

    def close_sums():
        sent = share(g2r, g2_s, g2_r)
        for copy in sent:
            copy.wait()
        total = (g2r[0] + g2r[1]) + (g2r[2] + g2r[3])
        for i in (0, 1):
            sm[i, 1:2, :] = sm[i, 1:2, :] + total[i:i + 1, :]
        for j in range(4):
            sm[2, 1:2, j * 256:(j + 1) * 256] = jnp.sum(fb1[j], axis=0, keepdims=True)
        for k in range(3):
            for slab in (0, 1):
                at = k * 256 + slab * 128
                sm[2, 3:4, at:at + 128] = jnp.sum(lanes[k, slab], axis=0, keepdims=True)
        every_start()

    def spill_out(i):
        return pltpu.make_async_copy(att.at[i], spill.at[i], spill_sem.at[i])

    def spill_back(i):
        return pltpu.make_async_copy(spill.at[i], att.at[i], spill_sem.at[2 + i])

    def ag(buf, i, k):
        ag_copy(buf, i, k).start()
        ag_copy(buf, i, k).wait()

    sm[...] = jnp.zeros_like(sm)
    fb1[...] = jnp.zeros_like(fb1)
    lanes[...] = jnp.zeros_like(lanes)
    g2r[...] = jnp.zeros_like(g2r)
    kv[...] = jnp.zeros_like(kv)
    for i in (0, 1):
        sm[i, 6:7, :] = jnp.zeros((1, width), F32) + labels[i].astype(F32)
    unpack(tok_hbm, 1, tok, (cot_hbm, 0))
    forward(0)
    rs_both(att, 0, ATT)
    y_start(att, 0, ATT)
    forward(1)
    rs_both(att, 1, ATT)
    y_start(att, 1, ATT)
    unpack(cot_hbm, 0, cot, (cot_hbm, 1))
    unpack(cot_hbm, 1, cot)
    for name in ("fc1w", "fc2w"):
        loads[name].wait()
    y_finish(att, 0, ATT)
    ag(att, 0, ATT)
    mlp(0)
    rs_both(dst, 0, DS)
    y_start(dst, 0, DS)
    y_finish(att, 1, ATT)
    ag(att, 1, ATT)
    mlp(1)
    rs_copy(dst, 1, DS).start()
    fc_grads((3, 4, 5,))
    rs_finish(dst, 1, DS)
    y_start(dst, 1, DS)
    fc_grads((2, 6, 0, 1,))
    serve((2, 3))
    serve((2, 4))
    fc_grads((7,))
    y_finish(dst, 0, DS)
    ag(dst, 0, DS)
    second_back(0)
    spill_out(0).start()
    serve((2, 5))
    attend_back(0, 0)
    serve((3, 4))
    attend_back(0, 1)
    serve((2, 2))
    serve((3, 5), (3, 3))
    serve((4, 4))
    spill_out(0).wait()
    first_grad(0)
    rs_both(att, 0, DF)
    y_start(att, 0, DF)
    serve((2, 6))
    serve((3, 2))
    serve((4, 5))
    y_finish(dst, 1, DS)
    ag(dst, 1, DS)
    second_back(1)
    spill_out(1).start()
    serve((3, 6), (2, 0))
    serve((4, 2))
    attend_back(1, 0)
    serve((3, 0))
    serve((4, 6), (2, 1))
    attend_back(1, 1)
    serve((3, 1))
    serve((4, 0))
    s5(5)
    spill_out(1).wait()
    first_grad(1)
    s5(4)
    serve((2, 7))
    rs_both(att, 1, DF)
    serve((3, 7), (4, 3))
    y_start(att, 1, DF)
    first_norm(0)
    first_norm(1)
    attention_grads((8, 10, 9,))
    serve((4, 1))
    attention_grads((11,))
    y_finish(att, 0, DF)
    ag(att, 0, DF)
    first_back(0)
    spill_back(0).start()
    s5(0)
    serve((4, 7))
    branch(0)
    s5(6)
    serve((2, 11))
    rs_both(dst, 0, BR)
    serve((2, 8))
    y_start(dst, 0, BR)
    y_finish(att, 1, DF)
    s5(3)
    ag(att, 1, DF)
    serve((3, 8))
    first_back(1)
    spill_back(1).start()
    branch(1)
    serve((3, 11))
    rs_both(dst, 1, BR)
    serve((2, 10), (3, 10))
    s5(2)
    serve((4, 8))
    s5(7)
    s5(1)
    serve((2, 9))
    y_start(dst, 1, BR)
    s6(5)
    serve((3, 9))
    serve((4, 10))
    serve((4, 9))
    close_sums()
    serve((4, 11))
    s6(0)
    y_finish(dst, 0, BR)
    s5(8)
    ag(dst, 0, BR)
    spill_back(0).wait()
    block_end(0)
    y_finish(dst, 1, BR)
    s5(11)
    s5(10)
    s6(8)
    ag(dst, 1, BR)
    s5(9)
    spill_back(1).wait()
    block_end(1)
    every_finish()
    for n in (4, 6, 2, 3, 5, 0, 1, 7, 10, 8, 9, 11):
        close_chunk(n)
    left(3).wait()


def run_block(n_dp, class_table, ada_b, ada_w, tok, cot, stops, labels, log_scale, qkvw, projw, fc1w, fc2w, qv_b, proj_b, fc1_b, fc2_b):
    items, slots, width = tok.shape
    padded = -(-slots // LN_TILE) * LN_TILE
    x_count = sum(r != "Z" for r in ROUTES)
    half = width // 2
    hidden = fc1w.shape[1]
    n_chunks = 12
    n_rest = max(1, (n_dp // 8).bit_length() - 1)
    hbm = pl.BlockSpec(memory_space=pl.ANY)
    vmem = pl.BlockSpec(memory_space=pltpu.VMEM)
    smem = pl.BlockSpec(memory_space=pltpu.SMEM)
    wide_b = (items, padded, width)
    wide_f = (items, 2, padded, half)
    dma = pltpu.SemaphoreType.DMA
    return pl.pallas_call(
        functools.partial(block_kernel, slots, n_dp),
        out_shape=(
            jax.ShapeDtypeStruct(tok.shape, BF16), jax.ShapeDtypeStruct(tok.shape, BF16),
            jax.ShapeDtypeStruct(fc1w.shape, F32), jax.ShapeDtypeStruct(fc2w.shape, F32),
            jax.ShapeDtypeStruct(projw.shape, F32), jax.ShapeDtypeStruct(qkvw.shape, F32),
            jax.ShapeDtypeStruct((n_dp, 3, 8, width), F32),
            jax.ShapeDtypeStruct((n_chunks, 128, width), F32), jax.ShapeDtypeStruct((n_chunks, 128, width), F32),
            jax.ShapeDtypeStruct((n_chunks, 256, width), F32), jax.ShapeDtypeStruct((n_chunks, 128, width), F32),
            jax.ShapeDtypeStruct((n_rest, n_chunks, 128, width), F32), jax.ShapeDtypeStruct(wide_f, F32),
        ),
        in_specs=[hbm, vmem, hbm, hbm, hbm, smem, smem, smem, hbm, hbm, hbm, hbm, vmem, vmem, vmem, vmem],
        out_specs=(hbm,) * 13,
        scratch_shapes=[
            *[pltpu.VMEM(wide_b, BF16) for _ in range(4)],
            pltpu.VMEM((items, padded, hidden), BF16), pltpu.VMEM((items, hidden // 256, padded, 256), BF16),
            *[pltpu.VMEM(wide_f, F32) for _ in range(2)],
            pltpu.VMEM((items, padded, half), F32),
            pltpu.VMEM((items, 3, 2, padded, 128), BF16),
            pltpu.VMEM((items, 2, padded, 128), BF16),
            pltpu.VMEM((2, padded, 128), BF16),
            pltpu.VMEM((2, 2, 768, 128), BF16),
            pltpu.VMEM((3, 768, 128), F32),
            pltpu.VMEM((items, slots, half), F32),
            pltpu.VMEM((items, slots, half), F32),
            pltpu.VMEM(qkvw.shape, BF16), pltpu.VMEM(projw.shape, BF16),
            pltpu.VMEM(fc1w.shape, BF16), pltpu.VMEM(fc2w.shape, BF16),
            pltpu.VMEM((slots, width), BF16), pltpu.VMEM(class_table.shape, BF16), pltpu.VMEM((1, qkvw.shape[2]), F32),
            pltpu.VMEM((max(1, x_count), 128, width), F32), pltpu.VMEM((max(1, n_chunks - x_count), 256, width), F32),
            pltpu.VMEM((2, 256, width), F32),
            pltpu.VMEM((4, items, 8, width), F32), pltpu.VMEM((items, 8, width), F32),
            pltpu.VMEM((4, 8, width), F32),
            pltpu.VMEM((4, 8, 256), F32), pltpu.VMEM((3, 2, 8, 128), F32), pltpu.VMEM((3, 8, width), F32),
            dma((11,)), dma, dma((5,)), dma((5,)), dma((2,)), dma((2,)), dma((n_chunks, 4)), dma((4,)), pltpu.SemaphoreType.REGULAR((2,)),
            dma((3,)), dma((3,)), dma((3,)), dma((3,)),
            *[dma((8,)) for _ in range(6)],
            *[dma((n_chunks,)) for _ in range(8)], *[dma((n_chunks, 4)) for _ in range(6)],
            dma((n_rest, n_chunks)), dma((n_rest, n_chunks)), dma((n_dp,)), dma((n_dp,)),
        ],
        compiler_params=pltpu.CompilerParams(
            collective_id=0, has_side_effects=True, vmem_limit_bytes=62 * 2**20),
        name="block",
    )(class_table, ada_b, ada_w, tok, cot, stops, labels, log_scale, qkvw, projw, fc1w, fc2w, qv_b, proj_b, fc1_b, fc2_b)


def tail_kernel(
    every_hbm, table_hbm, ada_hbm, g1_in, g2_in, gp_in, gq_in, out_in, tg_in,
    table_grad, ada_grad, ada_bias, qv_bias, head_scale, proj_bias, fc1_bias, fc2_bias, g1, g2, gp, gq, out, tg,
    every, table, ada, part, *room_and_sems,
):
    n_dp, width = every.shape[0], every.shape[3]
    rows = 2 * n_dp
    rooms, (sem, part_sem, in_sem, copy_sem) = room_and_sems[:-4], room_and_sems[-4:]
    moved = ((g1_in, g1), (g2_in, g2), (gq_in, gq), (out_in, out), (tg_in, tg), (gp_in, gp))
    fetches = [pltpu.make_async_copy(a, room, in_sem.at[k]) for k, ((a, _), room) in enumerate(zip(moved, rooms))]
    copies = [pltpu.make_async_copy(room, b, copy_sem.at[k]) for k, ((_, b), room) in enumerate(zip(moved, rooms))]

    def move(k):
        fetches[k].wait()
        copies[k].start()
    loads = [pltpu.make_async_copy(a, b, sem.at[k])
             for k, (a, b) in enumerate(((every_hbm, every), (table_hbm, table), (ada_hbm, ada)))]
    for copy in (*loads, *fetches):
        copy.start()
    loads[0].wait()
    total = every[0, 2]
    for d in range(1, n_dp):
        total = total + every[d, 2]
    fc2_bias[...] = total[0:1]
    fc1_bias[...] = total[1:2]
    proj_bias[...] = total[2:3]
    wide = qv_bias.shape[1]
    qv_bias[0:1, :] = total[3:4, 0:wide]
    qv_bias[1:2, :] = total[3:4, wide:2 * wide]
    lanes = total[3:4, 2 * wide:3 * wide]
    head_of = lax.broadcasted_iota(jnp.int32, lanes.shape, 1) // 64
    spot = lax.broadcasted_iota(jnp.int32, head_scale.shape, 1)
    heads = jnp.zeros(head_scale.shape, F32)
    for h in range(head_scale.shape[1]):
        heads = jnp.where(spot == h, jnp.sum(jnp.where(head_of == h, lanes, 0.0), axis=1, keepdims=True), heads)
    head_scale[...] = heads
    move(0)
    move(1)

    def gathered(k):
        return jnp.concatenate([every[d, i, k:k + 1, :] for d in range(n_dp) for i in (0, 1)], axis=0)
    label = gathered(6)[:, 0:1]
    classes = table.shape[0]
    hot = jnp.where(lax.broadcasted_iota(jnp.int32, (rows, classes), 1).astype(F32) == label, 1.0, 0.0)
    loads[1].wait()
    local = dot(hot.astype(BF16), table[...])
    gate = 1.0 / (1.0 + jnp.exp(-local))
    lifted = (local * gate).astype(BF16)
    move(2)
    move(3)
    loads[2].wait()
    lifted_grad = jnp.zeros(local.shape, F32)

    def out_copy(k):
        return pltpu.make_async_copy(part.at[k % 2], ada_grad.at[:, pl.ds(k * width, width)], part_sem.at[k % 2])
    for k in range(6):
        low = gathered(k).astype(BF16)
        ada_bias[:, k * width:(k + 1) * width] = jnp.sum(low.astype(F32), axis=0, keepdims=True)
        lifted_grad = lifted_grad + dot(low, ada[:, k * width:(k + 1) * width], NT)
        if k >= 2:
            out_copy(k - 2).wait()
        part[k % 2] = dot(lifted, low, TN)
        out_copy(k).start()
        if k in (1, 3):
            move(4 + k // 2)
    class_grad = lifted_grad * (gate * (1.0 + local * (1.0 - gate)))
    table_grad[...] = lax.dot_general(hot, class_grad, TN, precision=lax.Precision.HIGHEST, preferred_element_type=F32)
    out_copy(4).wait()
    out_copy(5).wait()
    for copy in copies:
        copy.wait()


def run_tail(heads, every, class_table, ada_weight, g1, g2, gp, gq, out, tg):
    classes, wide = class_table.shape
    width = every.shape[3]
    hbm = pl.BlockSpec(memory_space=pl.ANY)
    vmem = pl.BlockSpec(memory_space=pltpu.VMEM)
    dma = pltpu.SemaphoreType.DMA
    shape = lambda *dims: jax.ShapeDtypeStruct(dims, F32)
    return pl.pallas_call(
        tail_kernel,
        out_shape=(
            shape(classes, wide), shape(*ada_weight.shape), shape(1, ada_weight.shape[1]), shape(2, wide), shape(1, heads),
            shape(1, width), shape(1, width), shape(1, width), shape(*g1.shape), shape(*g2.shape), shape(*gp.shape), shape(*gq.shape),
            jax.ShapeDtypeStruct(out.shape, out.dtype), jax.ShapeDtypeStruct(tg.shape, tg.dtype)),
        in_specs=[hbm] * 9,
        out_specs=(vmem, hbm, vmem, vmem, vmem, vmem, vmem, vmem, hbm, hbm, hbm, hbm, hbm, hbm),
        scratch_shapes=[
            pltpu.VMEM(every.shape, F32), pltpu.VMEM(class_table.shape, BF16), pltpu.VMEM(ada_weight.shape, BF16),
            pltpu.VMEM((2, wide, width), F32),
            *[pltpu.VMEM(a.shape, a.dtype) for a in (g1, g2, gq, out, tg, gp)],
            dma((3,)), dma((2,)), dma((6,)), dma((6,)),
        ],
        compiler_params=pltpu.CompilerParams(vmem_limit_bytes=60 * 2**20),
        name="tail",
    )(every, class_table, ada_weight, g1, g2, gp, gq, out, tg)


def shards(
    n_dp, tokens, cotangent, stop_scales, labels, class_table, ada_weight, ada_bias, qkv_weight, qv_bias, log_scale,
    proj_weight, proj_bias, fc1_weight, fc1_bias, fc2_weight, fc2_bias,
):
    items, slots, width = tokens.shape
    heads = log_scale.shape[0]
    out, tg, g1, g2, gp, gq, every, *_ = run_block(
        n_dp, class_table, ada_bias[None, :], ada_weight, tokens, cotangent, stop_scales, labels, log_scale,
        jnp.transpose(qkv_weight, (1, 0, 2)), proj_weight, fc1_weight, fc2_weight,
        qv_bias, proj_bias[None, :], fc1_bias.reshape(-1, 1, 256), fc2_bias[None, :])
    table_grad, ada_grad, ada_bias_grad, qv_grad, scale_grad, proj_b, fc1_b, fc2_b, g1, g2, gp, gq, out, tg = run_tail(
        heads, every, class_table, ada_weight, g1, g2, gp, gq, out, tg)
    return (
        out, tg, table_grad, ada_grad, ada_bias_grad[0], jnp.transpose(gq, (1, 0, 2)), qv_grad, scale_grad[0],
        gp, proj_b[0], g1, fc1_b[0], g2, fc2_b[0],
    )


def solution(mesh):
    return jax.shard_map(
        functools.partial(shards, mesh.shape["dp"]),
        mesh=mesh,
        in_specs=(
            P("dp", None, None), P("dp", None, None), P("dp"), P("dp"), P(None, "mp"), P("mp", None), P(),
            P(None, None, "mp"), P(None, "mp"), P("mp"), P("mp", None), P(), P(None, "mp"), P("mp"), P("mp", None), P(),
        ),
        out_specs=(
            P("dp", None, None), P("dp", None, None), P(None, "mp"), P("mp", None), P(), P(None, None, "mp"), P(None, "mp"),
            P("mp"), P("mp", None), P(), P(None, "mp"), P("mp"), P("mp", None), P(),
        ),
        check_vma=False,
    )
```

```python
import functools

import jax
import jax.numpy as jnp
import numpy as np
from jax import lax
from jax.experimental import pallas as pl
from jax.experimental.pallas import tpu as pltpu
from jax.sharding import PartitionSpec as P

SIDE_LIST = (1, 2, 3, 4, 5, 6, 8, 10, 13, 16)
EPSILON = 1e-06
MESH = pl.DeviceIdType.MESH
F32, BF16 = jnp.float32, jnp.bfloat16
GELU_C = 0.7978845608028654
GELU_A = 0.044715
LN_TILE = 176
NT = (((1,), (1,)), ((), ()))
TN = (((0,), (0,)), ((), ()))
NN = (((1,), (0,)), ((), ()))
ATT, DS, DF, BR = 0, 2, 4, 6
ROUTES = "CAAZACBACAAZ"


def dot(a, b, dims=NN):
    return lax.dot_general(a, b, dims, preferred_element_type=F32)


def norm_rows(v):
    center = v - jnp.mean(v, axis=-1, keepdims=True)
    scale = lax.rsqrt(jnp.mean(center * center, axis=-1, keepdims=True) + EPSILON)
    return center * scale, scale


def fold(v):
    return jnp.sum(v.reshape(v.shape[0] // 8, 8, v.shape[1]), axis=0)


def head_sum(v, blocks):
    high = v.astype(BF16)
    rest = (v - high.astype(F32)).astype(BF16)
    return dot(high, blocks) + dot(rest, blocks)


def block_kernel(
    slots, n_dp,
    table_hbm, ada_b, ada_hbm, tok_hbm, cot_hbm, stops, labels, log_scale,
    qkvw_hbm, projw_hbm, fc1w_hbm, fc2w_hbm,
    qv_b, proj_b, fc1_b, fc2_b,
    out_hbm, tg_hbm, g1_out, g2_out, gp_out, gq_out, every, x_out, x_in, z_in, mid_in, rest_in, spill,
    tok, cot, sec, dbr, hid, dup,
    att, dst,
    qk, qkn, mix, dmx, kv, acc,
    rs_buf, y_buf,
    qkvw, projw, fc1w, fc2w,
    raw, table, es_row, px, pz, stage, modr, mod, g2r, fb1, lanes, sm,
    in_sem, raw_sem, out_sem, load_sem, store_sem, keep_sem, final_sem, spill_sem, y_free,
    mod_s, mod_r, g2_s, g2_r, rs_s, rs_r, y_s, y_r, ag_s, ag_r,
    x1_s, x1_r, zi_s, zi_r, mi_s, mi_r, zb_s, zb_r, zo_s, zo_r, x2_s, x2_r, zc_s, zc_r, re_s, re_r, ev_s, ev_r,
):
    items, padded, width = tok.shape
    half = width // 2
    me = lax.axis_index("mp")
    dp = lax.axis_index("dp")
    xb = lax.rem(dp, 2)
    z = lax.rem(dp // 2, 4)
    zh = z // 2
    inner = jnp.logical_or(z == 1, z == 2)
    edge = jnp.logical_or(z == 0, z == 3)
    x_mate = dp + 1 - 2 * xb
    z_mate = dp + 2 - 4 * lax.rem(z, 2)
    mid_mate = jnp.where(z == 1, dp + 2, jnp.where(z == 2, dp - 2, dp))
    n_rest = rest_in.shape[0] if n_dp > 8 else 0
    rest_mates = [dp + (8 << k) * (1 - 2 * lax.rem(dp // (8 << k), 2)) for k in range(n_rest)]
    core = lax.rem(me, 2)
    core_mate = me + 1 - 2 * core
    y_mate = lax.rem(me + 2, 4)
    n_ln = padded // LN_TILE
    mt = padded // 2

    def rows_of(t, n):
        return pl.ds(pl.multiple_of(t * n, n), n)

    def wide(buf, i, rows):
        return jnp.concatenate([buf[i, 0, rows, :], buf[i, 1, rows, :]], axis=1)

    def put_wide(buf, i, rows, v):
        buf[i, 0, rows, :] = v[:, :half]
        buf[i, 1, rows, :] = v[:, half:]

    def raw_copy(src, i):
        return pltpu.make_async_copy(src.at[i], raw, raw_sem)

    def unpack(src, i, to, then=None):
        raw_copy(src, i).wait()
        whole = slots // 16 * 16

        def body(t, _):
            rows = rows_of(t, 16)
            to[i, rows, :] = raw[rows, :]
            return 0
        lax.fori_loop(0, slots // 16, body, 0)
        tail = raw[whole:slots, :].astype(F32)
        rest = jnp.concatenate([tail, jnp.zeros((padded - slots, width), F32)], axis=0)
        to[i, whole:padded, :] = rest.astype(BF16)
        if then is not None:
            raw_copy(*then).start()

    raw_copy(tok_hbm, 0).start()
    rows_ada = ada_hbm.shape[0]
    ada_room = [buf.at[i, pl.ds(k * rows_ada, rows_ada)] for buf, i, k in (
        (hid, 0, 0), (hid, 0, 1), (hid, 1, 0), (hid, 1, 1), (sec, 0, 0), (sec, 1, 0))]
    loads = {}
    for k, (name, src, to) in enumerate((
        ("table", table_hbm, table),
        *[(f"ada{c}", ada_hbm.at[:, pl.ds(c * width, width)], ada_room[c]) for c in range(6)],
        ("qkvw", qkvw_hbm, qkvw), ("projw", projw_hbm, projw), ("fc1w", fc1w_hbm, fc1w), ("fc2w", fc2w_hbm, fc2w),
    )):
        loads[name] = pltpu.make_async_copy(src, to, in_sem.at[k])
        loads[name].start()

    barrier = pltpu.get_barrier_semaphore()
    for step in (1, 2, 3):
        pl.semaphore_signal(barrier, inc=1, device_id={"mp": lax.rem(me + step, 4)}, device_id_type=MESH)
    def greet(step, _):
        pl.semaphore_signal(barrier, inc=1, device_id={"dp": lax.rem(dp + step, n_dp)}, device_id_type=MESH)
        return 0
    lax.fori_loop(1, n_dp, greet, 0)

    def share(buf, send, recv):
        copies = []
        for step in (1, 2, 3):
            copies.append(pltpu.make_async_remote_copy(
                src_ref=buf.at[me], dst_ref=buf.at[me], send_sem=send.at[step - 1], recv_sem=recv.at[step - 1],
                device_id={"mp": lax.rem(me + step, 4)}, device_id_type=MESH))
        for copy in copies:
            copy.start()
        return copies

    loads["table"].wait()
    spot = (16, table.shape[0])
    item_at = lax.broadcasted_iota(jnp.int32, spot, 0)
    class_at = lax.broadcasted_iota(jnp.int32, spot, 1)
    hot = jnp.zeros(spot, F32)
    for i in range(items):
        hot = jnp.where(jnp.logical_and(item_at == i, class_at == labels[i]), 1.0, hot)
    local = dot(hot.astype(BF16), table[...])
    lifted = (local * (1.0 / (1.0 + jnp.exp(-local)))).astype(BF16)
    for c in range(6):
        loads[f"ada{c}"].wait()
        part = dot(lifted, ada_room[c][...])
        for i in range(items):
            modr[me, i, c:c + 1, :] = part[i:i + 1, :]
    for i in range(items):
        modr[me, i, 6:8, :] = jnp.zeros((2, width), F32)
    pl.semaphore_wait(barrier, 3 + n_dp - 1)
    sent = share(modr, mod_s, mod_r)
    unpack(tok_hbm, 0, tok, (tok_hbm, 1))

    def early(t, _):
        rows = rows_of(t, LN_TILE)
        n, _r = norm_rows(tok[0, rows, :].astype(F32))
        put_wide(att, 0, rows, n)
        return 0
    lax.fori_loop(0, n_ln, early, 0)
    for copy in sent:
        copy.wait()
    mod[...] = (modr[0] + modr[1]) + (modr[2] + modr[3])
    for i in range(items):
        for c in range(6):
            mod[i, c:c + 1, :] = mod[i, c:c + 1, :] + ada_b[:, c * width:(c + 1) * width]
    lane = lax.broadcasted_iota(jnp.int32, es_row.shape, 1) // 64
    scales = jnp.zeros(es_row.shape, F32)
    for h in range(es_row.shape[1] // 64):
        scales = jnp.where(lane == h, log_scale[h], scales)
    es_row[...] = jnp.exp(scales)

    def vec(i, k):
        return mod[i, k:k + 1, :]

    def rs_copy(buf, i, k):
        return pltpu.make_async_remote_copy(
            src_ref=buf.at[i, 1 - core, pl.ds(0, slots)], dst_ref=rs_buf.at[i], send_sem=rs_s.at[k + i], recv_sem=rs_r.at[k + i],
            device_id={"mp": core_mate}, device_id_type=MESH)

    def y_copy(buf, i, k):
        dst = qk.at[i, pl.ds(0, slots)] if k == BR else y_buf.at[i]
        return pltpu.make_async_remote_copy(
            src_ref=buf.at[i, core, pl.ds(0, slots)], dst_ref=dst, send_sem=y_s.at[k + i], recv_sem=y_r.at[k + i],
            device_id={"mp": y_mate}, device_id_type=MESH)

    def ag_copy(buf, i, k):
        return pltpu.make_async_remote_copy(
            src_ref=buf.at[i, core, pl.ds(0, slots)], dst_ref=buf.at[i, core, pl.ds(0, slots)],
            send_sem=ag_s.at[k + i], recv_sem=ag_r.at[k + i],
            device_id={"mp": core_mate}, device_id_type=MESH)

    add_rows = slots // 5

    def rs_finish(buf, i, k):
        rs_copy(buf, i, k).wait()

        def add(t, _):
            rows = rows_of(t, add_rows)
            buf[i, core, rows, :] = buf[i, core, rows, :] + rs_buf[i, rows, :]
            return 0
        lax.fori_loop(0, 5, add, 0)

    def y_finish(buf, i, k):
        y_copy(buf, i, k).wait()

        def add(t, _):
            rows = rows_of(t, add_rows)
            other = qk[i, rows, :] if k == BR else y_buf[i, rows, :]
            buf[i, core, rows, :] = buf[i, core, rows, :] + other
            return 0
        lax.fori_loop(0, 5, add, 0)
        if k in (ATT, DS):
            pl.semaphore_signal(y_free.at[i], inc=1, device_id={"mp": y_mate}, device_id_type=MESH)

    def y_start(buf, i, k):
        if k in (DS, DF):
            pl.semaphore_wait(y_free.at[i], 1)
        y_copy(buf, i, k).start()

    def blocks_of(n):
        a = lax.broadcasted_iota(jnp.int32, (n, n), 0) // 64
        b = lax.broadcasted_iota(jnp.int32, (n, n), 1) // 64
        return jnp.where(a == b, 1.0, 0.0).astype(BF16)

    ends = np.cumsum(np.array([s * s for s in SIDE_LIST]))
    tiles = ((0, 240, 1, 256), (240, 176, 1, 512), (416, 96, 3, 768))

    def keep_of(i, rows, keys):
        live = jnp.int32(0)
        for s in range(len(SIDE_LIST)):
            live = jnp.where(stops[i] == s + 1, int(ends[s]), live)
        n = rows.size
        at = rows.start + lax.broadcasted_iota(jnp.int32, (n, 1), 0)
        bound = jnp.full((n, 1), int(ends[0]), jnp.int32)
        for s in range(1, len(SIDE_LIST)):
            bound = jnp.where(at >= int(ends[s - 1]), int(ends[s]), bound)
        bound = jnp.minimum(bound, live)
        return lax.broadcasted_iota(jnp.int32, (n, keys), 1) < bound

    def one_head(h):
        lane = lax.broadcasted_iota(jnp.int32, (1, 128), 1) // 64
        return jnp.where(lane == h, 1.0, 0.0).astype(BF16)

    def fill_kv(i, slab):
        for c in (0, 1):
            for h in (0, 1):
                kv[c, h, 0:padded, :] = qkn[i, 1 + c, slab] * one_head(h)

    def exps(i, slab, rows, keys):
        keep = keep_of(i, rows, keys)
        s = dot(qkn[i, 0, slab, rows, :], kv[0, :, 0:keys, :].reshape(2 * keys, 128), NT)
        parts = []
        for h in (0, 1):
            e = jnp.where(keep, jnp.exp(s[:, h * keys:(h + 1) * keys]), 0.0)
            parts.append(e * (1.0 / jnp.sum(e, axis=-1, keepdims=True)))
        return parts

    def each_tile(body):
        for first_row, n, steps, keys in tiles:
            if steps == 1:
                body(pl.ds(first_row, n), keys)
            else:
                def step(t, _, first_row=first_row, n=n, keys=keys):
                    body(pl.ds(pl.multiple_of(first_row + t * n, 16), n), keys)
                    return 0
                lax.fori_loop(0, steps, step, 0)

    def first_norm(i, ready=False):
        def body(t, _):
            rows = rows_of(t, LN_TILE)
            n = wide(att, i, rows) if ready else norm_rows(tok[i, rows, :].astype(F32))[0]
            dbr[i, rows, :] = (n * (1.0 + vec(i, 2)) + vec(i, 4)).astype(BF16)
            return 0
        lax.fori_loop(0, n_ln, body, 0)

    def project(i):
        blocks = blocks_of(256)

        def body(t, _):
            rows = rows_of(t, mt)
            f = dbr[i, rows, :]
            q = dot(f, qkvw[0]) + qv_b[0:1, :]
            qk[i, rows, 0:256] = q
            u = q * lax.rsqrt(head_sum(q * q, blocks) + EPSILON) * es_row[...]
            qkn[i, 0, 0, rows, :] = u[:, :128].astype(BF16)
            qkn[i, 0, 1, rows, :] = u[:, 128:].astype(BF16)
            k = dot(f, qkvw[1])
            qk[i, rows, 256:512] = k
            u = k * lax.rsqrt(head_sum(k * k, blocks) + EPSILON)
            qkn[i, 1, 0, rows, :] = u[:, :128].astype(BF16)
            qkn[i, 1, 1, rows, :] = u[:, 128:].astype(BF16)
            v = dot(f, qkvw[2]) + qv_b[1:2, :]
            qkn[i, 2, 0, rows, :] = v[:, :128].astype(BF16)
            qkn[i, 2, 1, rows, :] = v[:, 128:].astype(BF16)
            return 0
        lax.fori_loop(0, 2, body, 0)

    def attend(i):
        def slab_body(slab, _):
            fill_kv(i, slab)

            def body(rows, keys):
                p = jnp.concatenate([v.astype(BF16) for v in exps(i, slab, rows, keys)], axis=1)
                o = dot(p, kv[1, :, 0:keys, :].reshape(2 * keys, 128))
                mix[i, slab, rows, :] = o.astype(BF16)
            each_tile(body)
            return 0
        lax.fori_loop(0, 2, slab_body, 0)

    def attend_out(i):
        def body(t, _):
            rows = rows_of(t, mt)
            m = jnp.concatenate([mix[i, 0, rows, :], mix[i, 1, rows, :]], axis=1)
            for h in (0, 1):
                att[i, h, rows, :] = dot(m, projw[:, h * half:(h + 1) * half])
            return 0
        lax.fori_loop(0, 2, body, 0)

    def mlp_norm(i):
        def body(t, total):
            rows = rows_of(t, LN_TILE)
            middle = tok[i, rows, :].astype(F32) + vec(i, 0) * (wide(att, i, rows) + proj_b[...])
            n, _r = norm_rows(middle)
            sec[i, rows, :] = (n * (1.0 + vec(i, 3)) + vec(i, 5)).astype(BF16)
            d = (cot[i, rows, :].astype(F32) * vec(i, 1)).astype(BF16)
            dbr[i, rows, :] = d
            return total + fold(d.astype(F32))
        total = lax.fori_loop(0, n_ln, body, jnp.zeros((8, width), F32))
        sm[2, 0:1, :] = sm[2, 0:1, :] + jnp.sum(total, axis=0, keepdims=True)

    def mlp_column(i, j):
        cols = pl.ds(pl.multiple_of(j * 256, 256), 256)

        def body(t, _):
            rows = rows_of(t, mt)
            u = dot(sec[i, rows, :], fc1w[:, cols]) + fc1_b[j]
            dh = dot(dbr[i, rows, :], fc2w[cols, :], NT)
            square = u * u
            th = jnp.tanh(u * (GELU_C + (GELU_C * GELU_A) * square))
            gate = 0.5 + 0.5 * th
            out = u * gate
            hid[i, rows, cols] = out.astype(BF16)
            slope = gate + out * (1.0 - th) * (GELU_C + (3.0 * GELU_C * GELU_A) * square)
            d = (dh * slope).astype(BF16)
            dup[i, j, rows, :] = d
            fb1[j] = fb1[j] + fold(d.astype(F32))
            return 0
        lax.fori_loop(0, 2, body, 0)

    def mlp_back(i):
        def back(t, _):
            rows = rows_of(t, mt)
            d = jnp.concatenate([dup[i, j, rows, :] for j in range(dup.shape[1])], axis=1)
            for h in (0, 1):
                dst[i, h, rows, :] = dot(d, fc1w[h * half:(h + 1) * half, :], NT)
            return 0
        lax.fori_loop(0, 2, back, 0)

    def mlp_columns(i):
        def column(j, _):
            mlp_column(i, j)
            return 0
        lax.fori_loop(0, dup.shape[1], column, 0)

    def mlp(i):
        mlp_norm(i)
        mlp_columns(i)
        mlp_back(i)

    x_list = [n for n in range(12) if ROUTES[n] != "Z"]
    z_list = [n for n in range(12) if ROUTES[n] == "Z"]

    def is_x(n):
        return ROUTES[n] != "Z"

    def side(h):
        return pl.ds(pl.multiple_of(h * 128, 128), 128)

    def own(n):
        return px.at[x_list.index(n)] if is_x(n) else pz.at[z_list.index(n), side(zh)]

    def final_of(n, h):
        if n < 8:
            return [(g2_out if n < 4 else g1_out).at[pl.ds(pl.multiple_of((n % 4) * 256 + h * 128, 128), 128)]]
        if n == 8:
            return [gp_out.at[side(h)]]
        return [gq_out.at[n - 9, pl.ds(pl.multiple_of(j * 256 + h * 128, 128), 128)] for j in range(4)]

    def in_pieces(n, ref):
        return [ref] if n < 9 else [ref.at[:, pl.ds(j * 256, 256)] for j in range(4)]

    def my_half(n):
        return xb if is_x(n) else zh

    class Pieces:
        def __init__(self, n, srcs, tos, send, recv, mate):
            self.parts = lambda: [
                to_dp(a, b, send.at[n, j], recv.at[n, j], mate) for j, (a, b) in enumerate(zip(srcs, tos))]

        def start(self):
            for part in self.parts():
                part.start()

        def wait_send(self):
            for part in self.parts():
                part.wait_send()

        def wait_recv(self):
            for part in self.parts():
                part.wait_recv()

        def wait(self):
            self.wait_send()
            self.wait_recv()

    def to_dp(src, to, send, recv, mate):
        return pltpu.make_async_remote_copy(
            src_ref=src, dst_ref=to, send_sem=send, recv_sem=recv, device_id={"dp": mate}, device_id_type=MESH)

    def x1(n):
        return to_dp(x_out.at[n] if is_x(n) else own(n), x_in.at[n], x1_s.at[n], x1_r.at[n], x_mate)

    def zin(n):
        if is_x(n):
            return to_dp(own(n), z_in.at[n, pl.ds(0, 128)], zi_s.at[n], zi_r.at[n], z_mate)
        return to_dp(far(n), z_in.at[n, side(1 - zh)], zi_s.at[n], zi_r.at[n], z_mate)

    def far(n):
        return pz.at[z_list.index(n), side(1 - zh)]

    def zin_b(n):
        return to_dp(own(n), z_in.at[n, side(zh)], zb_s.at[n], zb_r.at[n], z_mate)

    def mid(n):
        return to_dp(own(n) if is_x(n) else far(n), mid_in.at[n], mi_s.at[n], mi_r.at[n], mid_mate)

    def zout(n):
        return Pieces(n, in_pieces(n, own(n)), final_of(n, my_half(n)), zo_s, zo_r, z_mate)

    def zout_b(n):
        views = final_of(n, 1 - my_half(n))
        return Pieces(n, views, views, zc_s, zc_r, z_mate)

    def x2(n, at_the_edge=False):
        views = final_of(n, xb)
        return Pieces(n, views if at_the_edge else in_pieces(n, own(n)), views, x2_s, x2_r, x_mate)

    def swap(n):
        return Pieces(n, in_pieces(n, own(n)), final_of(n, zh), x2_s, x2_r, mid_mate)

    class store_final:
        def __init__(self, n):
            self.parts = lambda: [
                pltpu.make_async_copy(a, b, final_sem.at[n, j])
                for j, (a, b) in enumerate(zip(in_pieces(n, own(n)), final_of(n, my_half(n))))]

        def start(self):
            for part in self.parts():
                part.start()

        def wait(self):
            for part in self.parts():
                part.wait()

    def at_edge(body):
        pl.when(edge)(body)

    def at_inner(body):
        pl.when(inner)(body)

    def accumulate(to, what):
        def add(t, _):
            rows = rows_of(t, 16)
            to[rows, :] = to[rows, :] + what[rows, :]
            return 0
        lax.fori_loop(0, 8, add, 0)

    def add_all(items):
        def slot(k):
            return stage.at[0, pl.ds((k % 2) * 128, 128)]

        def load(k):
            return pltpu.make_async_copy(items[k][1], slot(k), load_sem.at[k % 4])

        def begin(k):
            items[k][0]()
            load(k).start()
        for k in range(min(2, len(items))):
            begin(k)
        for k in range(len(items)):
            load(k).wait()
            accumulate(items[k][2], slot(k))
            items[k][3]()
            if k + 2 < len(items):
                begin(k + 2)

    def rest_sum(n):
        for k in range(n_rest):
            copy = to_dp(own(n), rest_in.at[k, n], re_s.at[k, n], re_r.at[k, n], rest_mates[k])
            copy.start()
            copy.wait()
            extra = stage.at[1, pl.ds(0, 128)]
            load = pltpu.make_async_copy(rest_in.at[k, n], extra, load_sem.at[4])
            load.start()
            load.wait()
            accumulate(own(n), extra)

    def items_of(step, n):
        if is_x(n):
            if step == 2:
                return [(lambda: x1(n).wait(), x_in.at[n], own(n), lambda: at_edge(lambda: zin(n).start()))]
            if step == 3:
                return [(lambda: zin(n).wait_recv(), z_in.at[n, pl.ds(0, 128)], own(n), lambda: mid(n).start())]

            def close():
                rest_sum(n)
                zout(n).start()
                if ROUTES[n] != "C":
                    x2(n).start()
                store_final(n).start()
            return [(lambda: mid(n).wait(), mid_in.at[n], own(n), close)]
        if step == 2:
            return [(lambda: zin(n).wait_recv(), z_in.at[n, side(1 - zh)], far(n), lambda: mid(n).start())]
        if step == 3:
            def close():
                rest_sum(n)
                x1(n).start()
            return [
                (lambda: zin_b(n).wait_recv(), z_in.at[n, side(zh)], own(n), lambda: None),
                (lambda: mid(n).wait(), mid_in.at[n], own(n), close)]

        def close():
            swap(n).start()
            zout(n).start()
            store_final(n).start()
        return [(lambda: x1(n).wait(), x_in.at[n], own(n), close)]

    def serve(*tasks):
        at_inner(lambda: add_all([item for step, n in tasks for item in items_of(step, n)]))
        outer = [item for step, n in tasks if step == 2 and is_x(n) for item in items_of(step, n)]
        if outer:
            at_edge(lambda: add_all(outer))

    def s5(n):
        if ROUTES[n] == "Z":
            @at_inner
            def _():
                swap(n).wait()
                zout_b(n).start()
        elif ROUTES[n] == "B":
            @at_inner
            def _():
                x2(n).wait()
                zout_b(n).start()
        else:
            @at_edge
            def _():
                zin(n).wait_send()
                zout(n).wait_recv()
                x2(n, True).start()

    def s6(n):
        @at_edge
        def _():
            x2(n, True).wait()
            zout_b(n).start()

    def close_chunk(n):
        kind = ROUTES[n]

        @at_edge
        def _():
            if kind == "A":
                x2(n, True).wait()
            if kind in "BZ":
                zin(n).wait_send()
                if kind == "Z":
                    zin_b(n).wait_send()
                zout(n).wait_recv()
                zout_b(n).wait_recv()
            if kind == "C":
                zout_b(n).wait_send()

        @at_inner
        def _():
            if kind == "A":
                x2(n).wait()
            zout(n).wait_send()
            store_final(n).wait()
            if kind in "BZ":
                zout_b(n).wait_send()
            if kind == "C":
                zout_b(n).wait_recv()

    def produce(ns, make):
        turn = {n: k % 2 for k, n in enumerate(n for n in ns if is_x(n))}

        def copies(n):
            slot = stage.at[turn[n]]
            return (pltpu.make_async_copy(slot.at[side(1 - xb)], x_out.at[n], store_sem.at[turn[n]]),
                    pltpu.make_async_copy(slot.at[side(xb)], own(n), keep_sem.at[turn[n]]))

        def launch(n):
            for copy in copies(n):
                copy.wait()
            x1(n).start()
        waiting = []
        for n in ns:
            if is_x(n):
                make(stage.at[turn[n]], n)
                for copy in copies(n):
                    copy.start()
            else:
                make(pz.at[z_list.index(n)], n)

                @at_edge
                def _():
                    zin(n).start()
                    zin_b(n).start()
            for m in waiting:
                launch(m)
            waiting = [n] if is_x(n) else []
        for m in waiting:
            launch(m)

    def both(ref, *rest):
        return jnp.concatenate([ref[(0, *rest)], ref[(1, *rest)]], axis=0)

    def fc_grads(ns):
        def make(to, n):
            j = n % 4
            cols = pl.ds(j * 256, 256)
            if n < 4:
                to[...] = dot(both(hid, slice(None), cols), both(dbr), TN)
            else:
                d = jnp.concatenate([both(dup, m) for m in range(4)], axis=1)
                to[...] = dot(both(sec, slice(None), cols), d, TN)
        produce(ns, make)

    def attention_grads(ns):
        def make(to, n):
            if n == 8:
                for slab in (0, 1):
                    to[slab * 128:(slab + 1) * 128, :] = dot(both(mix, slab), both(sec), TN)
            else:
                def piece(j, _):
                    cols = pl.ds(pl.multiple_of(j * 256, 256), 256)
                    to[:, cols] = dot(both(dbr, slice(None), cols), both(dup, n - 9), TN)
                    return 0
                lax.fori_loop(0, 4, piece, 0)
        produce(ns, make)

    def second_back(i):
        zero = jnp.zeros((8, width), F32)

        def body(t, sums):
            rows = rows_of(t, LN_TILE)
            attended = wide(att, i, rows) + proj_b[...]
            n, r = norm_rows(tok[i, rows, :].astype(F32) + vec(i, 0) * attended)
            dy = wide(dst, i, rows)
            dn = dy * (1.0 + vec(i, 3))
            dm = cot[i, rows, :].astype(F32) + r * (
                dn - jnp.mean(dn, axis=-1, keepdims=True) - n * jnp.mean(dn * n, axis=-1, keepdims=True))
            put_wide(dst, i, rows, dm)
            da = (dm * vec(i, 0)).astype(BF16)
            sec[i, rows, :] = da
            return (sums[0] + fold(dm * attended), sums[1] + fold(dy * n), sums[2] + fold(dy), sums[3] + fold(da.astype(F32)))
        sums = lax.fori_loop(0, n_ln, body, (zero, zero, zero, zero))
        for k, s in zip((0, 3, 5), sums[:3]):
            sm[i, k:k + 1, :] = jnp.sum(s, axis=0, keepdims=True)
        sm[2, 2:3, :] = sm[2, 2:3, :] + jnp.sum(sums[3], axis=0, keepdims=True)

        def mixed(t, _):
            rows = rows_of(t, mt)
            d = dot(sec[i, rows, :], projw[...], NT)
            dmx[0, rows, :] = d[:, :128].astype(BF16)
            dmx[1, rows, :] = d[:, 128:].astype(BF16)
            return 0
        lax.fori_loop(0, 2, mixed, 0)

    def attend_back(i, slab):
        blocks = blocks_of(128)
        fill_kv(i, slab)
        acc[...] = jnp.zeros_like(acc)

        def body(rows, keys):
            p = exps(i, slab, rows, keys)
            d = dmx[slab, rows, :]
            q = qkn[i, 0, slab, rows, :]
            ds = []
            dp_both = dot(d, kv[1, :, 0:keys, :].reshape(2 * keys, 128), NT)
            for h in (0, 1):
                dpr = dp_both[:, h * keys:(h + 1) * keys]
                ds.append((p[h] * (dpr - jnp.sum(dpr * p[h], axis=-1, keepdims=True))).astype(BF16))
            acc[0, rows, :] = dot(jnp.concatenate(ds, axis=1), kv[0, :, 0:keys, :].reshape(2 * keys, 128))
            kr = pl.ds(0, keys)
            acc[1, kr, :] += dot(
                jnp.concatenate(ds, axis=0), jnp.concatenate([q * one_head(h) for h in (0, 1)], axis=0), TN)
            acc[2, kr, :] += dot(
                jnp.concatenate([v.astype(BF16) for v in p], axis=0),
                jnp.concatenate([d * one_head(h) for h in (0, 1)], axis=0), TN)
        each_tile(body)
        es = es_row[:, slab * 128:(slab + 1) * 128]

        def close(t, sums):
            rows = rows_of(t, LN_TILE)

            def unit(c, g):
                at = c * 256 + slab * 128
                pre = qk[i, rows, at:at + 128]
                r = lax.rsqrt(head_sum(pre * pre, blocks) + EPSILON)
                u = pre * r
                gu = g * u
                return r * (g - u * head_sum(gu, blocks)), gu
            dq, gu = unit(0, acc[0, rows, :] * es)
            dk, _g = unit(1, acc[1, rows, :])
            dq, dk, dv = dq.astype(BF16), dk.astype(BF16), acc[2, rows, :].astype(BF16)
            to = pl.ds(slab * 128, 128)
            dup[i, 0, rows, to] = dq
            dup[i, 1, rows, to] = dk
            dup[i, 2, rows, to] = dv
            return sums[0] + fold(dq.astype(F32)), sums[1] + fold(dv.astype(F32)), sums[2] + fold(gu)
        zero = jnp.zeros((8, 128), F32)
        sums = lax.fori_loop(0, n_ln, close, (zero, zero, zero))
        for k in range(3):
            lanes[k, slab] = lanes[k, slab] + sums[k]

    def first_grad(i):
        def body(t, _):
            rows = rows_of(t, mt)
            for h in (0, 1):
                total = None
                for c in range(3):
                    o = dot(dup[i, c, rows, :], qkvw[c, h * half:(h + 1) * half, :], NT)
                    total = o if total is None else total + o
                att[i, h, rows, :] = total
            return 0
        lax.fori_loop(0, 2, body, 0)

    def left(k):
        return pltpu.make_async_copy(raw, (tg_hbm, out_hbm)[k // 2].at[k % 2], out_sem.at[k])

    def leave(buf, i, to, k):
        if k > 0:
            left(k - 1).wait()

        def body(t, _):
            rows = rows_of(t, 16)
            raw[rows, :] = buf[i, rows, :]
            return 0
        lax.fori_loop(0, slots // 16, body, 0)
        whole = slots // 16 * 16
        raw[whole:slots, :] = buf[i, whole:whole + 16, :].astype(F32)[:slots - whole].astype(BF16)
        left(k).start()

    def first_back(i):
        zero = jnp.zeros((8, width), F32)

        def body(t, sums):
            rows = rows_of(t, LN_TILE)
            n, r = norm_rows(tok[i, rows, :].astype(F32))
            dy = wide(att, i, rows)
            dn = dy * (1.0 + vec(i, 2))
            g = wide(dst, i, rows) + r * (
                dn - jnp.mean(dn, axis=-1, keepdims=True) - n * jnp.mean(dn * n, axis=-1, keepdims=True))
            dbr[i, rows, :] = g.astype(BF16)
            return sums[0] + fold(dy * n), sums[1] + fold(dy)
        sums = lax.fori_loop(0, n_ln, body, (zero, zero))
        for k, s in zip((2, 4), sums):
            sm[i, k:k + 1, :] = jnp.sum(s, axis=0, keepdims=True)
        leave(dbr, i, tg_hbm, i)

    def branch(i):
        def body(t, _):
            rows = rows_of(t, mt)
            for h in (0, 1):
                dst[i, h, rows, :] = dot(hid[i, rows, :], fc2w[:, h * half:(h + 1) * half])
            return 0
        lax.fori_loop(0, 2, body, 0)

        def sums_of(t, sums):
            rows = rows_of(t, LN_TILE)
            g = cot[i, rows, :].astype(F32)
            return sums[0] + fold(g * wide(dst, i, rows)), sums[1] + fold(g)
        zero = jnp.zeros((8, width), F32)
        sums = lax.fori_loop(0, n_ln, sums_of, (zero, zero))
        g2r[me, i:i + 1, :] = jnp.sum(sums[0], axis=0, keepdims=True)
        sm[i, 1:2, :] = fc2_b[...] * jnp.sum(sums[1], axis=0, keepdims=True)

    def block_end(i):
        def body(t, _):
            rows = rows_of(t, LN_TILE)
            middle = tok[i, rows, :].astype(F32) + vec(i, 0) * (wide(att, i, rows) + proj_b[...])
            cot[i, rows, :] = (middle + vec(i, 1) * (wide(dst, i, rows) + fc2_b[...])).astype(BF16)
            return 0
        lax.fori_loop(0, n_ln, body, 0)
        leave(cot, i, out_hbm, 2 + i)

    def every_copy(to, source):
        return pltpu.make_async_remote_copy(
            src_ref=sm, dst_ref=every.at[source], send_sem=ev_s.at[to], recv_sem=ev_r.at[source],
            device_id={"dp": to}, device_id_type=MESH)

    def every_start():
        pltpu.make_async_copy(sm, every.at[dp], out_sem.at[4]).start()

        def body(step, _):
            every_copy(lax.rem(dp + step, n_dp), dp).start()
            return 0
        lax.fori_loop(1, n_dp, body, 0)

    def every_finish():
        pltpu.make_async_copy(sm, every.at[dp], out_sem.at[4]).wait()

        def body(step, _):
            every_copy(lax.rem(dp + step, n_dp), dp).wait_send()
            source = lax.rem(dp + n_dp - step, n_dp)
            every_copy(source, source).wait_recv()
            return 0
        lax.fori_loop(1, n_dp, body, 0)

    def rs_both(buf, i, k):
        rs_copy(buf, i, k).start()
        rs_finish(buf, i, k)

    def forward(i):
        first_norm(i, i == 0)
        if i == 0:
            loads["qkvw"].wait()
        project(i)
        attend(i)
        if i == 0:
            loads["projw"].wait()
        attend_out(i)

    def close_sums():
        sent = share(g2r, g2_s, g2_r)
        for copy in sent:
            copy.wait()
        total = (g2r[0] + g2r[1]) + (g2r[2] + g2r[3])
        for i in (0, 1):
            sm[i, 1:2, :] = sm[i, 1:2, :] + total[i:i + 1, :]
        for j in range(4):
            sm[2, 1:2, j * 256:(j + 1) * 256] = jnp.sum(fb1[j], axis=0, keepdims=True)
        for k in range(3):
            for slab in (0, 1):
                at = k * 256 + slab * 128
                sm[2, 3:4, at:at + 128] = jnp.sum(lanes[k, slab], axis=0, keepdims=True)
        every_start()

    def spill_out(i):
        return pltpu.make_async_copy(att.at[i], spill.at[i], spill_sem.at[i])

    def spill_back(i):
        return pltpu.make_async_copy(spill.at[i], att.at[i], spill_sem.at[2 + i])

    def ag(buf, i, k):
        ag_copy(buf, i, k).start()
        ag_copy(buf, i, k).wait()

    sm[...] = jnp.zeros_like(sm)
    fb1[...] = jnp.zeros_like(fb1)
    lanes[...] = jnp.zeros_like(lanes)
    g2r[...] = jnp.zeros_like(g2r)
    kv[...] = jnp.zeros_like(kv)
    for i in (0, 1):
        sm[i, 6:7, :] = jnp.zeros((1, width), F32) + labels[i].astype(F32)
    unpack(tok_hbm, 1, tok, (cot_hbm, 0))
    forward(0)
    rs_both(att, 0, ATT)
    y_start(att, 0, ATT)
    forward(1)
    rs_both(att, 1, ATT)
    y_start(att, 1, ATT)
    unpack(cot_hbm, 0, cot, (cot_hbm, 1))
    unpack(cot_hbm, 1, cot)
    for name in ("fc1w", "fc2w"):
        loads[name].wait()
    y_finish(att, 0, ATT)
    ag(att, 0, ATT)
    mlp(0)
    rs_both(dst, 0, DS)
    y_start(dst, 0, DS)
    y_finish(att, 1, ATT)
    ag(att, 1, ATT)
    mlp_norm(1)
    mlp_columns(1)
    fc_grads((3, 4, 5,))
    mlp_back(1)
    rs_copy(dst, 1, DS).start()
    fc_grads((2, 6, 0, 1,))
    rs_finish(dst, 1, DS)
    y_start(dst, 1, DS)
    serve((2, 3))
    serve((2, 4))
    fc_grads((7,))
    y_finish(dst, 0, DS)
    ag(dst, 0, DS)
    second_back(0)
    spill_out(0).start()
    serve((2, 5))
    attend_back(0, 0)
    serve((3, 4))
    attend_back(0, 1)
    serve((2, 2))
    serve((3, 5), (3, 3))
    serve((4, 4))
    spill_out(0).wait()
    first_grad(0)
    rs_both(att, 0, DF)
    y_start(att, 0, DF)
    serve((2, 6))
    serve((3, 2))
    serve((4, 5))
    y_finish(dst, 1, DS)
    ag(dst, 1, DS)
    second_back(1)
    spill_out(1).start()
    serve((3, 6), (2, 0))
    serve((4, 2))
    attend_back(1, 0)
    serve((3, 0))
    serve((4, 6), (2, 1))
    attend_back(1, 1)
    serve((3, 1))
    serve((4, 0))
    s5(5)
    spill_out(1).wait()
    first_grad(1)
    s5(4)
    serve((2, 7))
    rs_both(att, 1, DF)
    serve((3, 7), (4, 3))
    y_start(att, 1, DF)
    first_norm(0)
    first_norm(1)
    attention_grads((8, 10, 9,))
    serve((4, 1))
    attention_grads((11,))
    y_finish(att, 0, DF)
    ag(att, 0, DF)
    first_back(0)
    spill_back(0).start()
    s5(0)
    serve((4, 7))
    branch(0)
    s5(6)
    serve((2, 11))
    rs_both(dst, 0, BR)
    serve((2, 8))
    y_start(dst, 0, BR)
    y_finish(att, 1, DF)
    s5(3)
    ag(att, 1, DF)
    serve((3, 8))
    first_back(1)
    spill_back(1).start()
    branch(1)
    serve((3, 11))
    rs_both(dst, 1, BR)
    serve((2, 10), (3, 10))
    s5(2)
    serve((4, 8))
    s5(7)
    s5(1)
    serve((2, 9))
    y_start(dst, 1, BR)
    s6(5)
    serve((3, 9))
    serve((4, 10))
    serve((4, 9))
    close_sums()
    serve((4, 11))
    s6(0)
    y_finish(dst, 0, BR)
    s5(8)
    ag(dst, 0, BR)
    spill_back(0).wait()
    block_end(0)
    y_finish(dst, 1, BR)
    s5(11)
    s5(10)
    s6(8)
    ag(dst, 1, BR)
    s5(9)
    spill_back(1).wait()
    block_end(1)
    every_finish()
    for n in (4, 6, 2, 3, 5, 0, 1, 7, 10, 8, 9, 11):
        close_chunk(n)
    left(3).wait()


def run_block(n_dp, class_table, ada_b, ada_w, tok, cot, stops, labels, log_scale, qkvw, projw, fc1w, fc2w, qv_b, proj_b, fc1_b, fc2_b):
    items, slots, width = tok.shape
    padded = -(-slots // LN_TILE) * LN_TILE
    x_count = sum(r != "Z" for r in ROUTES)
    half = width // 2
    hidden = fc1w.shape[1]
    n_chunks = 12
    n_rest = max(1, (n_dp // 8).bit_length() - 1)
    hbm = pl.BlockSpec(memory_space=pl.ANY)
    vmem = pl.BlockSpec(memory_space=pltpu.VMEM)
    smem = pl.BlockSpec(memory_space=pltpu.SMEM)
    wide_b = (items, padded, width)
    wide_f = (items, 2, padded, half)
    dma = pltpu.SemaphoreType.DMA
    return pl.pallas_call(
        functools.partial(block_kernel, slots, n_dp),
        out_shape=(
            jax.ShapeDtypeStruct(tok.shape, BF16), jax.ShapeDtypeStruct(tok.shape, BF16),
            jax.ShapeDtypeStruct(fc1w.shape, F32), jax.ShapeDtypeStruct(fc2w.shape, F32),
            jax.ShapeDtypeStruct(projw.shape, F32), jax.ShapeDtypeStruct(qkvw.shape, F32),
            jax.ShapeDtypeStruct((n_dp, 3, 8, width), F32),
            jax.ShapeDtypeStruct((n_chunks, 128, width), F32), jax.ShapeDtypeStruct((n_chunks, 128, width), F32),
            jax.ShapeDtypeStruct((n_chunks, 256, width), F32), jax.ShapeDtypeStruct((n_chunks, 128, width), F32),
            jax.ShapeDtypeStruct((n_rest, n_chunks, 128, width), F32), jax.ShapeDtypeStruct(wide_f, F32),
        ),
        in_specs=[hbm, vmem, hbm, hbm, hbm, smem, smem, smem, hbm, hbm, hbm, hbm, vmem, vmem, vmem, vmem],
        out_specs=(hbm,) * 13,
        scratch_shapes=[
            *[pltpu.VMEM(wide_b, BF16) for _ in range(4)],
            pltpu.VMEM((items, padded, hidden), BF16), pltpu.VMEM((items, hidden // 256, padded, 256), BF16),
            *[pltpu.VMEM(wide_f, F32) for _ in range(2)],
            pltpu.VMEM((items, padded, half), F32),
            pltpu.VMEM((items, 3, 2, padded, 128), BF16),
            pltpu.VMEM((items, 2, padded, 128), BF16),
            pltpu.VMEM((2, padded, 128), BF16),
            pltpu.VMEM((2, 2, 768, 128), BF16),
            pltpu.VMEM((3, 768, 128), F32),
            pltpu.VMEM((items, slots, half), F32),
            pltpu.VMEM((items, slots, half), F32),
            pltpu.VMEM(qkvw.shape, BF16), pltpu.VMEM(projw.shape, BF16),
            pltpu.VMEM(fc1w.shape, BF16), pltpu.VMEM(fc2w.shape, BF16),
            pltpu.VMEM((slots, width), BF16), pltpu.VMEM(class_table.shape, BF16), pltpu.VMEM((1, qkvw.shape[2]), F32),
            pltpu.VMEM((max(1, x_count), 128, width), F32), pltpu.VMEM((max(1, n_chunks - x_count), 256, width), F32),
            pltpu.VMEM((2, 256, width), F32),
            pltpu.VMEM((4, items, 8, width), F32), pltpu.VMEM((items, 8, width), F32),
            pltpu.VMEM((4, 8, width), F32),
            pltpu.VMEM((4, 8, 256), F32), pltpu.VMEM((3, 2, 8, 128), F32), pltpu.VMEM((3, 8, width), F32),
            dma((11,)), dma, dma((5,)), dma((5,)), dma((2,)), dma((2,)), dma((n_chunks, 4)), dma((4,)), pltpu.SemaphoreType.REGULAR((2,)),
            dma((3,)), dma((3,)), dma((3,)), dma((3,)),
            *[dma((8,)) for _ in range(6)],
            *[dma((n_chunks,)) for _ in range(8)], *[dma((n_chunks, 4)) for _ in range(6)],
            dma((n_rest, n_chunks)), dma((n_rest, n_chunks)), dma((n_dp,)), dma((n_dp,)),
        ],
        compiler_params=pltpu.CompilerParams(
            collective_id=0, has_side_effects=True, vmem_limit_bytes=62 * 2**20),
        name="block",
    )(class_table, ada_b, ada_w, tok, cot, stops, labels, log_scale, qkvw, projw, fc1w, fc2w, qv_b, proj_b, fc1_b, fc2_b)


def tail_kernel(
    every_hbm, table_hbm, ada_hbm, g1_in, g2_in, gp_in, gq_in, out_in, tg_in,
    table_grad, ada_grad, ada_bias, qv_bias, head_scale, proj_bias, fc1_bias, fc2_bias, g1, g2, gp, gq, out, tg,
    every, table, ada, part, *room_and_sems,
):
    n_dp, width = every.shape[0], every.shape[3]
    rows = 2 * n_dp
    rooms, (sem, part_sem, in_sem, copy_sem) = room_and_sems[:-4], room_and_sems[-4:]
    moved = ((g1_in, g1), (g2_in, g2), (gq_in, gq), (out_in, out), (tg_in, tg), (gp_in, gp))
    fetches = [pltpu.make_async_copy(a, room, in_sem.at[k]) for k, ((a, _), room) in enumerate(zip(moved, rooms))]
    copies = [pltpu.make_async_copy(room, b, copy_sem.at[k]) for k, ((_, b), room) in enumerate(zip(moved, rooms))]

    def move(k):
        fetches[k].wait()
        copies[k].start()
    loads = [pltpu.make_async_copy(a, b, sem.at[k])
             for k, (a, b) in enumerate(((every_hbm, every), (table_hbm, table), (ada_hbm, ada)))]
    for copy in (*loads, *fetches):
        copy.start()
    loads[0].wait()
    total = every[0, 2]
    for d in range(1, n_dp):
        total = total + every[d, 2]
    fc2_bias[...] = total[0:1]
    fc1_bias[...] = total[1:2]
    proj_bias[...] = total[2:3]
    wide = qv_bias.shape[1]
    qv_bias[0:1, :] = total[3:4, 0:wide]
    qv_bias[1:2, :] = total[3:4, wide:2 * wide]
    lanes = total[3:4, 2 * wide:3 * wide]
    head_of = lax.broadcasted_iota(jnp.int32, lanes.shape, 1) // 64
    spot = lax.broadcasted_iota(jnp.int32, head_scale.shape, 1)
    heads = jnp.zeros(head_scale.shape, F32)
    for h in range(head_scale.shape[1]):
        heads = jnp.where(spot == h, jnp.sum(jnp.where(head_of == h, lanes, 0.0), axis=1, keepdims=True), heads)
    head_scale[...] = heads
    move(0)
    move(1)

    def gathered(k):
        return jnp.concatenate([every[d, i, k:k + 1, :] for d in range(n_dp) for i in (0, 1)], axis=0)
    label = gathered(6)[:, 0:1]
    classes = table.shape[0]
    hot = jnp.where(lax.broadcasted_iota(jnp.int32, (rows, classes), 1).astype(F32) == label, 1.0, 0.0)
    loads[1].wait()
    local = dot(hot.astype(BF16), table[...])
    gate = 1.0 / (1.0 + jnp.exp(-local))
    lifted = (local * gate).astype(BF16)
    move(2)
    move(3)
    loads[2].wait()
    lifted_grad = jnp.zeros(local.shape, F32)

    def out_copy(k):
        return pltpu.make_async_copy(part.at[k % 2], ada_grad.at[:, pl.ds(k * width, width)], part_sem.at[k % 2])
    for k in range(6):
        low = gathered(k).astype(BF16)
        ada_bias[:, k * width:(k + 1) * width] = jnp.sum(low.astype(F32), axis=0, keepdims=True)
        lifted_grad = lifted_grad + dot(low, ada[:, k * width:(k + 1) * width], NT)
        if k >= 2:
            out_copy(k - 2).wait()
        part[k % 2] = dot(lifted, low, TN)
        out_copy(k).start()
        if k in (1, 3):
            move(4 + k // 2)
    class_grad = lifted_grad * (gate * (1.0 + local * (1.0 - gate)))
    table_grad[...] = lax.dot_general(hot, class_grad, TN, precision=lax.Precision.HIGHEST, preferred_element_type=F32)
    out_copy(4).wait()
    out_copy(5).wait()
    for copy in copies:
        copy.wait()


def run_tail(heads, every, class_table, ada_weight, g1, g2, gp, gq, out, tg):
    classes, wide = class_table.shape
    width = every.shape[3]
    hbm = pl.BlockSpec(memory_space=pl.ANY)
    vmem = pl.BlockSpec(memory_space=pltpu.VMEM)
    dma = pltpu.SemaphoreType.DMA
    shape = lambda *dims: jax.ShapeDtypeStruct(dims, F32)
    return pl.pallas_call(
        tail_kernel,
        out_shape=(
            shape(classes, wide), shape(*ada_weight.shape), shape(1, ada_weight.shape[1]), shape(2, wide), shape(1, heads),
            shape(1, width), shape(1, width), shape(1, width), shape(*g1.shape), shape(*g2.shape), shape(*gp.shape), shape(*gq.shape),
            jax.ShapeDtypeStruct(out.shape, out.dtype), jax.ShapeDtypeStruct(tg.shape, tg.dtype)),
        in_specs=[hbm] * 9,
        out_specs=(vmem, hbm, vmem, vmem, vmem, vmem, vmem, vmem, hbm, hbm, hbm, hbm, hbm, hbm),
        scratch_shapes=[
            pltpu.VMEM(every.shape, F32), pltpu.VMEM(class_table.shape, BF16), pltpu.VMEM(ada_weight.shape, BF16),
            pltpu.VMEM((2, wide, width), F32),
            *[pltpu.VMEM(a.shape, a.dtype) for a in (g1, g2, gq, out, tg, gp)],
            dma((3,)), dma((2,)), dma((6,)), dma((6,)),
        ],
        compiler_params=pltpu.CompilerParams(vmem_limit_bytes=60 * 2**20),
        name="tail",
    )(every, class_table, ada_weight, g1, g2, gp, gq, out, tg)


def shards(
    n_dp, tokens, cotangent, stop_scales, labels, class_table, ada_weight, ada_bias, qkv_weight, qv_bias, log_scale,
    proj_weight, proj_bias, fc1_weight, fc1_bias, fc2_weight, fc2_bias,
):
    items, slots, width = tokens.shape
    heads = log_scale.shape[0]
    out, tg, g1, g2, gp, gq, every, *_ = run_block(
        n_dp, class_table, ada_bias[None, :], ada_weight, tokens, cotangent, stop_scales, labels, log_scale,
        jnp.transpose(qkv_weight, (1, 0, 2)), proj_weight, fc1_weight, fc2_weight,
        qv_bias, proj_bias[None, :], fc1_bias.reshape(-1, 1, 256), fc2_bias[None, :])
    table_grad, ada_grad, ada_bias_grad, qv_grad, scale_grad, proj_b, fc1_b, fc2_b, g1, g2, gp, gq, out, tg = run_tail(
        heads, every, class_table, ada_weight, g1, g2, gp, gq, out, tg)
    return (
        out, tg, table_grad, ada_grad, ada_bias_grad[0], jnp.transpose(gq, (1, 0, 2)), qv_grad, scale_grad[0],
        gp, proj_b[0], g1, fc1_b[0], g2, fc2_b[0],
    )


def solution(mesh):
    return jax.shard_map(
        functools.partial(shards, mesh.shape["dp"]),
        mesh=mesh,
        in_specs=(
            P("dp", None, None), P("dp", None, None), P("dp"), P("dp"), P(None, "mp"), P("mp", None), P(),
            P(None, None, "mp"), P(None, "mp"), P("mp"), P("mp", None), P(), P(None, "mp"), P("mp"), P("mp", None), P(),
        ),
        out_specs=(
            P("dp", None, None), P("dp", None, None), P(None, "mp"), P("mp", None), P(), P(None, None, "mp"), P(None, "mp"),
            P("mp"), P("mp", None), P(), P(None, "mp"), P("mp"), P("mp", None), P(),
        ),
        check_vma=False,
    )
```

```python
import functools

import jax
import jax.numpy as jnp
import numpy as np
from jax import lax
from jax.experimental import pallas as pl
from jax.experimental.pallas import tpu as pltpu
from jax.sharding import PartitionSpec as P

SIDE_LIST = (1, 2, 3, 4, 5, 6, 8, 10, 13, 16)
EPSILON = 1e-06
MESH = pl.DeviceIdType.MESH
F32, BF16 = jnp.float32, jnp.bfloat16
GELU_C = 0.7978845608028654
GELU_A = 0.044715
LN_TILE = 176
NT = (((1,), (1,)), ((), ()))
TN = (((0,), (0,)), ((), ()))
NN = (((1,), (0,)), ((), ()))
ATT, DS, DF, BR = 0, 2, 4, 6
ROUTES = "CAAZACBACAAZ"


def dot(a, b, dims=NN):
    return lax.dot_general(a, b, dims, preferred_element_type=F32)


def norm_rows(v):
    center = v - jnp.mean(v, axis=-1, keepdims=True)
    scale = lax.rsqrt(jnp.mean(center * center, axis=-1, keepdims=True) + EPSILON)
    return center * scale, scale


def fold(v):
    return jnp.sum(v.reshape(v.shape[0] // 8, 8, v.shape[1]), axis=0)


def head_sum(v, blocks):
    high = v.astype(BF16)
    rest = (v - high.astype(F32)).astype(BF16)
    return dot(high, blocks) + dot(rest, blocks)


def block_kernel(
    slots, n_dp,
    table_hbm, ada_b, ada_hbm, tok_hbm, cot_hbm, stops, labels, log_scale,
    qkvw_hbm, projw_hbm, fc1w_hbm, fc2w_hbm,
    qv_b, proj_b, fc1_b, fc2_b,
    out_hbm, tg_hbm, g1_out, g2_out, gp_out, gq_out, every, x_out, x_in, z_in, mid_in, rest_in, spill,
    tok, cot, sec, dbr, hid, dup,
    att, dst,
    qk, qkn, mix, dmx, kv, acc,
    rs_buf, y_buf,
    qkvw, projw, fc1w, fc2w,
    raw, table, es_row, px, pz, stage, modr, mod, g2r, fb1, lanes, sm,
    in_sem, raw_sem, out_sem, load_sem, store_sem, keep_sem, final_sem, spill_sem, y_free,
    mod_s, mod_r, g2_s, g2_r, rs_s, rs_r, y_s, y_r, ag_s, ag_r,
    x1_s, x1_r, zi_s, zi_r, mi_s, mi_r, zb_s, zb_r, zo_s, zo_r, x2_s, x2_r, zc_s, zc_r, re_s, re_r, ev_s, ev_r,
):
    items, padded, width = tok.shape
    half = width // 2
    me = lax.axis_index("mp")
    dp = lax.axis_index("dp")
    xb = lax.rem(dp, 2)
    z = lax.rem(dp // 2, 4)
    zh = z // 2
    inner = jnp.logical_or(z == 1, z == 2)
    edge = jnp.logical_or(z == 0, z == 3)
    x_mate = dp + 1 - 2 * xb
    z_mate = dp + 2 - 4 * lax.rem(z, 2)
    mid_mate = jnp.where(z == 1, dp + 2, jnp.where(z == 2, dp - 2, dp))
    n_rest = rest_in.shape[0] if n_dp > 8 else 0
    rest_mates = [dp + (8 << k) * (1 - 2 * lax.rem(dp // (8 << k), 2)) for k in range(n_rest)]
    core = lax.rem(me, 2)
    core_mate = me + 1 - 2 * core
    y_mate = lax.rem(me + 2, 4)
    n_ln = padded // LN_TILE
    mt = padded // 2

    def rows_of(t, n):
        return pl.ds(pl.multiple_of(t * n, n), n)

    def wide(buf, i, rows):
        return jnp.concatenate([buf[i, 0, rows, :], buf[i, 1, rows, :]], axis=1)

    def put_wide(buf, i, rows, v):
        buf[i, 0, rows, :] = v[:, :half]
        buf[i, 1, rows, :] = v[:, half:]

    def raw_copy(src, i):
        return pltpu.make_async_copy(src.at[i], raw, raw_sem)

    def unpack(src, i, to, then=None):
        raw_copy(src, i).wait()
        whole = slots // 16 * 16

        def body(t, _):
            rows = rows_of(t, 16)
            to[i, rows, :] = raw[rows, :]
            return 0
        lax.fori_loop(0, slots // 16, body, 0)
        tail = raw[whole:slots, :].astype(F32)
        rest = jnp.concatenate([tail, jnp.zeros((padded - slots, width), F32)], axis=0)
        to[i, whole:padded, :] = rest.astype(BF16)
        if then is not None:
            raw_copy(*then).start()

    raw_copy(tok_hbm, 0).start()
    rows_ada = ada_hbm.shape[0]
    ada_room = [buf.at[i, pl.ds(k * rows_ada, rows_ada)] for buf, i, k in (
        (hid, 0, 0), (hid, 0, 1), (hid, 1, 0), (hid, 1, 1), (sec, 0, 0), (sec, 1, 0))]
    loads = {}
    for k, (name, src, to) in enumerate((
        ("table", table_hbm, table),
        *[(f"ada{c}", ada_hbm.at[:, pl.ds(c * width, width)], ada_room[c]) for c in range(6)],
        ("qkvw", qkvw_hbm, qkvw), ("projw", projw_hbm, projw), ("fc1w", fc1w_hbm, fc1w), ("fc2w", fc2w_hbm, fc2w),
    )):
        loads[name] = pltpu.make_async_copy(src, to, in_sem.at[k])
        loads[name].start()

    barrier = pltpu.get_barrier_semaphore()
    for step in (1, 2, 3):
        pl.semaphore_signal(barrier, inc=1, device_id={"mp": lax.rem(me + step, 4)}, device_id_type=MESH)
    def greet(step, _):
        pl.semaphore_signal(barrier, inc=1, device_id={"dp": lax.rem(dp + step, n_dp)}, device_id_type=MESH)
        return 0
    lax.fori_loop(1, n_dp, greet, 0)

    def share(buf, send, recv):
        copies = []
        for step in (1, 2, 3):
            copies.append(pltpu.make_async_remote_copy(
                src_ref=buf.at[me], dst_ref=buf.at[me], send_sem=send.at[step - 1], recv_sem=recv.at[step - 1],
                device_id={"mp": lax.rem(me + step, 4)}, device_id_type=MESH))
        for copy in copies:
            copy.start()
        return copies

    loads["table"].wait()
    spot = (16, table.shape[0])
    item_at = lax.broadcasted_iota(jnp.int32, spot, 0)
    class_at = lax.broadcasted_iota(jnp.int32, spot, 1)
    hot = jnp.zeros(spot, F32)
    for i in range(items):
        hot = jnp.where(jnp.logical_and(item_at == i, class_at == labels[i]), 1.0, hot)
    local = dot(hot.astype(BF16), table[...])
    lifted = (local * (1.0 / (1.0 + jnp.exp(-local)))).astype(BF16)
    for c in range(6):
        loads[f"ada{c}"].wait()
        part = dot(lifted, ada_room[c][...])
        for i in range(items):
            modr[me, i, c:c + 1, :] = part[i:i + 1, :]
    for i in range(items):
        modr[me, i, 6:8, :] = jnp.zeros((2, width), F32)
    pl.semaphore_wait(barrier, 3 + n_dp - 1)
    sent = share(modr, mod_s, mod_r)
    unpack(tok_hbm, 0, tok, (tok_hbm, 1))

    def early(t, _):
        rows = rows_of(t, LN_TILE)
        n, _r = norm_rows(tok[0, rows, :].astype(F32))
        put_wide(att, 0, rows, n)
        return 0
    lax.fori_loop(0, n_ln, early, 0)
    for copy in sent:
        copy.wait()
    mod[...] = (modr[0] + modr[1]) + (modr[2] + modr[3])
    for i in range(items):
        for c in range(6):
            mod[i, c:c + 1, :] = mod[i, c:c + 1, :] + ada_b[:, c * width:(c + 1) * width]
    lane = lax.broadcasted_iota(jnp.int32, es_row.shape, 1) // 64
    scales = jnp.zeros(es_row.shape, F32)
    for h in range(es_row.shape[1] // 64):
        scales = jnp.where(lane == h, log_scale[h], scales)
    es_row[...] = jnp.exp(scales)

    def vec(i, k):
        return mod[i, k:k + 1, :]

    def rs_copy(buf, i, k):
        return pltpu.make_async_remote_copy(
            src_ref=buf.at[i, 1 - core, pl.ds(0, slots)], dst_ref=rs_buf.at[i], send_sem=rs_s.at[k + i], recv_sem=rs_r.at[k + i],
            device_id={"mp": core_mate}, device_id_type=MESH)

    def y_copy(buf, i, k):
        dst = qk.at[i, pl.ds(0, slots)] if k == BR else y_buf.at[i]
        return pltpu.make_async_remote_copy(
            src_ref=buf.at[i, core, pl.ds(0, slots)], dst_ref=dst, send_sem=y_s.at[k + i], recv_sem=y_r.at[k + i],
            device_id={"mp": y_mate}, device_id_type=MESH)

    def ag_copy(buf, i, k):
        return pltpu.make_async_remote_copy(
            src_ref=buf.at[i, core, pl.ds(0, slots)], dst_ref=buf.at[i, core, pl.ds(0, slots)],
            send_sem=ag_s.at[k + i], recv_sem=ag_r.at[k + i],
            device_id={"mp": core_mate}, device_id_type=MESH)

    add_rows = slots // 5

    def rs_finish(buf, i, k):
        rs_copy(buf, i, k).wait()

        def add(t, _):
            rows = rows_of(t, add_rows)
            buf[i, core, rows, :] = buf[i, core, rows, :] + rs_buf[i, rows, :]
            return 0
        lax.fori_loop(0, 5, add, 0)

    def y_finish(buf, i, k):
        y_copy(buf, i, k).wait()

        def add(t, _):
            rows = rows_of(t, add_rows)
            other = qk[i, rows, :] if k == BR else y_buf[i, rows, :]
            buf[i, core, rows, :] = buf[i, core, rows, :] + other
            return 0
        lax.fori_loop(0, 5, add, 0)
        if k in (ATT, DS):
            pl.semaphore_signal(y_free.at[i], inc=1, device_id={"mp": y_mate}, device_id_type=MESH)

    def y_start(buf, i, k):
        if k in (DS, DF):
            pl.semaphore_wait(y_free.at[i], 1)
        y_copy(buf, i, k).start()

    def blocks_of(n):
        a = lax.broadcasted_iota(jnp.int32, (n, n), 0) // 64
        b = lax.broadcasted_iota(jnp.int32, (n, n), 1) // 64
        return jnp.where(a == b, 1.0, 0.0).astype(BF16)

    ends = np.cumsum(np.array([s * s for s in SIDE_LIST]))
    tiles = ((0, 240, 1, 256), (240, 176, 1, 512), (416, 96, 3, 768))

    def keep_of(i, rows, keys):
        live = jnp.int32(0)
        for s in range(len(SIDE_LIST)):
            live = jnp.where(stops[i] == s + 1, int(ends[s]), live)
        n = rows.size
        at = rows.start + lax.broadcasted_iota(jnp.int32, (n, 1), 0)
        bound = jnp.full((n, 1), int(ends[0]), jnp.int32)
        for s in range(1, len(SIDE_LIST)):
            bound = jnp.where(at >= int(ends[s - 1]), int(ends[s]), bound)
        bound = jnp.minimum(bound, live)
        return lax.broadcasted_iota(jnp.int32, (n, keys), 1) < bound

    def one_head(h):
        lane = lax.broadcasted_iota(jnp.int32, (1, 128), 1) // 64
        return jnp.where(lane == h, 1.0, 0.0).astype(BF16)

    def fill_kv(i, slab):
        for c in (0, 1):
            for h in (0, 1):
                kv[c, h, 0:padded, :] = qkn[i, 1 + c, slab] * one_head(h)

    def exps(i, slab, rows, keys):
        keep = keep_of(i, rows, keys)
        s = dot(qkn[i, 0, slab, rows, :], kv[0, :, 0:keys, :].reshape(2 * keys, 128), NT)
        parts = []
        for h in (0, 1):
            e = jnp.where(keep, jnp.exp(s[:, h * keys:(h + 1) * keys]), 0.0)
            parts.append(e * (1.0 / jnp.sum(e, axis=-1, keepdims=True)))
        return parts

    def each_tile(body):
        for first_row, n, steps, keys in tiles:
            if steps == 1:
                body(pl.ds(first_row, n), keys)
            else:
                def step(t, _, first_row=first_row, n=n, keys=keys):
                    body(pl.ds(pl.multiple_of(first_row + t * n, 16), n), keys)
                    return 0
                lax.fori_loop(0, steps, step, 0)

    def first_norm(i, ready=False):
        def body(t, _):
            rows = rows_of(t, LN_TILE)
            n = wide(att, i, rows) if ready else norm_rows(tok[i, rows, :].astype(F32))[0]
            dbr[i, rows, :] = (n * (1.0 + vec(i, 2)) + vec(i, 4)).astype(BF16)
            return 0
        lax.fori_loop(0, n_ln, body, 0)

    def project(i):
        blocks = blocks_of(256)

        def body(t, _):
            rows = rows_of(t, mt)
            f = dbr[i, rows, :]
            q = dot(f, qkvw[0]) + qv_b[0:1, :]
            qk[i, rows, 0:256] = q
            u = q * lax.rsqrt(head_sum(q * q, blocks) + EPSILON) * es_row[...]
            qkn[i, 0, 0, rows, :] = u[:, :128].astype(BF16)
            qkn[i, 0, 1, rows, :] = u[:, 128:].astype(BF16)
            k = dot(f, qkvw[1])
            qk[i, rows, 256:512] = k
            u = k * lax.rsqrt(head_sum(k * k, blocks) + EPSILON)
            qkn[i, 1, 0, rows, :] = u[:, :128].astype(BF16)
            qkn[i, 1, 1, rows, :] = u[:, 128:].astype(BF16)
            v = dot(f, qkvw[2]) + qv_b[1:2, :]
            qkn[i, 2, 0, rows, :] = v[:, :128].astype(BF16)
            qkn[i, 2, 1, rows, :] = v[:, 128:].astype(BF16)
            return 0
        lax.fori_loop(0, 2, body, 0)

    def attend(i):
        def slab_body(slab, _):
            fill_kv(i, slab)

            def body(rows, keys):
                p = jnp.concatenate([v.astype(BF16) for v in exps(i, slab, rows, keys)], axis=1)
                o = dot(p, kv[1, :, 0:keys, :].reshape(2 * keys, 128))
                mix[i, slab, rows, :] = o.astype(BF16)
            each_tile(body)
            return 0
        lax.fori_loop(0, 2, slab_body, 0)

    def attend_out(i):
        def body(t, _):
            rows = rows_of(t, mt)
            m = jnp.concatenate([mix[i, 0, rows, :], mix[i, 1, rows, :]], axis=1)
            for h in (0, 1):
                att[i, h, rows, :] = dot(m, projw[:, h * half:(h + 1) * half])
            return 0
        lax.fori_loop(0, 2, body, 0)

    def mlp_norm(i):
        def body(t, total):
            rows = rows_of(t, LN_TILE)
            middle = tok[i, rows, :].astype(F32) + vec(i, 0) * (wide(att, i, rows) + proj_b[...])
            n, _r = norm_rows(middle)
            sec[i, rows, :] = (n * (1.0 + vec(i, 3)) + vec(i, 5)).astype(BF16)
            d = (cot[i, rows, :].astype(F32) * vec(i, 1)).astype(BF16)
            dbr[i, rows, :] = d
            return total + fold(d.astype(F32))
        total = lax.fori_loop(0, n_ln, body, jnp.zeros((8, width), F32))
        sm[2, 0:1, :] = sm[2, 0:1, :] + jnp.sum(total, axis=0, keepdims=True)

    def mlp_column(i, j):
        cols = pl.ds(pl.multiple_of(j * 256, 256), 256)

        def body(t, _):
            rows = rows_of(t, mt)
            u = dot(sec[i, rows, :], fc1w[:, cols]) + fc1_b[j]
            dh = dot(dbr[i, rows, :], fc2w[cols, :], NT)
            square = u * u
            th = jnp.tanh(u * (GELU_C + (GELU_C * GELU_A) * square))
            gate = 0.5 + 0.5 * th
            out = u * gate
            hid[i, rows, cols] = out.astype(BF16)
            slope = gate + out * (1.0 - th) * (GELU_C + (3.0 * GELU_C * GELU_A) * square)
            d = (dh * slope).astype(BF16)
            dup[i, j, rows, :] = d
            fb1[j] = fb1[j] + fold(d.astype(F32))
            return 0
        lax.fori_loop(0, 2, body, 0)

    def mlp_back(i):
        def back(t, _):
            rows = rows_of(t, mt)
            d = jnp.concatenate([dup[i, j, rows, :] for j in range(dup.shape[1])], axis=1)
            for h in (0, 1):
                dst[i, h, rows, :] = dot(d, fc1w[h * half:(h + 1) * half, :], NT)
            return 0
        lax.fori_loop(0, 2, back, 0)

    def mlp_columns(i):
        def column(j, _):
            mlp_column(i, j)
            return 0
        lax.fori_loop(0, dup.shape[1], column, 0)

    def mlp(i):
        mlp_norm(i)
        mlp_columns(i)
        mlp_back(i)

    x_list = [n for n in range(12) if ROUTES[n] != "Z"]
    z_list = [n for n in range(12) if ROUTES[n] == "Z"]

    def is_x(n):
        return ROUTES[n] != "Z"

    def side(h):
        return pl.ds(pl.multiple_of(h * 128, 128), 128)

    def own(n):
        return px.at[x_list.index(n)] if is_x(n) else pz.at[z_list.index(n), side(zh)]

    def final_of(n, h):
        if n < 8:
            return [(g2_out if n < 4 else g1_out).at[pl.ds(pl.multiple_of((n % 4) * 256 + h * 128, 128), 128)]]
        if n == 8:
            return [gp_out.at[side(h)]]
        return [gq_out.at[n - 9, pl.ds(pl.multiple_of(j * 256 + h * 128, 128), 128)] for j in range(4)]

    def in_pieces(n, ref):
        return [ref] if n < 9 else [ref.at[:, pl.ds(j * 256, 256)] for j in range(4)]

    def my_half(n):
        return xb if is_x(n) else zh

    class Pieces:
        def __init__(self, n, srcs, tos, send, recv, mate):
            self.parts = lambda: [
                to_dp(a, b, send.at[n, j], recv.at[n, j], mate) for j, (a, b) in enumerate(zip(srcs, tos))]

        def start(self):
            for part in self.parts():
                part.start()

        def wait_send(self):
            for part in self.parts():
                part.wait_send()

        def wait_recv(self):
            for part in self.parts():
                part.wait_recv()

        def wait(self):
            self.wait_send()
            self.wait_recv()

    def to_dp(src, to, send, recv, mate):
        return pltpu.make_async_remote_copy(
            src_ref=src, dst_ref=to, send_sem=send, recv_sem=recv, device_id={"dp": mate}, device_id_type=MESH)

    def x1(n):
        return to_dp(x_out.at[n] if is_x(n) else own(n), x_in.at[n], x1_s.at[n], x1_r.at[n], x_mate)

    def zin(n):
        if is_x(n):
            return to_dp(own(n), z_in.at[n, pl.ds(0, 128)], zi_s.at[n], zi_r.at[n], z_mate)
        return to_dp(far(n), z_in.at[n, side(1 - zh)], zi_s.at[n], zi_r.at[n], z_mate)

    def far(n):
        return pz.at[z_list.index(n), side(1 - zh)]

    def zin_b(n):
        return to_dp(own(n), z_in.at[n, side(zh)], zb_s.at[n], zb_r.at[n], z_mate)

    def mid(n):
        return to_dp(own(n) if is_x(n) else far(n), mid_in.at[n], mi_s.at[n], mi_r.at[n], mid_mate)

    def zout(n):
        return Pieces(n, in_pieces(n, own(n)), final_of(n, my_half(n)), zo_s, zo_r, z_mate)

    def zout_b(n):
        views = final_of(n, 1 - my_half(n))
        return Pieces(n, views, views, zc_s, zc_r, z_mate)

    def x2(n, at_the_edge=False):
        views = final_of(n, xb)
        return Pieces(n, views if at_the_edge else in_pieces(n, own(n)), views, x2_s, x2_r, x_mate)

    def swap(n):
        return Pieces(n, in_pieces(n, own(n)), final_of(n, zh), x2_s, x2_r, mid_mate)

    class store_final:
        def __init__(self, n):
            self.parts = lambda: [
                pltpu.make_async_copy(a, b, final_sem.at[n, j])
                for j, (a, b) in enumerate(zip(in_pieces(n, own(n)), final_of(n, my_half(n))))]

        def start(self):
            for part in self.parts():
                part.start()

        def wait(self):
            for part in self.parts():
                part.wait()

    def at_edge(body):
        pl.when(edge)(body)

    def at_inner(body):
        pl.when(inner)(body)

    def accumulate(to, what):
        def add(t, _):
            rows = rows_of(t, 16)
            to[rows, :] = to[rows, :] + what[rows, :]
            return 0
        lax.fori_loop(0, 8, add, 0)

    def add_all(items):
        def slot(k):
            return stage.at[0, pl.ds((k % 2) * 128, 128)]

        def load(k):
            return pltpu.make_async_copy(items[k][1], slot(k), load_sem.at[k % 4])

        def begin(k):
            items[k][0]()
            load(k).start()
        for k in range(min(2, len(items))):
            begin(k)
        for k in range(len(items)):
            load(k).wait()
            accumulate(items[k][2], slot(k))
            items[k][3]()
            if k + 2 < len(items):
                begin(k + 2)

    def rest_sum(n):
        for k in range(n_rest):
            copy = to_dp(own(n), rest_in.at[k, n], re_s.at[k, n], re_r.at[k, n], rest_mates[k])
            copy.start()
            copy.wait()
            extra = stage.at[1, pl.ds(0, 128)]
            load = pltpu.make_async_copy(rest_in.at[k, n], extra, load_sem.at[4])
            load.start()
            load.wait()
            accumulate(own(n), extra)

    def items_of(step, n):
        if is_x(n):
            if step == 2:
                return [(lambda: x1(n).wait(), x_in.at[n], own(n), lambda: at_edge(lambda: zin(n).start()))]
            if step == 3:
                return [(lambda: zin(n).wait_recv(), z_in.at[n, pl.ds(0, 128)], own(n), lambda: mid(n).start())]

            def close():
                rest_sum(n)
                zout(n).start()
                if ROUTES[n] != "C":
                    x2(n).start()
                store_final(n).start()
            return [(lambda: mid(n).wait(), mid_in.at[n], own(n), close)]
        if step == 2:
            return [(lambda: zin(n).wait_recv(), z_in.at[n, side(1 - zh)], far(n), lambda: mid(n).start())]
        if step == 3:
            def close():
                rest_sum(n)
                x1(n).start()
            return [
                (lambda: zin_b(n).wait_recv(), z_in.at[n, side(zh)], own(n), lambda: None),
                (lambda: mid(n).wait(), mid_in.at[n], own(n), close)]

        def close():
            swap(n).start()
            zout(n).start()
            store_final(n).start()
        return [(lambda: x1(n).wait(), x_in.at[n], own(n), close)]

    def serve(*tasks):
        at_inner(lambda: add_all([item for step, n in tasks for item in items_of(step, n)]))
        outer = [item for step, n in tasks if step == 2 and is_x(n) for item in items_of(step, n)]
        if outer:
            at_edge(lambda: add_all(outer))

    def s5(n):
        if ROUTES[n] == "Z":
            @at_inner
            def _():
                swap(n).wait()
                zout_b(n).start()
        elif ROUTES[n] == "B":
            @at_inner
            def _():
                x2(n).wait()
                zout_b(n).start()
        else:
            @at_edge
            def _():
                zin(n).wait_send()
                zout(n).wait_recv()
                x2(n, True).start()

    def s6(n):
        @at_edge
        def _():
            x2(n, True).wait()
            zout_b(n).start()

    def close_chunk(n):
        kind = ROUTES[n]

        @at_edge
        def _():
            if kind == "A":
                x2(n, True).wait()
            if kind in "BZ":
                zin(n).wait_send()
                if kind == "Z":
                    zin_b(n).wait_send()
                zout(n).wait_recv()
                zout_b(n).wait_recv()
            if kind == "C":
                zout_b(n).wait_send()

        @at_inner
        def _():
            if kind == "A":
                x2(n).wait()
            zout(n).wait_send()
            store_final(n).wait()
            if kind in "BZ":
                zout_b(n).wait_send()
            if kind == "C":
                zout_b(n).wait_recv()

    def produce(ns, make):
        turn = {n: k % 2 for k, n in enumerate(n for n in ns if is_x(n))}

        def copies(n):
            slot = stage.at[turn[n]]
            return (pltpu.make_async_copy(slot.at[side(1 - xb)], x_out.at[n], store_sem.at[turn[n]]),
                    pltpu.make_async_copy(slot.at[side(xb)], own(n), keep_sem.at[turn[n]]))

        def launch(n):
            for copy in copies(n):
                copy.wait()
            x1(n).start()
        waiting = []
        for n in ns:
            if is_x(n):
                make(stage.at[turn[n]], n)
                for copy in copies(n):
                    copy.start()
            else:
                make(pz.at[z_list.index(n)], n)

                @at_edge
                def _():
                    zin(n).start()
                    zin_b(n).start()
            for m in waiting:
                launch(m)
            waiting = [n] if is_x(n) else []
        for m in waiting:
            launch(m)

    def both(ref, *rest):
        return jnp.concatenate([ref[(0, *rest)], ref[(1, *rest)]], axis=0)

    def fc_grads(ns):
        def make(to, n):
            j = n % 4
            cols = pl.ds(j * 256, 256)
            if n < 4:
                to[...] = dot(both(hid, slice(None), cols), both(dbr), TN)
            else:
                d = jnp.concatenate([both(dup, m) for m in range(4)], axis=1)
                to[...] = dot(both(sec, slice(None), cols), d, TN)
        produce(ns, make)

    def attention_grads(ns):
        def make(to, n):
            if n == 8:
                for slab in (0, 1):
                    to[slab * 128:(slab + 1) * 128, :] = dot(both(mix, slab), both(sec), TN)
            else:
                def piece(j, _):
                    cols = pl.ds(pl.multiple_of(j * 256, 256), 256)
                    to[:, cols] = dot(both(dbr, slice(None), cols), both(dup, n - 9), TN)
                    return 0
                lax.fori_loop(0, 4, piece, 0)
        produce(ns, make)

    def second_back(i):
        zero = jnp.zeros((8, width), F32)

        def body(t, sums):
            rows = rows_of(t, LN_TILE)
            attended = wide(att, i, rows) + proj_b[...]
            n, r = norm_rows(tok[i, rows, :].astype(F32) + vec(i, 0) * attended)
            dy = wide(dst, i, rows)
            dn = dy * (1.0 + vec(i, 3))
            dm = cot[i, rows, :].astype(F32) + r * (
                dn - jnp.mean(dn, axis=-1, keepdims=True) - n * jnp.mean(dn * n, axis=-1, keepdims=True))
            put_wide(dst, i, rows, dm)
            da = (dm * vec(i, 0)).astype(BF16)
            sec[i, rows, :] = da
            return (sums[0] + fold(dm * attended), sums[1] + fold(dy * n), sums[2] + fold(dy), sums[3] + fold(da.astype(F32)))
        sums = lax.fori_loop(0, n_ln, body, (zero, zero, zero, zero))
        for k, s in zip((0, 3, 5), sums[:3]):
            sm[i, k:k + 1, :] = jnp.sum(s, axis=0, keepdims=True)
        sm[2, 2:3, :] = sm[2, 2:3, :] + jnp.sum(sums[3], axis=0, keepdims=True)

        def mixed(t, _):
            rows = rows_of(t, mt)
            d = dot(sec[i, rows, :], projw[...], NT)
            dmx[0, rows, :] = d[:, :128].astype(BF16)
            dmx[1, rows, :] = d[:, 128:].astype(BF16)
            return 0
        lax.fori_loop(0, 2, mixed, 0)

    def attend_back(i, slab):
        blocks = blocks_of(128)
        fill_kv(i, slab)
        acc[...] = jnp.zeros_like(acc)

        def body(rows, keys):
            p = exps(i, slab, rows, keys)
            d = dmx[slab, rows, :]
            q = qkn[i, 0, slab, rows, :]
            ds = []
            dp_both = dot(d, kv[1, :, 0:keys, :].reshape(2 * keys, 128), NT)
            for h in (0, 1):
                dpr = dp_both[:, h * keys:(h + 1) * keys]
                ds.append((p[h] * (dpr - jnp.sum(dpr * p[h], axis=-1, keepdims=True))).astype(BF16))
            acc[0, rows, :] = dot(jnp.concatenate(ds, axis=1), kv[0, :, 0:keys, :].reshape(2 * keys, 128))
            kr = pl.ds(0, keys)
            acc[1, kr, :] += dot(
                jnp.concatenate(ds, axis=0), jnp.concatenate([q * one_head(h) for h in (0, 1)], axis=0), TN)
            acc[2, kr, :] += dot(
                jnp.concatenate([v.astype(BF16) for v in p], axis=0),
                jnp.concatenate([d * one_head(h) for h in (0, 1)], axis=0), TN)
        each_tile(body)
        es = es_row[:, slab * 128:(slab + 1) * 128]

        def close(t, sums):
            rows = rows_of(t, LN_TILE)

            def unit(c, g):
                at = c * 256 + slab * 128
                pre = qk[i, rows, at:at + 128]
                r = lax.rsqrt(head_sum(pre * pre, blocks) + EPSILON)
                u = pre * r
                gu = g * u
                return r * (g - u * head_sum(gu, blocks)), gu
            dq, gu = unit(0, acc[0, rows, :] * es)
            dk, _g = unit(1, acc[1, rows, :])
            dq, dk, dv = dq.astype(BF16), dk.astype(BF16), acc[2, rows, :].astype(BF16)
            to = pl.ds(slab * 128, 128)
            dup[i, 0, rows, to] = dq
            dup[i, 1, rows, to] = dk
            dup[i, 2, rows, to] = dv
            return sums[0] + fold(dq.astype(F32)), sums[1] + fold(dv.astype(F32)), sums[2] + fold(gu)
        zero = jnp.zeros((8, 128), F32)
        sums = lax.fori_loop(0, n_ln, close, (zero, zero, zero))
        for k in range(3):
            lanes[k, slab] = lanes[k, slab] + sums[k]

    def first_grad(i):
        def body(t, _):
            rows = rows_of(t, mt)
            for h in (0, 1):
                total = None
                for c in range(3):
                    o = dot(dup[i, c, rows, :], qkvw[c, h * half:(h + 1) * half, :], NT)
                    total = o if total is None else total + o
                att[i, h, rows, :] = total
            return 0
        lax.fori_loop(0, 2, body, 0)

    def left(k):
        return pltpu.make_async_copy(raw, (tg_hbm, out_hbm)[k // 2].at[k % 2], out_sem.at[k])

    def leave(buf, i, to, k):
        if k > 0:
            left(k - 1).wait()

        def body(t, _):
            rows = rows_of(t, 16)
            raw[rows, :] = buf[i, rows, :]
            return 0
        lax.fori_loop(0, slots // 16, body, 0)
        whole = slots // 16 * 16
        raw[whole:slots, :] = buf[i, whole:whole + 16, :].astype(F32)[:slots - whole].astype(BF16)
        left(k).start()

    def first_back(i):
        zero = jnp.zeros((8, width), F32)

        def body(t, sums):
            rows = rows_of(t, LN_TILE)
            n, r = norm_rows(tok[i, rows, :].astype(F32))
            dy = wide(att, i, rows)
            dn = dy * (1.0 + vec(i, 2))
            g = wide(dst, i, rows) + r * (
                dn - jnp.mean(dn, axis=-1, keepdims=True) - n * jnp.mean(dn * n, axis=-1, keepdims=True))
            dbr[i, rows, :] = g.astype(BF16)
            return sums[0] + fold(dy * n), sums[1] + fold(dy)
        sums = lax.fori_loop(0, n_ln, body, (zero, zero))
        for k, s in zip((2, 4), sums):
            sm[i, k:k + 1, :] = jnp.sum(s, axis=0, keepdims=True)
        leave(dbr, i, tg_hbm, i)

    def branch(i):
        def body(t, _):
            rows = rows_of(t, mt)
            for h in (0, 1):
                dst[i, h, rows, :] = dot(hid[i, rows, :], fc2w[:, h * half:(h + 1) * half])
            return 0
        lax.fori_loop(0, 2, body, 0)

        def sums_of(t, sums):
            rows = rows_of(t, LN_TILE)
            g = cot[i, rows, :].astype(F32)
            return sums[0] + fold(g * wide(dst, i, rows)), sums[1] + fold(g)
        zero = jnp.zeros((8, width), F32)
        sums = lax.fori_loop(0, n_ln, sums_of, (zero, zero))
        g2r[me, i:i + 1, :] = jnp.sum(sums[0], axis=0, keepdims=True)
        sm[i, 1:2, :] = fc2_b[...] * jnp.sum(sums[1], axis=0, keepdims=True)

    def block_end(i):
        def body(t, _):
            rows = rows_of(t, LN_TILE)
            middle = tok[i, rows, :].astype(F32) + vec(i, 0) * (wide(att, i, rows) + proj_b[...])
            cot[i, rows, :] = (middle + vec(i, 1) * (wide(dst, i, rows) + fc2_b[...])).astype(BF16)
            return 0
        lax.fori_loop(0, n_ln, body, 0)
        leave(cot, i, out_hbm, 2 + i)

    def every_copy(to, source):
        return pltpu.make_async_remote_copy(
            src_ref=sm, dst_ref=every.at[source], send_sem=ev_s.at[to], recv_sem=ev_r.at[source],
            device_id={"dp": to}, device_id_type=MESH)

    def every_start():
        pltpu.make_async_copy(sm, every.at[dp], out_sem.at[4]).start()

        def body(step, _):
            every_copy(lax.rem(dp + step, n_dp), dp).start()
            return 0
        lax.fori_loop(1, n_dp, body, 0)

    def every_finish():
        pltpu.make_async_copy(sm, every.at[dp], out_sem.at[4]).wait()

        def body(step, _):
            every_copy(lax.rem(dp + step, n_dp), dp).wait_send()
            source = lax.rem(dp + n_dp - step, n_dp)
            every_copy(source, source).wait_recv()
            return 0
        lax.fori_loop(1, n_dp, body, 0)

    def rs_both(buf, i, k):
        rs_copy(buf, i, k).start()
        rs_finish(buf, i, k)

    def forward(i):
        first_norm(i, i == 0)
        if i == 0:
            loads["qkvw"].wait()
        project(i)
        attend(i)
        if i == 0:
            loads["projw"].wait()
        attend_out(i)

    def close_sums():
        sent = share(g2r, g2_s, g2_r)
        for copy in sent:
            copy.wait()
        total = (g2r[0] + g2r[1]) + (g2r[2] + g2r[3])
        for i in (0, 1):
            sm[i, 1:2, :] = sm[i, 1:2, :] + total[i:i + 1, :]
        for j in range(4):
            sm[2, 1:2, j * 256:(j + 1) * 256] = jnp.sum(fb1[j], axis=0, keepdims=True)
        for k in range(3):
            for slab in (0, 1):
                at = k * 256 + slab * 128
                sm[2, 3:4, at:at + 128] = jnp.sum(lanes[k, slab], axis=0, keepdims=True)
        every_start()

    def spill_out(i):
        return pltpu.make_async_copy(att.at[i], spill.at[i], spill_sem.at[i])

    def spill_back(i):
        return pltpu.make_async_copy(spill.at[i], att.at[i], spill_sem.at[2 + i])

    def ag(buf, i, k):
        ag_copy(buf, i, k).start()
        ag_copy(buf, i, k).wait()

    sm[...] = jnp.zeros_like(sm)
    fb1[...] = jnp.zeros_like(fb1)
    lanes[...] = jnp.zeros_like(lanes)
    g2r[...] = jnp.zeros_like(g2r)
    kv[...] = jnp.zeros_like(kv)
    for i in (0, 1):
        sm[i, 6:7, :] = jnp.zeros((1, width), F32) + labels[i].astype(F32)
    unpack(tok_hbm, 1, tok, (cot_hbm, 0))
    forward(0)
    rs_both(att, 0, ATT)
    y_start(att, 0, ATT)
    forward(1)
    rs_both(att, 1, ATT)
    y_start(att, 1, ATT)
    unpack(cot_hbm, 0, cot, (cot_hbm, 1))
    unpack(cot_hbm, 1, cot)
    for name in ("fc1w", "fc2w"):
        loads[name].wait()
    y_finish(att, 0, ATT)
    ag(att, 0, ATT)
    mlp(0)
    rs_both(dst, 0, DS)
    y_start(dst, 0, DS)
    y_finish(att, 1, ATT)
    ag(att, 1, ATT)
    mlp_norm(1)
    mlp_columns(1)
    fc_grads((3, 4, 5,))
    mlp_back(1)
    rs_copy(dst, 1, DS).start()
    fc_grads((2, 6, 0, 1,))
    rs_finish(dst, 1, DS)
    y_start(dst, 1, DS)
    serve((2, 3))
    serve((2, 4))
    fc_grads((7,))
    y_finish(dst, 0, DS)
    ag(dst, 0, DS)
    second_back(0)
    spill_out(0).start()
    serve((2, 5))
    attend_back(0, 0)
    serve((3, 4))
    attend_back(0, 1)
    serve((2, 2))
    serve((3, 5), (3, 3))
    serve((4, 4))
    spill_out(0).wait()
    first_grad(0)
    rs_both(att, 0, DF)
    y_start(att, 0, DF)
    serve((2, 6))
    serve((3, 2))
    serve((4, 5))
    y_finish(dst, 1, DS)
    ag(dst, 1, DS)
    second_back(1)
    spill_out(1).start()
    serve((3, 6), (2, 0))
    serve((4, 2))
    attend_back(1, 0)
    serve((3, 0))
    serve((4, 6), (2, 1))
    attend_back(1, 1)
    serve((3, 1))
    serve((4, 0))
    s5(5)
    spill_out(1).wait()
    first_grad(1)
    s5(4)
    serve((2, 7))
    rs_both(att, 1, DF)
    serve((3, 7), (4, 3))
    y_start(att, 1, DF)
    first_norm(0)
    first_norm(1)
    attention_grads((8, 10, 9,))
    serve((4, 1))
    attention_grads((11,))
    y_finish(att, 0, DF)
    ag(att, 0, DF)
    first_back(0)
    spill_back(0).start()
    s5(0)
    serve((4, 7))
    branch(0)
    s5(6)
    serve((2, 11))
    rs_both(dst, 0, BR)
    serve((2, 8))
    y_start(dst, 0, BR)
    y_finish(att, 1, DF)
    s5(3)
    ag(att, 1, DF)
    serve((3, 8))
    first_back(1)
    spill_back(1).start()
    branch(1)
    serve((3, 11))
    rs_both(dst, 1, BR)
    serve((2, 10), (3, 10))
    s5(2)
    serve((4, 8))
    s5(7)
    s5(1)
    serve((2, 9))
    y_start(dst, 1, BR)
    s6(5)
    serve((3, 9))
    serve((4, 10))
    serve((4, 9))
    close_sums()
    serve((4, 11))
    s6(0)
    y_finish(dst, 0, BR)
    s5(8)
    ag(dst, 0, BR)
    spill_back(0).wait()
    block_end(0)
    y_finish(dst, 1, BR)
    s5(11)
    s5(10)
    s6(8)
    ag(dst, 1, BR)
    s5(9)
    spill_back(1).wait()
    block_end(1)
    every_finish()
    for n in (4, 6, 2, 3, 5, 0, 1, 7, 10, 8, 9, 11):
        close_chunk(n)
    left(3).wait()


def run_block(n_dp, class_table, ada_b, ada_w, tok, cot, stops, labels, log_scale, qkvw, projw, fc1w, fc2w, qv_b, proj_b, fc1_b, fc2_b):
    items, slots, width = tok.shape
    padded = -(-slots // LN_TILE) * LN_TILE
    x_count = sum(r != "Z" for r in ROUTES)
    half = width // 2
    hidden = fc1w.shape[1]
    n_chunks = 12
    n_rest = max(1, (n_dp // 8).bit_length() - 1)
    hbm = pl.BlockSpec(memory_space=pl.ANY)
    vmem = pl.BlockSpec(memory_space=pltpu.VMEM)
    smem = pl.BlockSpec(memory_space=pltpu.SMEM)
    wide_b = (items, padded, width)
    wide_f = (items, 2, padded, half)
    dma = pltpu.SemaphoreType.DMA
    return pl.pallas_call(
        functools.partial(block_kernel, slots, n_dp),
        out_shape=(
            jax.ShapeDtypeStruct(tok.shape, BF16), jax.ShapeDtypeStruct(tok.shape, BF16),
            jax.ShapeDtypeStruct(fc1w.shape, F32), jax.ShapeDtypeStruct(fc2w.shape, F32),
            jax.ShapeDtypeStruct(projw.shape, F32), jax.ShapeDtypeStruct(qkvw.shape, F32),
            jax.ShapeDtypeStruct((n_dp, 3, 8, width), F32),
            jax.ShapeDtypeStruct((n_chunks, 128, width), F32), jax.ShapeDtypeStruct((n_chunks, 128, width), F32),
            jax.ShapeDtypeStruct((n_chunks, 256, width), F32), jax.ShapeDtypeStruct((n_chunks, 128, width), F32),
            jax.ShapeDtypeStruct((n_rest, n_chunks, 128, width), F32), jax.ShapeDtypeStruct(wide_f, F32),
        ),
        in_specs=[hbm, vmem, hbm, hbm, hbm, smem, smem, smem, hbm, hbm, hbm, hbm, vmem, vmem, vmem, vmem],
        out_specs=(hbm,) * 13,
        scratch_shapes=[
            *[pltpu.VMEM(wide_b, BF16) for _ in range(4)],
            pltpu.VMEM((items, padded, hidden), BF16), pltpu.VMEM((items, hidden // 256, padded, 256), BF16),
            *[pltpu.VMEM(wide_f, F32) for _ in range(2)],
            pltpu.VMEM((items, padded, half), F32),
            pltpu.VMEM((items, 3, 2, padded, 128), BF16),
            pltpu.VMEM((items, 2, padded, 128), BF16),
            pltpu.VMEM((2, padded, 128), BF16),
            pltpu.VMEM((2, 2, 768, 128), BF16),
            pltpu.VMEM((3, 768, 128), F32),
            pltpu.VMEM((items, slots, half), F32),
            pltpu.VMEM((items, slots, half), F32),
            pltpu.VMEM(qkvw.shape, BF16), pltpu.VMEM(projw.shape, BF16),
            pltpu.VMEM(fc1w.shape, BF16), pltpu.VMEM(fc2w.shape, BF16),
            pltpu.VMEM((slots, width), BF16), pltpu.VMEM(class_table.shape, BF16), pltpu.VMEM((1, qkvw.shape[2]), F32),
            pltpu.VMEM((max(1, x_count), 128, width), F32), pltpu.VMEM((max(1, n_chunks - x_count), 256, width), F32),
            pltpu.VMEM((2, 256, width), F32),
            pltpu.VMEM((4, items, 8, width), F32), pltpu.VMEM((items, 8, width), F32),
            pltpu.VMEM((4, 8, width), F32),
            pltpu.VMEM((4, 8, 256), F32), pltpu.VMEM((3, 2, 8, 128), F32), pltpu.VMEM((3, 8, width), F32),
            dma((11,)), dma, dma((5,)), dma((5,)), dma((2,)), dma((2,)), dma((n_chunks, 4)), dma((4,)), pltpu.SemaphoreType.REGULAR((2,)),
            dma((3,)), dma((3,)), dma((3,)), dma((3,)),
            *[dma((8,)) for _ in range(6)],
            *[dma((n_chunks,)) for _ in range(8)], *[dma((n_chunks, 4)) for _ in range(6)],
            dma((n_rest, n_chunks)), dma((n_rest, n_chunks)), dma((n_dp,)), dma((n_dp,)),
        ],
        compiler_params=pltpu.CompilerParams(
            collective_id=0, has_side_effects=True, vmem_limit_bytes=62 * 2**20),
        name="block",
    )(class_table, ada_b, ada_w, tok, cot, stops, labels, log_scale, qkvw, projw, fc1w, fc2w, qv_b, proj_b, fc1_b, fc2_b)


def tail_kernel(
    every_hbm, table_hbm, ada_hbm, g1_in, g2_in, gp_in, gq_in, out_in, tg_in,
    table_grad, ada_grad, ada_bias, qv_bias, head_scale, proj_bias, fc1_bias, fc2_bias, g1, g2, gp, gq, out, tg,
    every, table, ada, part, *room_and_sems,
):
    n_dp, width = every.shape[0], every.shape[3]
    rows = 2 * n_dp
    rooms, (sem, part_sem, in_sem, copy_sem) = room_and_sems[:-4], room_and_sems[-4:]
    moved = ((g1_in, g1), (g2_in, g2), (gq_in, gq), (out_in, out), (tg_in, tg), (gp_in, gp))
    pieces = []
    for (a, b), room in zip(moved, rooms):
        if len(a.shape) == 3:
            views = [a_i for a_i in range(a.shape[0])]
        else:
            views = [pl.ds(r, 256) for r in range(0, a.shape[0], 256)]
        pieces += [(a.at[v], b.at[v], room.at[v]) for v in views]
    fetches = [pltpu.make_async_copy(a, room, in_sem.at[k]) for k, (a, _, room) in enumerate(pieces)]
    copies = [pltpu.make_async_copy(room, b, copy_sem.at[k]) for k, (_, b, room) in enumerate(pieces)]

    def move(k):
        fetches[k].wait()
        copies[k].start()
    loads = [pltpu.make_async_copy(a, b, sem.at[k])
             for k, (a, b) in enumerate(((every_hbm, every), (table_hbm, table), (ada_hbm, ada)))]
    for copy in (*loads, *fetches):
        copy.start()
    loads[0].wait()
    total = every[0, 2]
    for d in range(1, n_dp):
        total = total + every[d, 2]
    fc2_bias[...] = total[0:1]
    fc1_bias[...] = total[1:2]
    proj_bias[...] = total[2:3]
    wide = qv_bias.shape[1]
    qv_bias[0:1, :] = total[3:4, 0:wide]
    qv_bias[1:2, :] = total[3:4, wide:2 * wide]
    lanes = total[3:4, 2 * wide:3 * wide]
    head_of = lax.broadcasted_iota(jnp.int32, lanes.shape, 1) // 64
    spot = lax.broadcasted_iota(jnp.int32, head_scale.shape, 1)
    heads = jnp.zeros(head_scale.shape, F32)
    for h in range(head_scale.shape[1]):
        heads = jnp.where(spot == h, jnp.sum(jnp.where(head_of == h, lanes, 0.0), axis=1, keepdims=True), heads)
    head_scale[...] = heads
    for k in range(6):
        move(k)

    def gathered(k):
        return jnp.concatenate([every[d, i, k:k + 1, :] for d in range(n_dp) for i in (0, 1)], axis=0)
    label = gathered(6)[:, 0:1]
    classes = table.shape[0]
    hot = jnp.where(lax.broadcasted_iota(jnp.int32, (rows, classes), 1).astype(F32) == label, 1.0, 0.0)
    loads[1].wait()
    local = dot(hot.astype(BF16), table[...])
    gate = 1.0 / (1.0 + jnp.exp(-local))
    lifted = (local * gate).astype(BF16)
    for k in range(6, 11):
        move(k)
    loads[2].wait()
    lifted_grad = jnp.zeros(local.shape, F32)

    def out_copy(k):
        return pltpu.make_async_copy(part.at[k % 2], ada_grad.at[:, pl.ds(k * width, width)], part_sem.at[k % 2])
    for k in range(6):
        low = gathered(k).astype(BF16)
        ada_bias[:, k * width:(k + 1) * width] = jnp.sum(low.astype(F32), axis=0, keepdims=True)
        lifted_grad = lifted_grad + dot(low, ada[:, k * width:(k + 1) * width], NT)
        if k >= 2:
            out_copy(k - 2).wait()
        part[k % 2] = dot(lifted, low, TN)
        out_copy(k).start()
        if k < 5:
            move(11 + k)
    class_grad = lifted_grad * (gate * (1.0 + local * (1.0 - gate)))
    table_grad[...] = lax.dot_general(hot, class_grad, TN, precision=lax.Precision.HIGHEST, preferred_element_type=F32)
    out_copy(4).wait()
    out_copy(5).wait()
    for copy in copies:
        copy.wait()


def run_tail(heads, every, class_table, ada_weight, g1, g2, gp, gq, out, tg):
    classes, wide = class_table.shape
    width = every.shape[3]
    hbm = pl.BlockSpec(memory_space=pl.ANY)
    vmem = pl.BlockSpec(memory_space=pltpu.VMEM)
    dma = pltpu.SemaphoreType.DMA
    shape = lambda *dims: jax.ShapeDtypeStruct(dims, F32)
    return pl.pallas_call(
        tail_kernel,
        out_shape=(
            shape(classes, wide), shape(*ada_weight.shape), shape(1, ada_weight.shape[1]), shape(2, wide), shape(1, heads),
            shape(1, width), shape(1, width), shape(1, width), shape(*g1.shape), shape(*g2.shape), shape(*gp.shape), shape(*gq.shape),
            jax.ShapeDtypeStruct(out.shape, out.dtype), jax.ShapeDtypeStruct(tg.shape, tg.dtype)),
        in_specs=[hbm] * 9,
        out_specs=(vmem, hbm, vmem, vmem, vmem, vmem, vmem, vmem, hbm, hbm, hbm, hbm, hbm, hbm),
        scratch_shapes=[
            pltpu.VMEM(every.shape, F32), pltpu.VMEM(class_table.shape, BF16), pltpu.VMEM(ada_weight.shape, BF16),
            pltpu.VMEM((2, wide, width), F32),
            *[pltpu.VMEM(a.shape, a.dtype) for a in (g1, g2, gq, out, tg, gp)],
            dma((3,)), dma((2,)), dma((16,)), dma((16,)),
        ],
        compiler_params=pltpu.CompilerParams(vmem_limit_bytes=60 * 2**20),
        name="tail",
    )(every, class_table, ada_weight, g1, g2, gp, gq, out, tg)


def shards(
    n_dp, tokens, cotangent, stop_scales, labels, class_table, ada_weight, ada_bias, qkv_weight, qv_bias, log_scale,
    proj_weight, proj_bias, fc1_weight, fc1_bias, fc2_weight, fc2_bias,
):
    items, slots, width = tokens.shape
    heads = log_scale.shape[0]
    out, tg, g1, g2, gp, gq, every, *_ = run_block(
        n_dp, class_table, ada_bias[None, :], ada_weight, tokens, cotangent, stop_scales, labels, log_scale,
        jnp.transpose(qkv_weight, (1, 0, 2)), proj_weight, fc1_weight, fc2_weight,
        qv_bias, proj_bias[None, :], fc1_bias.reshape(-1, 1, 256), fc2_bias[None, :])
    table_grad, ada_grad, ada_bias_grad, qv_grad, scale_grad, proj_b, fc1_b, fc2_b, g1, g2, gp, gq, out, tg = run_tail(
        heads, every, class_table, ada_weight, g1, g2, gp, gq, out, tg)
    return (
        out, tg, table_grad, ada_grad, ada_bias_grad[0], jnp.transpose(gq, (1, 0, 2)), qv_grad, scale_grad[0],
        gp, proj_b[0], g1, fc1_b[0], g2, fc2_b[0],
    )


def solution(mesh):
    return jax.shard_map(
        functools.partial(shards, mesh.shape["dp"]),
        mesh=mesh,
        in_specs=(
            P("dp", None, None), P("dp", None, None), P("dp"), P("dp"), P(None, "mp"), P("mp", None), P(),
            P(None, None, "mp"), P(None, "mp"), P("mp"), P("mp", None), P(), P(None, "mp"), P("mp"), P("mp", None), P(),
        ),
        out_specs=(
            P("dp", None, None), P("dp", None, None), P(None, "mp"), P("mp", None), P(), P(None, None, "mp"), P(None, "mp"),
            P("mp"), P("mp", None), P(), P(None, "mp"), P("mp"), P("mp", None), P(),
        ),
        check_vma=False,
    )
```
